512 devices in a mesh: dp: 64 (over y, z_hi, core), tp: 8 (over z_lo, x).
Axes of the slice: x: 4, y: 8, z: 8 (z_hi: 4, z_lo: 2; z = z_hi * 2 + z_lo), core: 2. Of those that a mesh axis runs over, the one named last changes fastest.
Arguments:
- pool: bfloat16 [4160, 16, 576], P('dp'), may hold values from -4 to 4
- page_table: int32 [320, 13], P('dp'), may hold values from 0 to 256, as said below
- lengths: int32 [320], P('dp'), may hold values from 1 to 208, as said below
- mig_page: int32 [64, 84], P('dp'), may hold values from 0 to 64
- mig_dest: int32 [64, 84], P('dp'), may hold values from 0 to 63, as said below
- queries: bfloat16 [640, 64, 576], P('dp', 'tp'), may hold values from -18 to 18
- new_latent: bfloat16 [640, 576], P('dp'), may hold values from -4 to 4
- w_uv: bfloat16 [64, 512, 128], P('tp'), may hold values from -0.25 to 0.25
- w_out: bfloat16 [8192, 8, 896], P('tp', None, 'dp'), may hold values from -0.0625 to 0.0625
- residual: bfloat16 [640, 8, 896], P(None, 'tp', 'dp'), may hold values from -25 to 25
- norm_gain: bfloat16 [7168], P('tp'), may hold values from 0.5 to 1.5
- w_gate: bfloat16 [7168, 18432], P('tp', 'dp'), may hold values from -0.0625 to 0.0625
- w_up: bfloat16 [7168, 18432], P('tp', 'dp'), may hold values from -0.0625 to 0.0625
- w_down: bfloat16 [18432, 7168], P('dp', 'tp'), may hold values from -0.046875 to 0.046875
Outputs:
- out: bfloat16 [640, 7168], P('dp', 'tp')
The draws below stay inside these ranges and needn't reach their ends.
Inputs may be any that keep to these rules, and one draw needn't show every extreme that they name: `page_table`: on each rank the entries of the first ceil(lengths/16) slots of its requests name pages that the rank holds after migration (its own, or inbox slots that the migration lists fill); no page is named twice on one rank. `lengths`: some request has exactly 208 cached tokens. `mig_dest`: each rank's list names 28 distinct other ranks, each in 3 consecutive entries.
All inputs are finite; a program needn't handle non-finite values.
Results may differ from the reference program's by a relative error of at most 0.02.
Values may be sent and summed in bfloat16 or wider, within the bound.
A program may use at most 64 MiB of HBM per device.

```python
import math
import jax
import jax.numpy as jnp
from jax import lax

D = 7168
FF = 18432
HEADS = 64
HD = 128
KVL = 512
ROPE = 64
LAT = 576
PAGE = 16
MAXP = 13
REQ = 5
CAP = 3
DESTS = 28
OUT = 84
POOL = 65
TOKENS = 640
N_DP = 64
N_TP = 8


def migration(key):
    key_offsets = jax.random.fold_in(key, 11)
    random_bits = jax.random.randint(key_offsets, (N_DP, N_DP - 1), 0, 65536)
    priority = random_bits * N_DP + jnp.arange(N_DP - 1, dtype=jnp.int32)[None, :]
    offsets = jnp.argsort(priority, axis=1).astype(jnp.int32)[:, :DESTS] + 1
    repeated = jnp.repeat(offsets, CAP, axis=1)
    source = jnp.arange(N_DP, dtype=jnp.int32)[:, None]
    return ((source + repeated) % N_DP).astype(jnp.int32)


def draw_mig_dest(key, part):
    destination = migration(key)
    return destination


def draw_page_table(key, part):
    destination = migration(key)
    key = jax.random.fold_in(key, 2)
    key_pick, key_mix = jax.random.split(key)
    slot_total = N_DP * CAP
    sends_to = jnp.any(destination[None, :, :] == jnp.arange(N_DP, dtype=jnp.int32)[:, None, None], axis=2)
    filled = jnp.repeat(sends_to, CAP, axis=1)
    own_class = jnp.ones((N_DP, POOL), jnp.int32)
    inbox_class = jnp.where(filled, 0, 2).astype(jnp.int32)
    priority_class = jnp.concatenate([own_class, inbox_class], axis=1)
    candidates = POOL + slot_total
    random_bits = jax.random.randint(key_pick, (N_DP, candidates), 0, 4096)
    priority = priority_class * (4096 * 1024) + random_bits * 1024 + jnp.arange(candidates, dtype=jnp.int32)[None, :]
    chosen = jnp.argsort(priority, axis=1)[:, :POOL].astype(jnp.int32)
    mixing = jax.random.randint(key_mix, (N_DP, POOL), 0, 65536) * 1024 + jnp.arange(POOL, dtype=jnp.int32)[None, :]
    shuffle = jnp.argsort(mixing, axis=1)
    page_rows = jnp.take_along_axis(chosen, shuffle, axis=1)
    return page_rows.reshape(N_DP * REQ, MAXP).astype(jnp.int32)


def draw_lengths(key, part):
    key = jax.random.fold_in(key, 3)
    key_ceiling, key_lengths, key_longest = jax.random.split(key, 3)
    longest = MAXP * PAGE
    ceiling = jax.random.randint(key_ceiling, (N_DP, 1), longest // 4, longest + 1)
    drawn = jax.random.randint(key_lengths, (N_DP, REQ), 1, ceiling + 1)
    longest_at = jax.random.randint(key_longest, (), 0, N_DP * REQ)
    flat_lengths = drawn.reshape(-1)
    return jnp.where(jnp.arange(N_DP * REQ) == longest_at, longest, flat_lengths).astype(jnp.int32)


def draw_queries(key, part):
    key = jax.random.fold_in(key, 4)
    return jnp.clip(jax.random.normal(key, (TOKENS, HEADS, LAT), jnp.float32), -4.0, 4.0).astype(jnp.bfloat16)


def draw_new_latent(key, part):
    key = jax.random.fold_in(key, 5)
    return jnp.clip(jax.random.normal(key, (TOKENS, LAT), jnp.float32), -4.0, 4.0).astype(jnp.bfloat16)


def draw_residual(key, part):
    key = jax.random.fold_in(key, 6)
    key_rows, key_cols, key_base = jax.random.split(key, 3)
    row_scale = jnp.exp(jax.random.uniform(key_rows, (TOKENS, 1, 1), jnp.float32, math.log(0.5), math.log(5.0)))
    col_scale = jnp.exp(jax.random.uniform(key_cols, (1, N_TP, D // N_TP), jnp.float32, math.log(0.5), math.log(5.0)))
    base_draw = jnp.clip(jax.random.normal(key_base, (TOKENS, N_TP, D // N_TP), jnp.float32), -4.0, 4.0)
    return (0.25 * base_draw * row_scale * col_scale).astype(jnp.bfloat16)


def touch_ends(values, own_key, smallest, high):
    longest = values.shape.index(max(values.shape))
    spots = []
    for shift in (0, 1):
        where = [jax.random.randint(jax.random.fold_in(own_key, axis), (), 0, length) for axis, length in enumerate(values.shape)]
        where[longest] = (where[longest] + shift) % values.shape[longest]
        spots.append(tuple(where))
    return values.at[spots[0]].set(smallest).at[spots[1]].set(high)


def level_of(rng, extent, cuts, smallest, top_value):
    gain = 1.0
    for dim, parts in cuts:
        heights = jax.random.uniform(jax.random.fold_in(jax.random.fold_in(rng, 6), dim), (parts,), jnp.float32, smallest / len(cuts), top_value / len(cuts))
        gain = gain * jnp.repeat(jnp.exp(heights), extent[dim] // parts).reshape((-1,) + (1,) * (len(extent) - 1 - dim))
    return gain


def normal_values(rng, dims, deviation, reach, shards=(), kind=jnp.bfloat16):
    entries = deviation * jax.random.normal(rng, dims, jnp.float32)
    if shards:
        entries = entries * level_of(rng, dims, shards, -0.22, 0.18)
    return jnp.clip(entries, -reach, reach).astype(kind)


def setup_inputs(seed: int = 0) -> dict:
    seeds = jax.random.split(jax.random.key(seed), 15)
    return {
        "pool": normal_values(seeds[0], (N_DP * POOL, PAGE, LAT), 1.0, 4.0, ((0, 64),)),
        "page_table": draw_page_table(jax.random.fold_in(seeds[14], 71), 0),
        "lengths": draw_lengths(jax.random.fold_in(seeds[14], 71), 0),
        "mig_page": touch_ends(jax.random.randint(seeds[3], (N_DP, OUT), 0, POOL), jax.random.fold_in(seeds[3], 1), 0, POOL - 1).astype(jnp.int32),
        "mig_dest": draw_mig_dest(jax.random.fold_in(seeds[14], 71), 0),
        "queries": draw_queries(jax.random.fold_in(seeds[14], 71), 0),
        "new_latent": draw_new_latent(jax.random.fold_in(seeds[14], 71), 0),
        "w_uv": normal_values(seeds[7], (HEADS, KVL, HD), KVL ** -0.5, 0.25, ((0, 8),)),
        "w_out": normal_values(seeds[8], (HEADS * HD, N_TP, D // N_TP), (HEADS * HD) ** -0.5, 0.0625, ((0, 8), (2, 64))),
        "residual": draw_residual(jax.random.fold_in(seeds[14], 71), 0),
        "norm_gain": jnp.clip(1.0 + 0.1 * jax.random.normal(seeds[10], (D,), jnp.float32), 0.5, 1.5).astype(jnp.bfloat16),
        "w_gate": normal_values(seeds[11], (D, FF), D ** -0.5, 0.0625, ((0, 8), (1, 64))),
        "w_up": normal_values(seeds[12], (D, FF), D ** -0.5, 0.0625, ((0, 8), (1, 64))),
        "w_down": normal_values(seeds[13], (FF, D), FF ** -0.5, 0.046875, ((0, 64), (1, 8))),
    }


epsilon = 1e-06

def inbox_table(mig_page, mig_dest):
    entry_count = mig_dest.shape[1]
    same_dest = mig_dest[:, :, None] == mig_dest[:, None, :]
    earlier = jnp.arange(entry_count)[None, :] < jnp.arange(entry_count)[:, None]
    slot_order = lax.optimization_barrier(jnp.sum(jnp.logical_and(same_dest, earlier[None, :, :]), axis=2)).astype(jnp.int32)
    source = jnp.broadcast_to(jnp.arange(N_DP, dtype=jnp.int32)[:, None], mig_dest.shape)
    global_page = (source * POOL + mig_page).astype(jnp.int32)
    slot_total = N_DP * CAP
    target = jnp.where(slot_order < CAP, mig_dest * slot_total + source * CAP + slot_order, N_DP * slot_total).astype(jnp.int32)
    flat_table = jnp.zeros((N_DP * slot_total + 1,), jnp.int32).at[target.reshape(-1)].set(global_page.reshape(-1))
    return flat_table[:-1].reshape(N_DP, slot_total)

def attend(queries, new_latent, cache_keys, lengths, w_uv):
    requests = cache_keys.shape[0]
    head_count = queries.shape[1]
    score_scale = (HD + ROPE) ** (-0.5)
    query_rows = queries.reshape(requests, 2, head_count, LAT).astype(jnp.float32)
    new_rows = new_latent.reshape(requests, 2, LAT).astype(jnp.float32)
    cached = cache_keys.astype(jnp.float32)
    cache_scores = jnp.einsum('rqhc,rkc->rqhk', query_rows, cached) * score_scale
    position = jnp.arange(cache_keys.shape[1], dtype=jnp.int32)
    live_mask = position[None, :] < lengths[:, None]
    cache_scores = jnp.where(live_mask[:, None, None, :], cache_scores, -jnp.inf)
    new_scores = jnp.einsum('rqhc,rkc->rqhk', query_rows, new_rows) * score_scale
    causal_mask = jnp.arange(2)[None, :] <= jnp.arange(2)[:, None]
    new_scores = jnp.where(causal_mask[None, :, None, :], new_scores, -jnp.inf)
    row_max = jnp.maximum(lax.optimization_barrier(jnp.max(cache_scores, axis=3)), lax.optimization_barrier(jnp.max(new_scores, axis=3)))
    cache_exp = jnp.exp(cache_scores - row_max[..., None])
    new_exp = jnp.exp(new_scores - row_max[..., None])
    row_total = lax.optimization_barrier(jnp.sum(cache_exp, axis=3)) + lax.optimization_barrier(jnp.sum(new_exp, axis=3))
    cache_weights = (cache_exp / row_total[..., None]).astype(jnp.bfloat16)
    new_weights = (new_exp / row_total[..., None]).astype(jnp.bfloat16)
    latent_out = jnp.einsum('rqhk,rkc->rqhc', cache_weights.astype(jnp.float32), cached[..., :KVL])
    latent_out = latent_out + jnp.einsum('rqhk,rkc->rqhc', new_weights.astype(jnp.float32), new_rows[..., :KVL])
    latent_out = latent_out.astype(jnp.bfloat16)
    heads_out = jnp.einsum('rqhc,hcd->rqhd', latent_out.astype(jnp.float32), w_uv.astype(jnp.float32))
    return heads_out.astype(jnp.bfloat16).reshape(2 * requests, head_count * HD)

def reference(pool, page_table, lengths, mig_page, mig_dest, queries, new_latent, w_uv, w_out, residual, norm_gain, w_gate, w_up, w_down):
    inbox = inbox_table(mig_page, mig_dest)
    rank_ids = jnp.arange(N_DP, dtype=jnp.int32)
    rank_tables = page_table.reshape(N_DP, REQ, MAXP)
    rank_lengths = lengths.reshape(N_DP, REQ)
    rank_queries = queries.reshape(N_DP, 2 * REQ, HEADS, LAT)
    rank_latent = new_latent.reshape(N_DP, 2 * REQ, LAT)

    def one_rank(rank_items):
        rank_id, rank_table, inbox_row, rank_length, query_block, latent_block = rank_items
        own_page = rank_table < POOL
        inbox_slot = jnp.clip(rank_table - POOL, 0, N_DP * CAP - 1).astype(jnp.int32)
        global_page = jnp.where(own_page, rank_id * POOL + rank_table, inbox_row[inbox_slot]).astype(jnp.int32)
        cache_keys = pool[global_page].reshape(REQ, MAXP * PAGE, LAT)
        return attend(query_block, latent_block, cache_keys, rank_length, w_uv)
    heads_out = lax.map(one_rank, (rank_ids, rank_tables, inbox, rank_lengths, rank_queries, rank_latent))
    heads_out = heads_out.reshape(TOKENS, HEADS * HD)
    projected = jnp.dot(heads_out, w_out.reshape(HEADS * HD, D), preferred_element_type=jnp.float32)
    stream = (residual.reshape(TOKENS, D).astype(jnp.float32) + projected).astype(jnp.bfloat16)
    stream_wide = lax.optimization_barrier(stream).astype(jnp.float32)
    mean_square = lax.optimization_barrier(jnp.mean(stream_wide * stream_wide, axis=1, keepdims=True))
    normed = (stream_wide * lax.rsqrt(mean_square + epsilon) * norm_gain.astype(jnp.float32)[None, :]).astype(jnp.bfloat16)
    gate_sum = jnp.dot(normed, w_gate, preferred_element_type=jnp.float32)
    up_sum = jnp.dot(normed, w_up, preferred_element_type=jnp.float32)
    hidden = (jax.nn.silu(gate_sum) * up_sum).astype(jnp.bfloat16)
    down_sum = jnp.dot(hidden, w_down, preferred_element_type=jnp.float32)
    return (stream_wide + down_sum).astype(jnp.bfloat16)
```

```python
import functools

import jax
import jax.numpy as jnp
from jax import lax
from jax.experimental import pallas as pl
from jax.experimental.pallas import tpu as pltpu
from jax.sharding import PartitionSpec as P

D = 7168
HD = 128
KVL = 512
LAT = 576
PAGE = 16
MAXP = 13
REQ = 5
POOL = 65
CAP = 3
NY = 8
NG = 8
NT = 8
KEYS = 32
TOK = 640
EPS = 1e-06
SCALE = 192 ** (-0.5)
BF = jnp.bfloat16
F32 = jnp.float32
MESH = pl.DeviceIdType.MESH
DEAD = -1e30


def dot(a, b, dims):
    return lax.dot_general(a, b, (dims, ((), ())), preferred_element_type=F32)


def iota(shape, axis):
    return lax.broadcasted_iota(jnp.int32, shape, axis)


class Links:
    def __init__(self, send_sems, recv_sems):
        self.send_sems, self.recv_sems, self.used, self.sent = send_sems, recv_sems, 0, []

    def reserve(self, count):
        first = self.used
        self.used += count
        return first

    def copy(self, slot, src, dst, dp, tp):
        return pltpu.make_async_remote_copy(
            src_ref=src,
            dst_ref=dst,
            send_sem=self.send_sems.at[slot],
            recv_sem=self.recv_sems.at[slot],
            device_id={"dp": dp, "tp": tp},
            device_id_type=MESH,
        )

    def send(self, slot, src, dst, dp, tp):
        copy = self.copy(slot, src, dst, dp, tp)
        copy.start()
        self.sent.append(copy)

    def arrived(self, slot, dst, dp, tp):
        self.copy(slot, dst, dst, dp, tp).wait_recv()

    def finish(self):
        for copy in self.sent:
            copy.wait_send()


def ring_gather(links, buf, dp_of, y, core, tp):
    right, left = dp_of(lax.rem(y + 1, NY)), dp_of(lax.rem(y + NY - 1, NY))
    partner = dp_of(y) + 1 - 2 * core
    to_right, to_left, over = links.reserve(4), links.reserve(3), links.reserve(8)

    def pass_on(order, index):
        links.send(over + order, buf.at[core, index], buf.at[core, index], partner, tp)

    links.send(to_right, buf.at[core, y], buf.at[core, y], right, tp)
    links.send(to_left, buf.at[core, y], buf.at[core, y], left, tp)
    pass_on(0, y)
    indices = [y]
    for step in range(4):
        index = lax.rem(y + NY - 1 - step, NY)
        links.arrived(to_right + step, buf.at[core, index], left, tp)
        if step < 3:
            links.send(to_right + step + 1, buf.at[core, index], buf.at[core, index], right, tp)
        pass_on(len(indices), index)
        indices.append(index)
        if step < 3:
            index = lax.rem(y + 1 + step, NY)
            links.arrived(to_left + step, buf.at[core, index], right, tp)
            if step < 2:
                links.send(to_left + step + 1, buf.at[core, index], buf.at[core, index], left, tp)
            pass_on(len(indices), index)
            indices.append(index)
    for order, index in enumerate(indices):
        links.arrived(over + order, buf.at[1 - core, index], partner, tp)


def kernel(
    table, lengths, q, own, inbox, fresh, w_uv, w_out, res, w_gu, w_down, out,
    q_all, keys, o_out, o_in, ho, b_in, heads, pj, c_in, stream, gu, e_in, h_all, part, f_out, f_in,
    acc, r_out, r_in, l_out, l_in, g_out, g_in, send_sems, recv_sems,
):
    dp, t = lax.axis_index("dp"), lax.axis_index("tp")
    y, g = dp // NG, lax.rem(dp, NG)
    z, core = g // 2, lax.rem(g, 2)
    links = Links(send_sems, recv_sems)
    t_to = [lax.rem(t + k, NT) for k in range(NT)]
    t_from = [lax.rem(t + NT - k, NT) for k in range(NT)]
    g_to = [lax.rem(g + k, NG) for k in range(NG)]
    g_from = [lax.rem(g + NG - k, NG) for k in range(NG)]
    z_to = [lax.rem(z + k, 4) for k in range(4)]
    z_from = [lax.rem(z + 4 - k, 4) for k in range(4)]

    def dp_of(yy):
        return yy * NG + g

    def group(gg):
        return y * NG + gg

    barrier = pltpu.get_barrier_semaphore()
    for k in range(1, NT):
        pl.semaphore_signal(barrier, inc=1, device_id={"dp": dp, "tp": t_to[k]}, device_id_type=MESH)
    for k in range(1, NG):
        pl.semaphore_signal(barrier, inc=1, device_id={"dp": group(g_to[k]), "tp": t}, device_id_type=MESH)
    for step in (1, NY - 1):
        pl.semaphore_signal(
            barrier, inc=1, device_id={"dp": dp_of(lax.rem(y + step, NY)), "tp": t}, device_id_type=MESH
        )
    pl.semaphore_wait(barrier, 16)

    slot = links.reserve(NT)
    for k in range(1, NT):
        links.send(slot + k, q, q_all.at[t], dp, t_to[k])
    q_all[t] = q[...]

    def pick(r, carry):
        row = iota((KEYS, 1), 0)
        page = row // 2
        index = jnp.full((KEYS, 1), -1, jnp.int32)
        for k in range(MAXP):
            entry = table[r, k]
            base = jnp.where(entry < POOL, 2 * entry, 1024 + ((entry - POOL) // CAP) * 8 + lax.rem(entry - POOL + CAP, CAP) * 2)
            index = jnp.where(page == k, base + lax.rem(row, 2), index)
        from_own = (index == iota((KEYS, 2 * POOL), 1)).astype(BF)
        from_inbox = (index == iota((KEYS, 512), 1) + 1024).astype(BF)
        from_fresh = (row - 2 * MAXP + 2 * r == iota((KEYS, 2 * REQ), 1)).astype(BF)
        from_fresh = jnp.where(jnp.logical_and(row >= 26, row < 28), from_fresh, jnp.zeros((), BF))
        nn = ((1,), (0,))
        rows = dot(from_own, own[...], nn) + dot(from_inbox, inbox[...], nn) + dot(from_fresh, fresh[...], nn)
        keys[r] = rows.astype(BF)
        return carry

    lax.fori_loop(0, REQ, pick, 0)
    for k in range(1, NT):
        links.arrived(slot + k, q_all.at[t_from[k]], dp, t_from[k])

    def attend(r, carry):
        rows = q_all[:, r].reshape(NT * 16, LAT)
        scores = dot(rows, keys[r], ((1,), (1,))) * SCALE
        row, col = iota((NT * 16, KEYS), 0), iota((NT * 16, KEYS), 1)
        cached = jnp.logical_and(col < 26, (col // 2) * PAGE + 2 * t + lax.rem(col, 2) < lengths[r])
        second = lax.rem(row // 8, 2)
        newer = jnp.logical_and(jnp.logical_and(col >= 26, col <= 26 + second), t == 0)
        live = jnp.logical_or(cached, newer)
        scores = jnp.where(live, scores, DEAD)
        top = jnp.max(scores, axis=1, keepdims=True)
        weights = jnp.where(live, jnp.exp(scores - top), 0.0)
        total = jnp.sum(weights, axis=1, keepdims=True)
        some = total > 0.0
        total = jnp.where(some, total, 1.0)
        latent = dot((weights / total).astype(BF), keys[r][:, :KVL], ((1,), (0,)))
        lse = jnp.where(some, top + jnp.log(total), DEAD)
        high = lse.astype(BF).astype(F32)
        middle = (lse - high).astype(BF).astype(F32)
        low = lse - high - middle
        lane = iota((NT * 16, 128), 1)
        parts = jnp.where(lane == 0, high, jnp.where(lane == 1, middle, jnp.where(lane == 2, low, 0.0)))
        o_out[:, r, :, :KVL] = latent.astype(BF).reshape(NT, 16, KVL)
        o_out[:, r, :, KVL:] = parts.astype(BF).reshape(NT, 16, 128)
        return carry

    lax.fori_loop(0, REQ, attend, 0)
    slot = links.reserve(NT)
    for k in range(1, NT):
        links.send(slot + k, o_out.at[t_to[k]], o_in.at[t], dp, t_to[k])
    o_in[t] = o_out[t]
    for k in range(1, NT):
        links.arrived(slot + k, o_in.at[t_from[k]], dp, t_from[k])
    lse = [jnp.sum(o_in[s, :, :, KVL:].astype(F32), axis=2, keepdims=True) for s in range(NT)]
    top = functools.reduce(jnp.maximum, lse)
    shares = [jnp.exp(v - top) for v in lse]
    total = functools.reduce(jnp.add, shares)
    latent = jnp.zeros((REQ, 16, KVL), F32)
    for s in range(NT):
        latent = latent + o_in[s, :, :, :KVL].astype(F32) * (shares[s] / total)
    latent = latent.astype(BF).reshape(REQ * 16, KVL)

    of_token = (iota((16, 80), 1) // 8 == iota((16, 80), 0)).astype(BF)
    head = lax.rem(iota((80, HD), 0), 8)
    for h in range(8):
        values = jnp.where(head == h, dot(latent, w_uv[h], ((1,), (0,))), 0.0).astype(BF)
        values = dot(of_token, values, ((1,), (0,))).astype(BF)
        ho[h // 4, :, (h % 4) * HD : (h % 4 + 1) * HD] = values

    slot = links.reserve(NG)
    for k in range(1, NG):
        links.send(slot + k, ho.at[lax.rem(g_to[k], 2)], b_in.at[g], group(g_to[k]), t)
    b_in[g] = ho[core]
    for k in range(1, NG):
        links.arrived(slot + k, b_in.at[g_from[k]], group(g_from[k]), t)
    row, col = iota((80, 128), 0), iota((80, 128), 1)
    pack = (col == (row // 10) * 16 + lax.rem(row, 10)).astype(BF)
    heads[core, y] = dot(pack, b_in[...].reshape(128, KVL), ((1,), (0,))).astype(BF)
    ring_gather(links, heads, dp_of, y, core, t)

    nt = ((1,), (1,))
    for half in range(2):
        x = heads[half].reshape(TOK, KVL)
        add = dot(w_out[:, half * KVL : (half + 1) * KVL], x, nt)
        projected = add if half == 0 else projected + add
    pj[...] = projected.astype(BF).reshape(NT, 16, TOK)
    slot = links.reserve(NT)
    for k in range(1, NT):
        links.send(slot + k, pj.at[t_to[k]], c_in.at[t], dp, t_to[k])
    c_in[t] = pj[t]
    for k in range(1, NT):
        links.arrived(slot + k, c_in.at[t_from[k]], dp, t_from[k])
    summed = res[...].astype(F32)
    for s in range(NT):
        summed = summed + c_in[s].astype(F32)
    summed = summed.astype(BF).astype(F32)
    squares = jnp.sum(summed * summed, axis=0, keepdims=True)
    high = squares.astype(BF).astype(F32)
    row = iota((16, TOK), 0)
    piece = jnp.where(row == 14, high, jnp.where(row == 15, squares - high, summed)).astype(BF)
    stream[core, y, z] = piece

    slot = links.reserve(4)
    for k in range(1, 4):
        mine = stream.at[core, y, z]
        links.send(slot + k, mine, mine, group(z_to[k] * 2 + core), t)
    for k in range(1, 4):
        links.arrived(slot + k, stream.at[core, y, z_from[k]], group(z_from[k] * 2 + core), t)
    ring_gather(links, stream, dp_of, y, core, t)

    nn = ((1,), (0,))
    slot = links.reserve(NT)
    columns = stream[...].reshape(1024, TOK)
    for k in range(1, NT + 1):
        to = lax.rem(t + k, NT)
        first = pl.multiple_of(to * 80, 80)
        gu[to] = dot(w_gu[pl.ds(first, 80), :], columns, nn).astype(BF)
        if k < NT:
            links.send(slot + k, gu.at[to], e_in.at[t], dp, to)
        else:
            e_in[t] = gu[t]
    for k in range(1, NT):
        links.arrived(slot + k, e_in.at[t_from[k]], dp, t_from[k])
    total = jnp.zeros((80, TOK), F32)
    for s in range(NT):
        total = total + e_in[s].astype(F32)
    scale = lax.rsqrt(total[36:37] / D + EPS)
    gate, up = total[:40] * scale, total[40:] * scale
    hidden = gate / (1.0 + jnp.exp(-gate)) * up
    hidden = jnp.where(iota((40, TOK), 0) < 36, hidden, 0.0)
    hidden = jnp.concatenate([hidden, jnp.zeros((8, TOK), F32)], axis=0).astype(BF)
    h_all[t] = hidden
    slot = links.reserve(NT)
    for k in range(1, NT):
        links.send(slot + k, h_all.at[t], h_all.at[t], dp, t_to[k])
    for k in range(1, NT):
        links.arrived(slot + k, h_all.at[t_from[k]], dp, t_from[k])

    place = jnp.logical_and(iota((16, 896), 1) == dp * 14 + iota((16, 896), 0), iota((16, 896), 0) < 14).astype(BF)
    tn = ((0,), (0,))
    for block in range(TOK // 128):
        lanes = slice(block * 128, (block + 1) * 128)
        value = dot(h_all[:, :, lanes].reshape(384, 128), w_down[...], tn)
        part[lanes] = value + dot(stream[core, y, z, :, lanes], place, tn)

    partner = dp + 1 - 2 * core
    mine = pl.ds(pl.multiple_of(core * 384, 128), KVL)
    other = pl.ds(pl.multiple_of((1 - core) * 384, 128), KVL)
    f_out[...] = part[:, other].astype(BF)
    slot = links.reserve(1)
    links.send(slot, f_out, f_in, partner, t)
    links.arrived(slot, f_in, partner, t)
    acc[...] = (part[:, mine] + f_in[...].astype(F32)).reshape(NY, 80, KVL)
    right, left = dp_of(lax.rem(y + 1, NY)), dp_of(lax.rem(y + NY - 1, NY))
    to_right, to_left = links.reserve(4), links.reserve(3)
    for step in range(4):
        value = acc[lax.rem(y + 4 - step, NY)]
        if step > 0:
            links.arrived(to_right + step - 1, r_in.at[step - 1], left, t)
            value = value + r_in[step - 1].astype(F32)
        r_out[step] = value.astype(BF)
        links.send(to_right + step, r_out.at[step], r_in.at[step], right, t)
        if step < 3:
            value = acc[lax.rem(y + NY - 3 + step, NY)]
            if step > 0:
                links.arrived(to_left + step - 1, l_in.at[step - 1], right, t)
                value = value + l_in[step - 1].astype(F32)
            l_out[step] = value.astype(BF)
            links.send(to_left + step, l_out.at[step], l_in.at[step], left, t)
    links.arrived(to_right + 3, r_in.at[3], left, t)
    links.arrived(to_left + 2, l_in.at[2], right, t)
    value = (acc[y] + r_in[3].astype(F32) + l_in[2].astype(F32)).astype(BF)
    row, col = iota((128, 80), 0), iota((128, 80), 1)
    spread = jnp.logical_and(lax.rem(row, 16) < 10, col == (row // 16) * 10 + lax.rem(row, 16)).astype(BF)
    g_out[...] = dot(spread, value, nn).astype(BF).reshape(NG, 16, KVL)
    slot = links.reserve(NG)
    for k in range(1, NG):
        links.send(slot + k, g_out.at[g_to[k]], g_in.at[g], group(g_to[k]), t)
    g_in[g] = g_out[g]
    for k in range(1, NG):
        links.arrived(slot + k, g_in.at[g_from[k]], group(g_from[k]), t)
    first = jnp.zeros((16, KVL), F32)
    second = jnp.zeros((16, KVL), F32)
    for s in range(4):
        first = first + g_in[2 * s].astype(F32)
        second = second + g_in[2 * s + 1].astype(F32)
    out[:, :KVL] = first.astype(BF)[:10]
    out[:, KVL:] = second.astype(BF)[:10, 128:]
    links.finish()


SLOTS = 8 * 7 + 2 * 15 + 4 + 8


def layer(*operands):
    scratch = [
        ((NT, REQ, 16, LAT), BF),
        ((REQ, KEYS, LAT), BF),
        ((NT, REQ, 16, 640), BF),
        ((NT, REQ, 16, 640), BF),
        ((2, 16, KVL), BF),
        ((NG, 16, KVL), BF),
        ((2, NY, 80, KVL), BF),
        ((NT, 16, TOK), BF),
        ((NT, 16, TOK), BF),
        ((2, NY, 4, 16, TOK), BF),
        ((NT, 80, TOK), BF),
        ((NT, 80, TOK), BF),
        ((NT, 48, TOK), BF),
        ((TOK, 896), F32),
        ((TOK, KVL), BF),
        ((TOK, KVL), BF),
        ((NY, 80, KVL), F32),
        ((4, 80, KVL), BF),
        ((4, 80, KVL), BF),
        ((3, 80, KVL), BF),
        ((3, 80, KVL), BF),
        ((NG, 16, KVL), BF),
        ((NG, 16, KVL), BF),
    ]
    smem = pl.BlockSpec(memory_space=pltpu.SMEM)
    vmem = pl.BlockSpec(memory_space=pltpu.VMEM)
    return pl.pallas_call(
        kernel,
        out_shape=jax.ShapeDtypeStruct((10, 896), BF),
        in_specs=[smem] * 2 + [vmem] * 9,
        out_specs=vmem,
        scratch_shapes=[pltpu.VMEM(shape, kind) for shape, kind in scratch]
        + [pltpu.SemaphoreType.DMA((SLOTS,)), pltpu.SemaphoreType.DMA((SLOTS,))],
        compiler_params=pltpu.CompilerParams(
            collective_id=0, has_side_effects=True, vmem_limit_bytes=48 * 1024 * 1024
        ),
        cost_estimate=pl.CostEstimate(flops=3 * 10**9, bytes_accessed=10**7, transcendentals=10**6),
        name="layer",
    )(*operands)


def local(
    pool,
    page_table,
    lengths,
    mig_page,
    mig_dest,
    queries,
    new_latent,
    w_uv,
    w_out,
    residual,
    norm_gain,
    w_gate,
    w_up,
    w_down,
):
    t = lax.axis_index("tp")
    own = lax.dynamic_slice(pool, (0, 2 * t, 0), (POOL, 2, LAT)).reshape(2 * POOL, LAT)
    order = jnp.arange(CAP * 28, dtype=jnp.int32) % CAP
    row = jnp.arange(512, dtype=jnp.int32)
    match = jnp.logical_and(
        mig_dest[0][None, :] == (row // 8)[:, None], order[None, :] == ((row % 8) // 2)[:, None]
    )
    source = jnp.sum(jnp.where(match, 2 * mig_page[0][None, :] + 1 + (row % 2)[:, None], 0), axis=1) - 1
    select = (source[:, None] == jnp.arange(2 * POOL, dtype=jnp.int32)[None, :]).astype(BF)
    outgoing = jnp.dot(select, own, preferred_element_type=F32).astype(BF).reshape(64, 8, LAT)
    inbox = lax.all_to_all(outgoing, "dp", split_axis=0, concat_axis=0, tiled=True).reshape(512, LAT)

    gain = norm_gain.astype(F32)[:, None]

    def widen(w):
        w = (w.astype(F32) * gain).astype(BF).reshape(64, 14, NT, 36)
        return jnp.pad(w, ((0, 0), (0, 2), (0, 0), (0, 4)))

    w_gu = jnp.stack([widen(w_gate), widen(w_up)], axis=3)
    inner, slot = jnp.arange(16)[:, None], jnp.arange(80)[None, :]
    ones = jnp.logical_and(inner >= 14, slot == 36).reshape(1, 16, 1, 2, 40)
    w_gu = jnp.where(ones, jnp.ones((), BF), w_gu)
    w_gu = w_gu.reshape(NY, 4, 2, 16, TOK).transpose(4, 2, 0, 1, 3).reshape(TOK, 1024)
    w_out_t = jnp.pad(w_out, ((0, 0), (0, 0), (0, 2))).reshape(1024, 128).T
    res_t = jnp.pad(residual.reshape(TOK, 14).T, ((0, 2), (0, 0)))
    w_down_p = jnp.pad(w_down.reshape(NT, 36, 896), ((0, 0), (0, 12), (0, 0))).reshape(384, 896)
    q = queries.reshape(REQ, 16, LAT)
    return layer(page_table, lengths, q, own, inbox, new_latent, w_uv, w_out_t, res_t, w_gu, w_down_p)


def solution(mesh):
    in_specs = (
        P("dp", None, None),
        P("dp", None),
        P("dp"),
        P("dp", None),
        P("dp", None),
        P("dp", "tp", None),
        P("dp", None),
        P("tp", None, None),
        P("tp", None, "dp"),
        P(None, "tp", "dp"),
        P("tp"),
        P("tp", "dp"),
        P("tp", "dp"),
        P("dp", "tp"),
    )
    out_specs = P("dp", "tp")
    return jax.shard_map(local, mesh=mesh, in_specs=in_specs, out_specs=out_specs, check_vma=False)
```

```python
import functools

import jax
import jax.numpy as jnp
from jax import lax
from jax.experimental import pallas as pl
from jax.experimental.pallas import tpu as pltpu
from jax.sharding import PartitionSpec as P

D = 7168
HD = 128
KVL = 512
LAT = 576
PAGE = 16
MAXP = 13
REQ = 5
POOL = 65
CAP = 3
NY = 8
NG = 8
NT = 8
KEYS = 32
TOK = 640
EPS = 1e-06
SCALE = 192 ** (-0.5)
BF = jnp.bfloat16
F32 = jnp.float32
MESH = pl.DeviceIdType.MESH
DEAD = -1e30


def dot(a, b, dims):
    return lax.dot_general(a, b, (dims, ((), ())), preferred_element_type=F32)


def iota(shape, axis):
    return lax.broadcasted_iota(jnp.int32, shape, axis)


class Links:
    def __init__(self, send_sems, recv_sems):
        self.send_sems, self.recv_sems, self.used, self.sent = send_sems, recv_sems, 0, []

    def reserve(self, count):
        first = self.used
        self.used += count
        return first

    def copy(self, slot, src, dst, dp, tp):
        return pltpu.make_async_remote_copy(
            src_ref=src,
            dst_ref=dst,
            send_sem=self.send_sems.at[slot],
            recv_sem=self.recv_sems.at[slot],
            device_id={"dp": dp, "tp": tp},
            device_id_type=MESH,
        )

    def send(self, slot, src, dst, dp, tp):
        copy = self.copy(slot, src, dst, dp, tp)
        copy.start()
        self.sent.append(copy)

    def arrived(self, slot, dst, dp, tp):
        self.copy(slot, dst, dst, dp, tp).wait_recv()

    def finish(self):
        for copy in self.sent:
            copy.wait_send()


def ring_gather(links, buf, dp_of, y, core, tp):
    right, left = dp_of(lax.rem(y + 1, NY)), dp_of(lax.rem(y + NY - 1, NY))
    partner = dp_of(y) + 1 - 2 * core
    to_right, to_left, over = links.reserve(4), links.reserve(3), links.reserve(8)

    def pass_on(order, index):
        links.send(over + order, buf.at[core, index], buf.at[core, index], partner, tp)

    links.send(to_right, buf.at[core, y], buf.at[core, y], right, tp)
    links.send(to_left, buf.at[core, y], buf.at[core, y], left, tp)
    pass_on(0, y)
    indices = [y]
    for step in range(4):
        index = lax.rem(y + NY - 1 - step, NY)
        links.arrived(to_right + step, buf.at[core, index], left, tp)
        if step < 3:
            links.send(to_right + step + 1, buf.at[core, index], buf.at[core, index], right, tp)
        pass_on(len(indices), index)
        indices.append(index)
        if step < 3:
            index = lax.rem(y + 1 + step, NY)
            links.arrived(to_left + step, buf.at[core, index], right, tp)
            if step < 2:
                links.send(to_left + step + 1, buf.at[core, index], buf.at[core, index], left, tp)
            pass_on(len(indices), index)
            indices.append(index)
    for order, index in enumerate(indices):
        links.arrived(over + order, buf.at[1 - core, index], partner, tp)


def kernel(
    table, lengths, mig_page, mig_dest, q, pool, fresh, w_uv, w_out, res, gain, w_gate, w_up, w_down, out,
    own, a_y1, a_y2, a_y3, a_y4, a_z1, a_z2, a_z3, a_z4, w_gu, w_o, w_d,
    q_all, keys, o_out, o_in, ho, b_in, heads, pj, c_in, stream, gu, e_in, h_all, part, f_out, f_in,
    acc, r_out, r_in, l_out, l_in, g_out, g_in, send_sems, recv_sems,
):
    dp, t = lax.axis_index("dp"), lax.axis_index("tp")
    y, g = dp // NG, lax.rem(dp, NG)
    z, core = g // 2, lax.rem(g, 2)
    links = Links(send_sems, recv_sems)
    t_to = [lax.rem(t + k, NT) for k in range(NT)]
    t_from = [lax.rem(t + NT - k, NT) for k in range(NT)]
    g_to = [lax.rem(g + k, NG) for k in range(NG)]
    g_from = [lax.rem(g + NG - k, NG) for k in range(NG)]
    y_to = [lax.rem(y + k, NY) for k in range(NY)]
    y_from = [lax.rem(y + NY - k, NY) for k in range(NY)]
    z_to = [lax.rem(z + k, 4) for k in range(4)]
    z_from = [lax.rem(z + 4 - k, 4) for k in range(4)]
    nn, nt, tn = ((1,), (0,)), ((1,), (1,)), ((0,), (0,))

    def dp_of(yy):
        return yy * NG + g

    def group(gg):
        return y * NG + gg

    barrier = pltpu.get_barrier_semaphore()
    for k in range(1, NT):
        pl.semaphore_signal(barrier, inc=1, device_id={"dp": dp, "tp": t_to[k]}, device_id_type=MESH)
    for k in range(1, NG):
        pl.semaphore_signal(barrier, inc=1, device_id={"dp": group(g_to[k]), "tp": t}, device_id_type=MESH)
    for k in range(1, NY):
        pl.semaphore_signal(barrier, inc=1, device_id={"dp": dp_of(y_to[k]), "tp": t}, device_id_type=MESH)

    row = iota((144, 1), 0)
    column = (row // 2) * PAGE + 2 * t + lax.rem(row, 2)
    own[...] = dot((column == iota((144, POOL * PAGE), 1)).astype(BF), pool[...], nn).astype(BF)
    row = iota((384, 1), 0)
    inner = lax.rem(row, 6)
    entry = lax.rem(iota((1, CAP * 28), 1), CAP)

    def outgoing(rank):
        match = jnp.logical_and(mig_dest[...] == rank, entry == inner // 2)
        source = jnp.sum(jnp.where(match, (mig_page[...] + 1).astype(F32), 0.0), axis=1, keepdims=True)
        source = source.astype(jnp.int32) * 2 - 2 + lax.rem(inner, 2)
        return (source == iota((384, 144), 1)).astype(BF)

    first, second = row // 48, lax.rem(row, 48) // 6
    a_y1[...] = dot(outgoing(first * NG + second), own[:, :384], nn).astype(BF).reshape(NY, 48, 384)
    a_z1[...] = dot(outgoing(second * NG + first), own[:, 384:], nn).astype(BF).reshape(NG, 48, 192)
    q_all[t] = q[...]

    pl.semaphore_wait(barrier, 21)
    along_y, along_g = links.reserve(NY), links.reserve(NG)
    for k in range(1, NY):
        links.send(along_y + k, a_y1.at[y_to[k]], a_y2.at[y], dp_of(y_to[k]), t)
        links.send(along_g + k, a_z1.at[g_to[k]], a_z2.at[g], group(g_to[k]), t)
    to_heads = links.reserve(NT)
    for k in range(1, NT):
        links.send(to_heads + k, q_all.at[t], q_all.at[t], dp, t_to[k])
    a_y2[y] = a_y1[y]
    a_z2[g] = a_z1[g]

    row, col = iota((128, 1), 0), iota((128, 112), 1)
    spread = jnp.logical_and(lax.rem(row, 16) < 14, col == lax.rem(row, 16) * 8 + row // 16).astype(BF)
    w_o[...] = dot(spread, w_out[...], nn).astype(BF)
    row, col = iota((384, 1), 0), iota((384, 288), 1)
    spread = jnp.logical_and(lax.rem(row, 48) < 36, col == (row // 48) * 36 + lax.rem(row, 48)).astype(BF)
    w_d[...] = dot(spread, w_down[...], nn).astype(BF)

    for k in range(1, NY):
        links.arrived(along_y + k, a_y2.at[y_from[k]], dp_of(y_from[k]), t)
        links.arrived(along_g + k, a_z2.at[g_from[k]], group(g_from[k]), t)
    row, col = iota((384, 1), 0), iota((384, 384), 1)
    swap = (col == (lax.rem(row, 48) // 6) * 48 + (row // 48) * 6 + lax.rem(row, 6)).astype(BF)
    a_y3[...] = dot(swap, a_y2[...].reshape(384, 384), nn).astype(BF).reshape(NG, 48, 384)
    a_z3[...] = dot(swap, a_z2[...].reshape(384, 192), nn).astype(BF).reshape(NY, 48, 192)
    along_g, along_y = links.reserve(NG), links.reserve(NY)
    for k in range(1, NY):
        links.send(along_g + k, a_y3.at[g_to[k]], a_y4.at[g], group(g_to[k]), t)
        links.send(along_y + k, a_z3.at[y_to[k]], a_z4.at[y], dp_of(y_to[k]), t)
    a_y4[g] = a_y3[g]
    a_z4[y] = a_z3[y]

    row, col = iota((NT * 80, 1), 0), iota((NT * 80, 288), 1)
    slot = lax.rem(row, 80)
    of_gate = jnp.logical_and(slot < 36, col == (row // 80) * 36 + slot).astype(BF)
    of_up = jnp.logical_and(jnp.logical_and(slot >= 40, slot < 76), col == (row // 80) * 36 + slot - 40).astype(BF)
    scale = gain[...].astype(F32)
    rows = dot(of_gate, (w_gate[...].astype(F32) * scale).astype(BF), nn)
    rows = (rows + dot(of_up, (w_up[...].astype(F32) * scale).astype(BF), nn)).astype(BF)
    row, col = iota((896, 1), 0), iota((896, 1024), 1)
    rank = row // 14
    at = lax.rem(rank, 2) * 512 + (rank // 2) * 16 + lax.rem(row, 14)
    spread = (col == at).astype(BF)
    squares_at = jnp.logical_and(lax.rem(iota((NT * 80, 1), 0), 80) == 36, lax.rem(iota((1, 1024), 1), 16) >= 14)
    w_gu[...] = jnp.where(squares_at, 1.0, dot(rows, spread, nn)).astype(BF)

    for k in range(1, NY):
        links.arrived(along_g + k, a_y4.at[g_from[k]], group(g_from[k]), t)
        links.arrived(along_y + k, a_z4.at[y_from[k]], dp_of(y_from[k]), t)

    row = iota((REQ * KEYS, 1), 0)
    place, request = lax.rem(row, KEYS), row // KEYS
    named = jnp.full((REQ * KEYS, 1), -1, jnp.int32)
    for r in range(REQ):
        for k in range(MAXP):
            named = jnp.where(jnp.logical_and(request == r, place // 2 == k), table[r, k], named)
    token = lax.rem(place, 2)
    from_own = (jnp.where(jnp.logical_and(named >= 0, named < POOL), 2 * named + token, -1) == iota((REQ * KEYS, 144), 1)).astype(BF)
    migrated = jnp.maximum(named - POOL, 0)
    rank = (migrated * 171) // 512
    inner = (migrated - CAP * rank) * 2 + token
    rank_y, rank_g = rank // NG, lax.rem(rank, NG)
    in_inbox = named >= POOL
    at = jnp.where(in_inbox, rank_g * 48 + rank_y * 6 + inner, -1)
    from_y = (at == iota((REQ * KEYS, 384), 1)).astype(BF)
    at = jnp.where(in_inbox, rank_y * 48 + rank_g * 6 + inner, -1)
    from_z = (at == iota((REQ * KEYS, 384), 1)).astype(BF)
    at = jnp.where(jnp.logical_and(place >= 26, place < 28), 2 * request + place - 26, -1)
    from_fresh = (at == iota((REQ * KEYS, 2 * REQ), 1)).astype(BF)
    low = dot(from_own, own[:, :384], nn) + dot(from_fresh, fresh[:, :384], nn)
    high = dot(from_own, own[:, 384:], nn) + dot(from_fresh, fresh[:, 384:], nn)
    low = low + dot(from_y, a_y4[...].reshape(384, 384), nn)
    high = high + dot(from_z, a_z4[...].reshape(384, 192), nn)
    keys[:, :, :384] = low.astype(BF).reshape(REQ, KEYS, 384)
    keys[:, :, 384:] = high.astype(BF).reshape(REQ, KEYS, 192)
    for k in range(1, NT):
        links.arrived(to_heads + k, q_all.at[t_from[k]], dp, t_from[k])

    scores = [dot(q_all[:, r].reshape(NT * 16, LAT), keys[r], nt) for r in range(REQ)]
    scores = jnp.concatenate(scores, axis=0) * SCALE
    row, col = iota((REQ * 128, 1), 0), iota((REQ * 128, KEYS), 1)
    length = jnp.full((REQ * 128, 1), lengths[0], jnp.int32)
    for r in range(1, REQ):
        length = jnp.where(row >= r * 128, lengths[r], length)
    cached = jnp.logical_and(col < 26, (col // 2) * PAGE + 2 * t + lax.rem(col, 2) < length)
    newer = jnp.logical_and(jnp.logical_and(col >= 26, col <= 26 + lax.rem(row // 8, 2)), t == 0)
    live = jnp.logical_or(cached, newer)
    scores = jnp.where(live, scores, DEAD)
    top = jnp.max(scores, axis=1, keepdims=True)
    weights = jnp.where(live, jnp.exp(scores - top), 0.0)
    total = jnp.sum(weights, axis=1, keepdims=True)
    some = total > 0.0
    total = jnp.where(some, total, 1.0)
    weights = (weights / total).astype(BF)
    lse = jnp.where(some, top + jnp.log(total), DEAD)
    high = lse.astype(BF).astype(F32)
    middle = (lse - high).astype(BF).astype(F32)
    low = lse - high - middle
    lane = iota((REQ * 128, 128), 1)
    parts = jnp.where(lane == 0, high, jnp.where(lane == 1, middle, jnp.where(lane == 2, low, 0.0))).astype(BF)
    for r in range(REQ):
        latent = dot(weights[r * 128 : (r + 1) * 128], keys[r][:, :KVL], nn)
        o_out[:, r, :, :KVL] = latent.astype(BF).reshape(NT, 16, KVL)
        o_out[:, r, :, KVL:] = parts[r * 128 : (r + 1) * 128].reshape(NT, 16, 128)
    slot = links.reserve(NT)
    for k in range(1, NT):
        links.send(slot + k, o_out.at[t_to[k]], o_in.at[t], dp, t_to[k])
    o_in[t] = o_out[t]
    for k in range(1, NT):
        links.arrived(slot + k, o_in.at[t_from[k]], dp, t_from[k])
    lse = [jnp.sum(o_in[s, :, :, KVL:].astype(F32), axis=2, keepdims=True) for s in range(NT)]
    top = functools.reduce(jnp.maximum, lse)
    shares = [jnp.exp(v - top) for v in lse]
    total = functools.reduce(jnp.add, shares)
    latent = jnp.zeros((REQ, 16, KVL), F32)
    for s in range(NT):
        latent = latent + o_in[s, :, :, :KVL].astype(F32) * (shares[s] / total)
    latent = latent.astype(BF).reshape(REQ * 16, KVL)

    of_token = (iota((16, 80), 1) // 8 == iota((16, 80), 0)).astype(BF)
    head = lax.rem(iota((80, HD), 0), 8)
    for h in range(8):
        values = jnp.where(head == h, dot(latent, w_uv[h], ((1,), (0,))), 0.0).astype(BF)
        values = dot(of_token, values, ((1,), (0,))).astype(BF)
        ho[h // 4, :, (h % 4) * HD : (h % 4 + 1) * HD] = values

    slot = links.reserve(NG)
    for k in range(1, NG):
        links.send(slot + k, ho.at[lax.rem(g_to[k], 2)], b_in.at[g], group(g_to[k]), t)
    b_in[g] = ho[core]
    for k in range(1, NG):
        links.arrived(slot + k, b_in.at[g_from[k]], group(g_from[k]), t)
    row, col = iota((80, 1), 0), iota((80, 128), 1)
    pack = (col == (row // 10) * 16 + lax.rem(row, 10)).astype(BF)
    heads[core, y] = dot(pack, b_in[...].reshape(128, KVL), ((1,), (0,))).astype(BF)
    ring_gather(links, heads, dp_of, y, core, t)

    for half in range(2):
        x = heads[half].reshape(TOK, KVL)
        add = dot(w_o[:, half * KVL : (half + 1) * KVL], x, nt)
        projected = add if half == 0 else projected + add
    pj[...] = projected.astype(BF).reshape(NT, 16, TOK)
    slot = links.reserve(NT)
    for k in range(1, NT):
        links.send(slot + k, pj.at[t_to[k]], c_in.at[t], dp, t_to[k])
    c_in[t] = pj[t]
    for k in range(1, NT):
        links.arrived(slot + k, c_in.at[t_from[k]], dp, t_from[k])
    summed = jnp.concatenate([res[...].astype(F32), jnp.zeros((2, TOK), F32)], axis=0)
    for s in range(NT):
        summed = summed + c_in[s].astype(F32)
    summed = summed.astype(BF).astype(F32)
    squares = jnp.sum(summed * summed, axis=0, keepdims=True)
    high = squares.astype(BF).astype(F32)
    row = iota((16, TOK), 0)
    piece = jnp.where(row == 14, high, jnp.where(row == 15, squares - high, summed)).astype(BF)
    stream[core, y, z] = piece

    slot = links.reserve(4)
    for k in range(1, 4):
        mine = stream.at[core, y, z]
        links.send(slot + k, mine, mine, group(z_to[k] * 2 + core), t)
    for k in range(1, 4):
        links.arrived(slot + k, stream.at[core, y, z_from[k]], group(z_from[k] * 2 + core), t)
    ring_gather(links, stream, dp_of, y, core, t)

    slot = links.reserve(NT)
    columns = stream[...].reshape(1024, TOK)
    for k in range(1, NT + 1):
        to = lax.rem(t + k, NT)
        first = pl.multiple_of(to * 80, 80)
        gu[to] = dot(w_gu[pl.ds(first, 80), :], columns, nn).astype(BF)
        if k < NT:
            links.send(slot + k, gu.at[to], e_in.at[t], dp, to)
        else:
            e_in[t] = gu[t]
    for k in range(1, NT):
        links.arrived(slot + k, e_in.at[t_from[k]], dp, t_from[k])
    total = jnp.zeros((80, TOK), F32)
    for s in range(NT):
        total = total + e_in[s].astype(F32)
    scale = lax.rsqrt(total[36:37] / D + EPS)
    gate, up = total[:40] * scale, total[40:] * scale
    hidden = gate / (1.0 + jnp.exp(-gate)) * up
    hidden = jnp.where(iota((40, TOK), 0) < 36, hidden, 0.0)
    hidden = jnp.concatenate([hidden, jnp.zeros((8, TOK), F32)], axis=0).astype(BF)
    h_all[t] = hidden
    slot = links.reserve(NT)
    for k in range(1, NT):
        links.send(slot + k, h_all.at[t], h_all.at[t], dp, t_to[k])
    for k in range(1, NT):
        links.arrived(slot + k, h_all.at[t_from[k]], dp, t_from[k])

    place = jnp.logical_and(iota((16, 896), 1) == dp * 14 + iota((16, 896), 0), iota((16, 896), 0) < 14).astype(BF)
    for block in range(TOK // 128):
        lanes = slice(block * 128, (block + 1) * 128)
        value = dot(h_all[:, :, lanes].reshape(384, 128), w_d[...], tn)
        part[lanes] = value + dot(stream[core, y, z, :, lanes], place, tn)

    partner = dp + 1 - 2 * core
    mine = pl.ds(pl.multiple_of(core * 384, 128), KVL)
    other = pl.ds(pl.multiple_of((1 - core) * 384, 128), KVL)
    f_out[...] = part[:, other].astype(BF)
    slot = links.reserve(1)
    links.send(slot, f_out, f_in, partner, t)
    links.arrived(slot, f_in, partner, t)
    acc[...] = (part[:, mine] + f_in[...].astype(F32)).reshape(NY, 80, KVL)
    right, left = dp_of(lax.rem(y + 1, NY)), dp_of(lax.rem(y + NY - 1, NY))
    to_right, to_left = links.reserve(4), links.reserve(3)
    for step in range(4):
        value = acc[lax.rem(y + 4 - step, NY)]
        if step > 0:
            links.arrived(to_right + step - 1, r_in.at[step - 1], left, t)
            value = value + r_in[step - 1].astype(F32)
        r_out[step] = value.astype(BF)
        links.send(to_right + step, r_out.at[step], r_in.at[step], right, t)
        if step < 3:
            value = acc[lax.rem(y + NY - 3 + step, NY)]
            if step > 0:
                links.arrived(to_left + step - 1, l_in.at[step - 1], right, t)
                value = value + l_in[step - 1].astype(F32)
            l_out[step] = value.astype(BF)
            links.send(to_left + step, l_out.at[step], l_in.at[step], left, t)
    links.arrived(to_right + 3, r_in.at[3], left, t)
    links.arrived(to_left + 2, l_in.at[2], right, t)
    value = (acc[y] + r_in[3].astype(F32) + l_in[2].astype(F32)).astype(BF)
    row, col = iota((128, 1), 0), iota((128, 80), 1)
    spread = jnp.logical_and(lax.rem(row, 16) < 10, col == (row // 16) * 10 + lax.rem(row, 16)).astype(BF)
    g_out[...] = dot(spread, value, nn).astype(BF).reshape(NG, 16, KVL)
    slot = links.reserve(NG)
    for k in range(1, NG):
        links.send(slot + k, g_out.at[g_to[k]], g_in.at[g], group(g_to[k]), t)
    g_in[g] = g_out[g]
    for k in range(1, NG):
        links.arrived(slot + k, g_in.at[g_from[k]], group(g_from[k]), t)
    first = jnp.zeros((16, KVL), F32)
    second = jnp.zeros((16, KVL), F32)
    for s in range(4):
        first = first + g_in[2 * s].astype(F32)
        second = second + g_in[2 * s + 1].astype(F32)
    out[:, :KVL] = first.astype(BF)[:10]
    out[:, KVL:] = second.astype(BF)[:10, 128:]
    links.finish()


SLOTS = 8 * 11 + 2 * 15 + 4 + 8


def layer(*operands):
    scratch = [
        ((144, LAT), BF),
        ((NY, 48, 384), BF),
        ((NY, 48, 384), BF),
        ((NG, 48, 384), BF),
        ((NG, 48, 384), BF),
        ((NG, 48, 192), BF),
        ((NG, 48, 192), BF),
        ((NY, 48, 192), BF),
        ((NY, 48, 192), BF),
        ((NT * 80, 1024), BF),
        ((128, 1024), BF),
        ((384, 896), BF),
        ((NT, REQ, 16, LAT), BF),
        ((REQ, KEYS, LAT), BF),
        ((NT, REQ, 16, 640), BF),
        ((NT, REQ, 16, 640), BF),
        ((2, 16, KVL), BF),
        ((NG, 16, KVL), BF),
        ((2, NY, 80, KVL), BF),
        ((NT, 16, TOK), BF),
        ((NT, 16, TOK), BF),
        ((2, NY, 4, 16, TOK), BF),
        ((NT, 80, TOK), BF),
        ((NT, 80, TOK), BF),
        ((NT, 48, TOK), BF),
        ((TOK, 896), F32),
        ((TOK, KVL), BF),
        ((TOK, KVL), BF),
        ((NY, 80, KVL), F32),
        ((4, 80, KVL), BF),
        ((4, 80, KVL), BF),
        ((3, 80, KVL), BF),
        ((3, 80, KVL), BF),
        ((NG, 16, KVL), BF),
        ((NG, 16, KVL), BF),
    ]
    smem = pl.BlockSpec(memory_space=pltpu.SMEM)
    vmem = pl.BlockSpec(memory_space=pltpu.VMEM)
    return pl.pallas_call(
        kernel,
        out_shape=jax.ShapeDtypeStruct((10, 896), BF),
        in_specs=[smem] * 2 + [vmem] * 12,
        out_specs=vmem,
        scratch_shapes=[pltpu.VMEM(shape, kind) for shape, kind in scratch]
        + [pltpu.SemaphoreType.DMA((SLOTS,)), pltpu.SemaphoreType.DMA((SLOTS,))],
        compiler_params=pltpu.CompilerParams(
            collective_id=0, has_side_effects=True, vmem_limit_bytes=48 * 1024 * 1024
        ),
        cost_estimate=pl.CostEstimate(flops=3 * 10**9, bytes_accessed=10**7, transcendentals=10**6),
        name="layer",
    )(*operands)


def local(
    pool,
    page_table,
    lengths,
    mig_page,
    mig_dest,
    queries,
    new_latent,
    w_uv,
    w_out,
    residual,
    norm_gain,
    w_gate,
    w_up,
    w_down,
):
    return layer(
        page_table,
        lengths,
        mig_page,
        mig_dest,
        queries.reshape(REQ, 16, LAT),
        pool.reshape(POOL * PAGE, LAT),
        new_latent,
        w_uv,
        w_out.transpose(2, 1, 0).reshape(112, 1024),
        residual.reshape(TOK, 14).T,
        norm_gain.reshape(1, 896),
        w_gate.T,
        w_up.T,
        w_down,
    )


def solution(mesh):
    in_specs = (
        P("dp", None, None),
        P("dp", None),
        P("dp"),
        P("dp", None),
        P("dp", None),
        P("dp", "tp", None),
        P("dp", None),
        P("tp", None, None),
        P("tp", None, "dp"),
        P(None, "tp", "dp"),
        P("tp"),
        P("tp", "dp"),
        P("tp", "dp"),
        P("dp", "tp"),
    )
    out_specs = P("dp", "tp")
    return jax.shard_map(local, mesh=mesh, in_specs=in_specs, out_specs=out_specs, check_vma=False)
```

```python
import functools

import jax
import jax.numpy as jnp
from jax import lax
from jax.experimental import pallas as pl
from jax.experimental.pallas import tpu as pltpu
from jax.sharding import PartitionSpec as P

D = 7168
HD = 128
KVL = 512
LAT = 576
PAGE = 16
MAXP = 13
REQ = 5
POOL = 65
CAP = 3
NY = 8
NG = 8
NT = 8
KEYS = 32
TOK = 640
EPS = 1e-06
SCALE = 192 ** (-0.5)
BF = jnp.bfloat16
F32 = jnp.float32
MESH = pl.DeviceIdType.MESH
DEAD = -1e30


def dot(a, b, dims):
    return lax.dot_general(a, b, (dims, ((), ())), preferred_element_type=F32)


def div(value, by):
    return lax.shift_right_logical(value * (-(-(1 << 20) // by)), 20)


def rem(value, by):
    return value - by * div(value, by)


def iota(shape, axis):
    return lax.broadcasted_iota(jnp.int32, shape, axis)


class Links:
    def __init__(self, send_sems, recv_sems):
        self.send_sems, self.recv_sems, self.used, self.sent = send_sems, recv_sems, 0, []

    def reserve(self, count):
        first = self.used
        self.used += count
        return first

    def copy(self, slot, src, dst, dp, tp):
        return pltpu.make_async_remote_copy(
            src_ref=src,
            dst_ref=dst,
            send_sem=self.send_sems.at[slot],
            recv_sem=self.recv_sems.at[slot],
            device_id={"dp": dp, "tp": tp},
            device_id_type=MESH,
        )

    def send(self, slot, src, dst, dp, tp):
        copy = self.copy(slot, src, dst, dp, tp)
        copy.start()
        self.sent.append(copy)

    def arrived(self, slot, dst, dp, tp):
        self.copy(slot, dst, dst, dp, tp).wait_recv()

    def finish(self):
        for copy in self.sent:
            copy.wait_send()


def ring_gather(links, buf, dp_of, y, core, tp):
    right, left = dp_of(lax.rem(y + 1, NY)), dp_of(lax.rem(y + NY - 1, NY))
    partner = dp_of(y) + 1 - 2 * core
    to_right, to_left, over = links.reserve(4), links.reserve(3), links.reserve(8)

    def pass_on(order, index):
        links.send(over + order, buf.at[core, index], buf.at[core, index], partner, tp)

    links.send(to_right, buf.at[core, y], buf.at[core, y], right, tp)
    links.send(to_left, buf.at[core, y], buf.at[core, y], left, tp)
    pass_on(0, y)
    indices = [y]
    for step in range(4):
        index = lax.rem(y + NY - 1 - step, NY)
        links.arrived(to_right + step, buf.at[core, index], left, tp)
        if step < 3:
            links.send(to_right + step + 1, buf.at[core, index], buf.at[core, index], right, tp)
        pass_on(len(indices), index)
        indices.append(index)
        if step < 3:
            index = lax.rem(y + 1 + step, NY)
            links.arrived(to_left + step, buf.at[core, index], right, tp)
            if step < 2:
                links.send(to_left + step + 1, buf.at[core, index], buf.at[core, index], left, tp)
            pass_on(len(indices), index)
            indices.append(index)
    for order, index in enumerate(indices):
        links.arrived(over + order, buf.at[1 - core, index], partner, tp)


def kernel(
    *refs
):
    operands, (out, *held), rest = refs[:14], refs[14:29], refs[29:]
    (
        table, lengths, mig_page, mig_dest, q, pool, fresh, w_uv, w_out, res, gain, w_gate, w_up, w_down
    ) = held
    (
    own, a_y1, a_y2, a_y3, a_y4, a_z1, a_z2, a_z3, a_z4, w_gu, w_o, w_d,
    q_all, keys, o_out, o_in, ho, b_in, heads, pj, c_in, stream, gu, e_in, h_all, part, f_out, f_in,
    acc, r_out, r_in, l_out, l_in, g_out, g_in, send_sems, recv_sems, load_sems,
    ) = rest
    loads = [pltpu.make_async_copy(*pair, load_sems.at[i]) for i, pair in enumerate(zip(operands, held))]
    for i in (5, 2, 3, 4, 8, 13, 10, 11, 12, 6, 0, 1, 7, 9):
        loads[i].start()

    dp, t = lax.axis_index("dp"), lax.axis_index("tp")
    y, g = dp // NG, lax.rem(dp, NG)
    z, core = g // 2, lax.rem(g, 2)
    links = Links(send_sems, recv_sems)
    t_to = [lax.rem(t + k, NT) for k in range(NT)]
    t_from = [lax.rem(t + NT - k, NT) for k in range(NT)]
    g_to = [lax.rem(g + k, NG) for k in range(NG)]
    g_from = [lax.rem(g + NG - k, NG) for k in range(NG)]
    y_to = [lax.rem(y + k, NY) for k in range(NY)]
    y_from = [lax.rem(y + NY - k, NY) for k in range(NY)]
    z_to = [lax.rem(z + k, 4) for k in range(4)]
    z_from = [lax.rem(z + 4 - k, 4) for k in range(4)]
    nn, nt, tn = ((1,), (0,)), ((1,), (1,)), ((0,), (0,))

    def dp_of(yy):
        return yy * NG + g

    def group(gg):
        return y * NG + gg

    barrier = pltpu.get_barrier_semaphore()
    for k in range(1, NT):
        pl.semaphore_signal(barrier, inc=1, device_id={"dp": dp, "tp": t_to[k]}, device_id_type=MESH)
    for k in range(1, NG):
        pl.semaphore_signal(barrier, inc=1, device_id={"dp": group(g_to[k]), "tp": t}, device_id_type=MESH)
    for k in range(1, NY):
        pl.semaphore_signal(barrier, inc=1, device_id={"dp": dp_of(y_to[k]), "tp": t}, device_id_type=MESH)

    for i in (5, 2, 3, 4):
        loads[i].wait()
    row = iota((144, 1), 0)
    column = (div(row, 2)) * PAGE + 2 * t + rem(row, 2)
    own[...] = dot((column == iota((144, POOL * PAGE), 1)).astype(BF), pool[...], nn).astype(BF)
    row = iota((384, 1), 0)
    inner = rem(row, 6)
    entry = rem(iota((1, CAP * 28), 1), CAP)

    def outgoing(rank):
        match = jnp.logical_and(mig_dest[...] == rank, entry == div(inner, 2))
        source = jnp.sum(jnp.where(match, (mig_page[...] + 1).astype(F32), 0.0), axis=1, keepdims=True)
        source = source.astype(jnp.int32) * 2 - 2 + rem(inner, 2)
        return (source == iota((384, 144), 1)).astype(BF)

    first, second = div(row, 48), div(rem(row, 48), 6)
    a_y1[...] = dot(outgoing(first * NG + second), own[:, :384], nn).astype(BF).reshape(NY, 48, 384)
    a_z1[...] = dot(outgoing(second * NG + first), own[:, 384:], nn).astype(BF).reshape(NG, 48, 192)
    q_all[t] = q[...]

    pl.semaphore_wait(barrier, 21)
    along_y, along_g = links.reserve(NY), links.reserve(NG)
    for k in range(1, NY):
        links.send(along_y + k, a_y1.at[y_to[k]], a_y2.at[y], dp_of(y_to[k]), t)
        links.send(along_g + k, a_z1.at[g_to[k]], a_z2.at[g], group(g_to[k]), t)
    to_heads = links.reserve(NT)
    for k in range(1, NT):
        links.send(to_heads + k, q_all.at[t], q_all.at[t], dp, t_to[k])
    a_y2[y] = a_y1[y]
    a_z2[g] = a_z1[g]

    for i in (8, 13, 10, 11, 12):
        loads[i].wait()
    row, col = iota((128, 1), 0), iota((128, 112), 1)
    spread = jnp.logical_and(rem(row, 16) < 14, col == rem(row, 16) * 8 + div(row, 16)).astype(BF)
    w_o[...] = dot(spread, w_out[...], nn).astype(BF)
    row, col = iota((384, 1), 0), iota((384, 288), 1)
    spread = jnp.logical_and(rem(row, 48) < 36, col == (div(row, 48)) * 36 + rem(row, 48)).astype(BF)
    w_d[...] = dot(spread, w_down[...], nn).astype(BF)

    for k in range(1, NY):
        links.arrived(along_y + k, a_y2.at[y_from[k]], dp_of(y_from[k]), t)
        links.arrived(along_g + k, a_z2.at[g_from[k]], group(g_from[k]), t)
    row, col = iota((384, 1), 0), iota((384, 384), 1)
    swap = (col == (div(rem(row, 48), 6)) * 48 + (div(row, 48)) * 6 + rem(row, 6)).astype(BF)
    a_y3[...] = dot(swap, a_y2[...].reshape(384, 384), nn).astype(BF).reshape(NG, 48, 384)
    a_z3[...] = dot(swap, a_z2[...].reshape(384, 192), nn).astype(BF).reshape(NY, 48, 192)
    along_g, along_y = links.reserve(NG), links.reserve(NY)
    for k in range(1, NY):
        links.send(along_g + k, a_y3.at[g_to[k]], a_y4.at[g], group(g_to[k]), t)
        links.send(along_y + k, a_z3.at[y_to[k]], a_z4.at[y], dp_of(y_to[k]), t)
    a_y4[g] = a_y3[g]
    a_z4[y] = a_z3[y]

    row, col = iota((NT * 80, 1), 0), iota((NT * 80, 288), 1)
    slot = rem(row, 80)
    of_gate = jnp.logical_and(slot < 36, col == (div(row, 80)) * 36 + slot).astype(BF)
    of_up = jnp.logical_and(jnp.logical_and(slot >= 40, slot < 76), col == (div(row, 80)) * 36 + slot - 40).astype(BF)
    scale = gain[...].astype(F32)
    rows = dot(of_gate, (w_gate[...].astype(F32) * scale).astype(BF), nn)
    rows = (rows + dot(of_up, (w_up[...].astype(F32) * scale).astype(BF), nn)).astype(BF)
    row, col = iota((896, 1), 0), iota((896, 1024), 1)
    rank = div(row, 14)
    at = rem(rank, 2) * 512 + (div(rank, 2)) * 16 + rem(row, 14)
    spread = (col == at).astype(BF)
    squares_at = jnp.logical_and(rem(iota((NT * 80, 1), 0), 80) == 36, rem(iota((1, 1024), 1), 16) >= 14)
    w_gu[...] = jnp.where(squares_at, 1.0, dot(rows, spread, nn)).astype(BF)

    for k in range(1, NY):
        links.arrived(along_g + k, a_y4.at[g_from[k]], group(g_from[k]), t)
        links.arrived(along_y + k, a_z4.at[y_from[k]], dp_of(y_from[k]), t)

    for i in (6, 0, 1):
        loads[i].wait()
    row = iota((REQ * KEYS, 1), 0)
    place, request = rem(row, KEYS), div(row, KEYS)
    named = jnp.full((REQ * KEYS, 1), -1, jnp.int32)
    for r in range(REQ):
        for k in range(MAXP):
            named = jnp.where(jnp.logical_and(request == r, div(place, 2) == k), table[r, k], named)
    token = rem(place, 2)
    from_own = (jnp.where(jnp.logical_and(named >= 0, named < POOL), 2 * named + token, -1) == iota((REQ * KEYS, 144), 1)).astype(BF)
    migrated = jnp.maximum(named - POOL, 0)
    rank = div(migrated, 3)
    inner = (migrated - CAP * rank) * 2 + token
    rank_y, rank_g = div(rank, NG), rem(rank, NG)
    in_inbox = named >= POOL
    at = jnp.where(in_inbox, rank_g * 48 + rank_y * 6 + inner, -1)
    from_y = (at == iota((REQ * KEYS, 384), 1)).astype(BF)
    at = jnp.where(in_inbox, rank_y * 48 + rank_g * 6 + inner, -1)
    from_z = (at == iota((REQ * KEYS, 384), 1)).astype(BF)
    at = jnp.where(jnp.logical_and(place >= 26, place < 28), 2 * request + place - 26, -1)
    from_fresh = (at == iota((REQ * KEYS, 2 * REQ), 1)).astype(BF)
    low = dot(from_own, own[:, :384], nn) + dot(from_fresh, fresh[:, :384], nn)
    high = dot(from_own, own[:, 384:], nn) + dot(from_fresh, fresh[:, 384:], nn)
    low = low + dot(from_y, a_y4[...].reshape(384, 384), nn)
    high = high + dot(from_z, a_z4[...].reshape(384, 192), nn)
    keys[:, :, :384] = low.astype(BF).reshape(REQ, KEYS, 384)
    keys[:, :, 384:] = high.astype(BF).reshape(REQ, KEYS, 192)
    for k in range(1, NT):
        links.arrived(to_heads + k, q_all.at[t_from[k]], dp, t_from[k])

    scores = [dot(q_all[:, r].reshape(NT * 16, LAT), keys[r], nt) for r in range(REQ)]
    scores = jnp.concatenate(scores, axis=0) * SCALE
    row, col = iota((REQ * 128, 1), 0), iota((REQ * 128, KEYS), 1)
    length = jnp.full((REQ * 128, 1), lengths[0], jnp.int32)
    for r in range(1, REQ):
        length = jnp.where(row >= r * 128, lengths[r], length)
    cached = jnp.logical_and(col < 26, (div(col, 2)) * PAGE + 2 * t + rem(col, 2) < length)
    newer = jnp.logical_and(jnp.logical_and(col >= 26, col <= 26 + rem(div(row, 8), 2)), t == 0)
    live = jnp.logical_or(cached, newer)
    scores = jnp.where(live, scores, DEAD)
    top = jnp.max(scores, axis=1, keepdims=True)
    weights = jnp.where(live, jnp.exp(scores - top), 0.0)
    total = jnp.sum(weights, axis=1, keepdims=True)
    some = total > 0.0
    total = jnp.where(some, total, 1.0)
    weights = (weights / total).astype(BF)
    lse = jnp.where(some, top + jnp.log(total), DEAD)
    high = lse.astype(BF).astype(F32)
    middle = (lse - high).astype(BF).astype(F32)
    low = lse - high - middle
    lane = iota((REQ * 128, 128), 1)
    parts = jnp.where(lane == 0, high, jnp.where(lane == 1, middle, jnp.where(lane == 2, low, 0.0))).astype(BF)
    for r in range(REQ):
        latent = dot(weights[r * 128 : (r + 1) * 128], keys[r][:, :KVL], nn)
        o_out[:, r, :, :KVL] = latent.astype(BF).reshape(NT, 16, KVL)
        o_out[:, r, :, KVL:] = parts[r * 128 : (r + 1) * 128].reshape(NT, 16, 128)
    slot = links.reserve(NT)
    for k in range(1, NT):
        links.send(slot + k, o_out.at[t_to[k]], o_in.at[t], dp, t_to[k])
    o_in[t] = o_out[t]
    for k in range(1, NT):
        links.arrived(slot + k, o_in.at[t_from[k]], dp, t_from[k])
    lse = [jnp.sum(o_in[s, :, :, KVL:].astype(F32), axis=2, keepdims=True) for s in range(NT)]
    top = functools.reduce(jnp.maximum, lse)
    shares = [jnp.exp(v - top) for v in lse]
    total = functools.reduce(jnp.add, shares)
    latent = jnp.zeros((REQ, 16, KVL), F32)
    for s in range(NT):
        latent = latent + o_in[s, :, :, :KVL].astype(F32) * (shares[s] / total)
    latent = latent.astype(BF).reshape(REQ * 16, KVL)

    for i in (7, 9):
        loads[i].wait()
    of_token = (div(iota((16, 80), 1), 8) == iota((16, 80), 0)).astype(BF)
    head = rem(iota((80, HD), 0), 8)
    for h in range(8):
        values = jnp.where(head == h, dot(latent, w_uv[h], ((1,), (0,))), 0.0).astype(BF)
        values = dot(of_token, values, ((1,), (0,))).astype(BF)
        ho[h // 4, :, (h % 4) * HD : (h % 4 + 1) * HD] = values

    slot = links.reserve(NG)
    for k in range(1, NG):
        links.send(slot + k, ho.at[lax.rem(g_to[k], 2)], b_in.at[g], group(g_to[k]), t)
    b_in[g] = ho[core]
    for k in range(1, NG):
        links.arrived(slot + k, b_in.at[g_from[k]], group(g_from[k]), t)
    row, col = iota((80, 1), 0), iota((80, 128), 1)
    pack = (col == (div(row, 10)) * 16 + rem(row, 10)).astype(BF)
    heads[core, y] = dot(pack, b_in[...].reshape(128, KVL), ((1,), (0,))).astype(BF)
    ring_gather(links, heads, dp_of, y, core, t)

    for half in range(2):
        x = heads[half].reshape(TOK, KVL)
        add = dot(w_o[:, half * KVL : (half + 1) * KVL], x, nt)
        projected = add if half == 0 else projected + add
    pj[...] = projected.astype(BF).reshape(NT, 16, TOK)
    slot = links.reserve(NT)
    for k in range(1, NT):
        links.send(slot + k, pj.at[t_to[k]], c_in.at[t], dp, t_to[k])
    c_in[t] = pj[t]
    for k in range(1, NT):
        links.arrived(slot + k, c_in.at[t_from[k]], dp, t_from[k])
    summed = jnp.concatenate([res[...].astype(F32), jnp.zeros((2, TOK), F32)], axis=0)
    for s in range(NT):
        summed = summed + c_in[s].astype(F32)
    summed = summed.astype(BF).astype(F32)
    squares = jnp.sum(summed * summed, axis=0, keepdims=True)
    high = squares.astype(BF).astype(F32)
    row = iota((16, TOK), 0)
    piece = jnp.where(row == 14, high, jnp.where(row == 15, squares - high, summed)).astype(BF)
    stream[core, y, z] = piece

    slot = links.reserve(4)
    for k in range(1, 4):
        mine = stream.at[core, y, z]
        links.send(slot + k, mine, mine, group(z_to[k] * 2 + core), t)
    for k in range(1, 4):
        links.arrived(slot + k, stream.at[core, y, z_from[k]], group(z_from[k] * 2 + core), t)
    ring_gather(links, stream, dp_of, y, core, t)

    slot = links.reserve(NT)
    columns = stream[...].reshape(1024, TOK)
    for k in range(1, NT + 1):
        to = lax.rem(t + k, NT)
        first = pl.multiple_of(to * 80, 80)
        gu[to] = dot(w_gu[pl.ds(first, 80), :], columns, nn).astype(BF)
        if k < NT:
            links.send(slot + k, gu.at[to], e_in.at[t], dp, to)
        else:
            e_in[t] = gu[t]
    for k in range(1, NT):
        links.arrived(slot + k, e_in.at[t_from[k]], dp, t_from[k])
    total = jnp.zeros((80, TOK), F32)
    for s in range(NT):
        total = total + e_in[s].astype(F32)
    scale = lax.rsqrt(total[36:37] / D + EPS)
    gate, up = total[:40] * scale, total[40:] * scale
    hidden = gate / (1.0 + jnp.exp(-gate)) * up
    hidden = jnp.where(iota((40, TOK), 0) < 36, hidden, 0.0)
    hidden = jnp.concatenate([hidden, jnp.zeros((8, TOK), F32)], axis=0).astype(BF)
    h_all[t] = hidden
    slot = links.reserve(NT)
    for k in range(1, NT):
        links.send(slot + k, h_all.at[t], h_all.at[t], dp, t_to[k])
    for k in range(1, NT):
        links.arrived(slot + k, h_all.at[t_from[k]], dp, t_from[k])

    place = jnp.logical_and(iota((16, 896), 1) == dp * 14 + iota((16, 896), 0), iota((16, 896), 0) < 14).astype(BF)
    for block in range(TOK // 128):
        lanes = slice(block * 128, (block + 1) * 128)
        value = dot(h_all[:, :, lanes].reshape(384, 128), w_d[...], tn)
        part[lanes] = value + dot(stream[core, y, z, :, lanes], place, tn)

    partner = dp + 1 - 2 * core
    mine = pl.ds(pl.multiple_of(core * 384, 128), KVL)
    other = pl.ds(pl.multiple_of((1 - core) * 384, 128), KVL)
    f_out[...] = part[:, other].astype(BF)
    slot = links.reserve(1)
    links.send(slot, f_out, f_in, partner, t)
    links.arrived(slot, f_in, partner, t)
    acc[...] = (part[:, mine] + f_in[...].astype(F32)).reshape(NY, 80, KVL)
    right, left = dp_of(lax.rem(y + 1, NY)), dp_of(lax.rem(y + NY - 1, NY))
    to_right, to_left = links.reserve(4), links.reserve(3)
    for step in range(4):
        value = acc[lax.rem(y + 4 - step, NY)]
        if step > 0:
            links.arrived(to_right + step - 1, r_in.at[step - 1], left, t)
            value = value + r_in[step - 1].astype(F32)
        r_out[step] = value.astype(BF)
        links.send(to_right + step, r_out.at[step], r_in.at[step], right, t)
        if step < 3:
            value = acc[lax.rem(y + NY - 3 + step, NY)]
            if step > 0:
                links.arrived(to_left + step - 1, l_in.at[step - 1], right, t)
                value = value + l_in[step - 1].astype(F32)
            l_out[step] = value.astype(BF)
            links.send(to_left + step, l_out.at[step], l_in.at[step], left, t)
    links.arrived(to_right + 3, r_in.at[3], left, t)
    links.arrived(to_left + 2, l_in.at[2], right, t)
    value = (acc[y] + r_in[3].astype(F32) + l_in[2].astype(F32)).astype(BF)
    row, col = iota((128, 1), 0), iota((128, 80), 1)
    spread = jnp.logical_and(rem(row, 16) < 10, col == (div(row, 16)) * 10 + rem(row, 16)).astype(BF)
    g_out[...] = dot(spread, value, nn).astype(BF).reshape(NG, 16, KVL)
    slot = links.reserve(NG)
    for k in range(1, NG):
        links.send(slot + k, g_out.at[g_to[k]], g_in.at[g], group(g_to[k]), t)
    g_in[g] = g_out[g]
    for k in range(1, NG):
        links.arrived(slot + k, g_in.at[g_from[k]], group(g_from[k]), t)
    first = jnp.zeros((16, KVL), F32)
    second = jnp.zeros((16, KVL), F32)
    for s in range(4):
        first = first + g_in[2 * s].astype(F32)
        second = second + g_in[2 * s + 1].astype(F32)
    out[:, :KVL] = first.astype(BF)[:10]
    out[:, KVL:] = second.astype(BF)[:10, 128:]
    links.finish()


SLOTS = 8 * 11 + 2 * 15 + 4 + 8


def layer(*operands):
    scratch = [
        ((144, LAT), BF),
        ((NY, 48, 384), BF),
        ((NY, 48, 384), BF),
        ((NG, 48, 384), BF),
        ((NG, 48, 384), BF),
        ((NG, 48, 192), BF),
        ((NG, 48, 192), BF),
        ((NY, 48, 192), BF),
        ((NY, 48, 192), BF),
        ((NT * 80, 1024), BF),
        ((128, 1024), BF),
        ((384, 896), BF),
        ((NT, REQ, 16, LAT), BF),
        ((REQ, KEYS, LAT), BF),
        ((NT, REQ, 16, 640), BF),
        ((NT, REQ, 16, 640), BF),
        ((2, 16, KVL), BF),
        ((NG, 16, KVL), BF),
        ((2, NY, 80, KVL), BF),
        ((NT, 16, TOK), BF),
        ((NT, 16, TOK), BF),
        ((2, NY, 4, 16, TOK), BF),
        ((NT, 80, TOK), BF),
        ((NT, 80, TOK), BF),
        ((NT, 48, TOK), BF),
        ((TOK, 896), F32),
        ((TOK, KVL), BF),
        ((TOK, KVL), BF),
        ((NY, 80, KVL), F32),
        ((4, 80, KVL), BF),
        ((4, 80, KVL), BF),
        ((3, 80, KVL), BF),
        ((3, 80, KVL), BF),
        ((NG, 16, KVL), BF),
        ((NG, 16, KVL), BF),
    ]
    vmem = pl.BlockSpec(memory_space=pltpu.VMEM)
    held = [
        (pltpu.SMEM if i < 2 else pltpu.VMEM)(operand.shape, operand.dtype) for i, operand in enumerate(operands)
    ]
    return pl.pallas_call(
        kernel,
        out_shape=jax.ShapeDtypeStruct((10, 896), BF),
        in_specs=[pl.BlockSpec(memory_space=pl.ANY)] * 14,
        out_specs=vmem,
        scratch_shapes=held
        + [pltpu.VMEM(shape, kind) for shape, kind in scratch]
        + [pltpu.SemaphoreType.DMA((SLOTS,)), pltpu.SemaphoreType.DMA((SLOTS,)), pltpu.SemaphoreType.DMA((14,))],
        compiler_params=pltpu.CompilerParams(
            collective_id=0, has_side_effects=True, vmem_limit_bytes=60 * 1024 * 1024
        ),
        cost_estimate=pl.CostEstimate(flops=3 * 10**9, bytes_accessed=10**7, transcendentals=10**6),
        name="layer",
    )(*operands)


def local(
    pool,
    page_table,
    lengths,
    mig_page,
    mig_dest,
    queries,
    new_latent,
    w_uv,
    w_out,
    residual,
    norm_gain,
    w_gate,
    w_up,
    w_down,
):
    return layer(
        page_table,
        lengths,
        mig_page,
        mig_dest,
        queries.reshape(REQ, 16, LAT),
        pool.reshape(POOL * PAGE, LAT),
        new_latent,
        w_uv,
        w_out.transpose(2, 1, 0).reshape(112, 1024),
        residual.reshape(TOK, 14).T,
        norm_gain.reshape(1, 896),
        w_gate.T,
        w_up.T,
        w_down,
    )


def solution(mesh):
    in_specs = (
        P("dp", None, None),
        P("dp", None),
        P("dp"),
        P("dp", None),
        P("dp", None),
        P("dp", "tp", None),
        P("dp", None),
        P("tp", None, None),
        P("tp", None, "dp"),
        P(None, "tp", "dp"),
        P("tp"),
        P("tp", "dp"),
        P("tp", "dp"),
        P("dp", "tp"),
    )
    out_specs = P("dp", "tp")
    return jax.shard_map(local, mesh=mesh, in_specs=in_specs, out_specs=out_specs, check_vma=False)
```

```python
import functools

import jax
import jax.numpy as jnp
from jax import lax
from jax.experimental import pallas as pl
from jax.experimental.pallas import tpu as pltpu
from jax.sharding import PartitionSpec as P

D = 7168
HD = 128
KVL = 512
LAT = 576
PAGE = 16
MAXP = 13
REQ = 5
POOL = 65
CAP = 3
NY = 8
NG = 8
NT = 8
KEYS = 32
TOK = 640
EPS = 1e-06
SCALE = 192 ** (-0.5)
BF = jnp.bfloat16
F32 = jnp.float32
MESH = pl.DeviceIdType.MESH
DEAD = -1e30
ROWS = (48, 32)
PER_HALF = 14
DONE = object()


def dot(a, b, dims):
    return lax.dot_general(a, b, (dims, ((), ())), preferred_element_type=F32)


def div(value, by):
    return lax.shift_right_logical(value * (-(-(1 << 20) // by)), 20)


def rem(value, by):
    return value - by * div(value, by)


def iota(shape, axis):
    return lax.broadcasted_iota(jnp.int32, shape, axis)


class Links:
    def __init__(self, send_sems, recv_sems):
        self.send_sems, self.recv_sems, self.used, self.sent = send_sems, recv_sems, 0, []

    def reserve(self, count):
        first = self.used
        self.used += count
        return first

    def copy(self, slot, src, dst, dp, tp):
        return pltpu.make_async_remote_copy(
            src_ref=src,
            dst_ref=dst,
            send_sem=self.send_sems.at[slot],
            recv_sem=self.recv_sems.at[slot],
            device_id={"dp": dp, "tp": tp},
            device_id_type=MESH,
        )

    def send(self, slot, src, dst, dp, tp):
        copy = self.copy(slot, src, dst, dp, tp)
        copy.start()
        self.sent.append(copy)

    def arrived(self, slot, dst, dp, tp):
        self.copy(slot, dst, dst, dp, tp).wait_recv()

    def finish(self):
        for copy in self.sent:
            copy.wait_send()


def kernel(
    *refs
):
    operands, (out, *held), rest = refs[:14], refs[14:29], refs[29:]
    (
        table, lengths, mig_page, mig_dest, q, pool, fresh, w_uv, w_out, res, gain, w_gate, w_up, w_down
    ) = held
    (
    own, a_y1, a_y2, a_y3, a_y4, a_z1, a_z2, a_z3, a_z4, w_gu, w_o, w_d,
    q_all, keys, o_out, o_in, ho, b_in, last, g_out, g_in, *halves, send_sems, recv_sems, load_sems,
    ) = rest
    loads = [pltpu.make_async_copy(*pair, load_sems.at[i]) for i, pair in enumerate(zip(operands, held))]
    for i in (5, 2, 3, 4, 8, 9, 13, 10, 11, 12, 6, 0, 1, 7):
        loads[i].start()

    dp, t = lax.axis_index("dp"), lax.axis_index("tp")
    y, g = dp // NG, lax.rem(dp, NG)
    z, core = g // 2, lax.rem(g, 2)
    links = Links(send_sems, recv_sems)
    t_to = [lax.rem(t + k, NT) for k in range(NT)]
    t_from = [lax.rem(t + NT - k, NT) for k in range(NT)]
    g_to = [lax.rem(g + k, NG) for k in range(NG)]
    g_from = [lax.rem(g + NG - k, NG) for k in range(NG)]
    y_to = [lax.rem(y + k, NY) for k in range(NY)]
    y_from = [lax.rem(y + NY - k, NY) for k in range(NY)]
    z_to = [lax.rem(z + k, 4) for k in range(4)]
    z_from = [lax.rem(z + 4 - k, 4) for k in range(4)]
    nn, nt, tn = ((1,), (0,)), ((1,), (1,)), ((0,), (0,))

    def dp_of(yy):
        return yy * NG + g

    def group(gg):
        return y * NG + gg

    barrier = pltpu.get_barrier_semaphore()
    for k in range(1, NT):
        pl.semaphore_signal(barrier, inc=1, device_id={"dp": dp, "tp": t_to[k]}, device_id_type=MESH)
    for k in range(1, NG):
        pl.semaphore_signal(barrier, inc=1, device_id={"dp": group(g_to[k]), "tp": t}, device_id_type=MESH)
    for k in range(1, NY):
        pl.semaphore_signal(barrier, inc=1, device_id={"dp": dp_of(y_to[k]), "tp": t}, device_id_type=MESH)

    for i in (5, 2, 3, 4):
        loads[i].wait()
    row = iota((144, 1), 0)
    column = (div(row, 2)) * PAGE + 2 * t + rem(row, 2)
    own[...] = dot((column == iota((144, POOL * PAGE), 1)).astype(BF), pool[...], nn).astype(BF)
    row = iota((384, 1), 0)
    inner = rem(row, 6)
    entry = rem(iota((1, CAP * 28), 1), CAP)

    def outgoing(rank):
        match = jnp.logical_and(mig_dest[...] == rank, entry == div(inner, 2))
        source = jnp.sum(jnp.where(match, (mig_page[...] + 1).astype(F32), 0.0), axis=1, keepdims=True)
        source = source.astype(jnp.int32) * 2 - 2 + rem(inner, 2)
        return (source == iota((384, 144), 1)).astype(BF)

    first, second = div(row, 48), div(rem(row, 48), 6)
    a_y1[...] = dot(outgoing(first * NG + second), own[:, :384], nn).astype(BF).reshape(NY, 48, 384)
    a_z1[...] = dot(outgoing(second * NG + first), own[:, 384:], nn).astype(BF).reshape(NG, 48, 192)
    q_all[t] = q[...]

    pl.semaphore_wait(barrier, 21)
    along_y, along_g = links.reserve(NY), links.reserve(NG)
    for k in range(1, NY):
        links.send(along_y + k, a_y1.at[y_to[k]], a_y2.at[y], dp_of(y_to[k]), t)
        links.send(along_g + k, a_z1.at[g_to[k]], a_z2.at[g], group(g_to[k]), t)
    to_heads = links.reserve(NT)
    for k in range(1, NT):
        links.send(to_heads + k, q_all.at[t], q_all.at[t], dp, t_to[k])
    a_y2[y] = a_y1[y]
    a_z2[g] = a_z1[g]

    for i in (8, 9, 13, 10, 11, 12):
        loads[i].wait()
    row, col = iota((128, 1), 0), iota((128, 112), 1)
    spread = jnp.logical_and(rem(row, 16) < 14, col == rem(row, 16) * 8 + div(row, 16)).astype(BF)
    w_o[...] = dot(spread, w_out[...], nn).astype(BF)
    row, col = iota((384, 1), 0), iota((384, 288), 1)
    spread = jnp.logical_and(rem(row, 48) < 36, col == (div(row, 48)) * 36 + rem(row, 48)).astype(BF)
    w_d[...] = dot(spread, w_down[...], nn).astype(BF)
    for h, rows in enumerate(ROWS):
        row, col = iota((TOK, 1), 0), iota((1, NY * rows), 1)
        at = div(col, rows) * 80 + rem(col, rows) + h * ROWS[0]
        values = dot(res[...], (row == at).astype(BF), nn)
        halves[h * PER_HALF][...] = jnp.concatenate([values, jnp.zeros((2, NY * rows), F32)], axis=0)

    for k in range(1, NY):
        links.arrived(along_y + k, a_y2.at[y_from[k]], dp_of(y_from[k]), t)
        links.arrived(along_g + k, a_z2.at[g_from[k]], group(g_from[k]), t)
    row, col = iota((384, 1), 0), iota((384, 384), 1)
    swap = (col == (div(rem(row, 48), 6)) * 48 + (div(row, 48)) * 6 + rem(row, 6)).astype(BF)
    a_y3[...] = dot(swap, a_y2[...].reshape(384, 384), nn).astype(BF).reshape(NG, 48, 384)
    a_z3[...] = dot(swap, a_z2[...].reshape(384, 192), nn).astype(BF).reshape(NY, 48, 192)
    along_g, along_y = links.reserve(NG), links.reserve(NY)
    for k in range(1, NY):
        links.send(along_g + k, a_y3.at[g_to[k]], a_y4.at[g], group(g_to[k]), t)
        links.send(along_y + k, a_z3.at[y_to[k]], a_z4.at[y], dp_of(y_to[k]), t)
    a_y4[g] = a_y3[g]
    a_z4[y] = a_z3[y]

    row, col = iota((NT * 80, 1), 0), iota((NT * 80, 288), 1)
    slot = rem(row, 80)
    of_gate = jnp.logical_and(slot < 36, col == (div(row, 80)) * 36 + slot).astype(BF)
    of_up = jnp.logical_and(jnp.logical_and(slot >= 40, slot < 76), col == (div(row, 80)) * 36 + slot - 40).astype(BF)
    scale = gain[...].astype(F32)
    rows = dot(of_gate, (w_gate[...].astype(F32) * scale).astype(BF), nn)
    rows = (rows + dot(of_up, (w_up[...].astype(F32) * scale).astype(BF), nn)).astype(BF)
    row, col = iota((896, 1), 0), iota((896, 1024), 1)
    rank = div(row, 14)
    at = rem(rank, 2) * 512 + (div(rank, 2)) * 16 + rem(row, 14)
    spread = (col == at).astype(BF)
    squares_at = jnp.logical_and(rem(iota((NT * 80, 1), 0), 80) == 36, rem(iota((1, 1024), 1), 16) >= 14)
    w_gu[...] = jnp.where(squares_at, 1.0, dot(rows, spread, nn)).astype(BF)

    for k in range(1, NY):
        links.arrived(along_g + k, a_y4.at[g_from[k]], group(g_from[k]), t)
        links.arrived(along_y + k, a_z4.at[y_from[k]], dp_of(y_from[k]), t)

    for i in (6, 0, 1):
        loads[i].wait()
    row = iota((REQ * KEYS, 1), 0)
    place, request = rem(row, KEYS), div(row, KEYS)
    named = jnp.full((REQ * KEYS, 1), -1, jnp.int32)
    for r in range(REQ):
        for k in range(MAXP):
            named = jnp.where(jnp.logical_and(request == r, div(place, 2) == k), table[r, k], named)
    token = rem(place, 2)
    from_own = (jnp.where(jnp.logical_and(named >= 0, named < POOL), 2 * named + token, -1) == iota((REQ * KEYS, 144), 1)).astype(BF)
    migrated = jnp.maximum(named - POOL, 0)
    rank = div(migrated, 3)
    inner = (migrated - CAP * rank) * 2 + token
    rank_y, rank_g = div(rank, NG), rem(rank, NG)
    in_inbox = named >= POOL
    at = jnp.where(in_inbox, rank_g * 48 + rank_y * 6 + inner, -1)
    from_y = (at == iota((REQ * KEYS, 384), 1)).astype(BF)
    at = jnp.where(in_inbox, rank_y * 48 + rank_g * 6 + inner, -1)
    from_z = (at == iota((REQ * KEYS, 384), 1)).astype(BF)
    at = jnp.where(jnp.logical_and(place >= 26, place < 28), 2 * request + place - 26, -1)
    from_fresh = (at == iota((REQ * KEYS, 2 * REQ), 1)).astype(BF)
    low = dot(from_own, own[:, :384], nn) + dot(from_fresh, fresh[:, :384], nn)
    high = dot(from_own, own[:, 384:], nn) + dot(from_fresh, fresh[:, 384:], nn)
    low = low + dot(from_y, a_y4[...].reshape(384, 384), nn)
    high = high + dot(from_z, a_z4[...].reshape(384, 192), nn)
    keys[:, :, :384] = low.astype(BF).reshape(REQ, KEYS, 384)
    keys[:, :, 384:] = high.astype(BF).reshape(REQ, KEYS, 192)
    for k in range(1, NT):
        links.arrived(to_heads + k, q_all.at[t_from[k]], dp, t_from[k])

    scores = [dot(q_all[:, r].reshape(NT * 16, LAT), keys[r], nt) for r in range(REQ)]
    scores = jnp.concatenate(scores, axis=0) * SCALE
    row, col = iota((REQ * 128, 1), 0), iota((REQ * 128, KEYS), 1)
    length = jnp.full((REQ * 128, 1), lengths[0], jnp.int32)
    for r in range(1, REQ):
        length = jnp.where(row >= r * 128, lengths[r], length)
    cached = jnp.logical_and(col < 26, (div(col, 2)) * PAGE + 2 * t + rem(col, 2) < length)
    newer = jnp.logical_and(jnp.logical_and(col >= 26, col <= 26 + rem(div(row, 8), 2)), t == 0)
    live = jnp.logical_or(cached, newer)
    scores = jnp.where(live, scores, DEAD)
    top = jnp.max(scores, axis=1, keepdims=True)
    weights = jnp.where(live, jnp.exp(scores - top), 0.0)
    total = jnp.sum(weights, axis=1, keepdims=True)
    some = total > 0.0
    total = jnp.where(some, total, 1.0)
    weights = (weights / total).astype(BF)
    lse = jnp.where(some, top + jnp.log(total), DEAD)
    high = lse.astype(BF).astype(F32)
    middle = (lse - high).astype(BF).astype(F32)
    low = lse - high - middle
    lane = iota((REQ * 128, 128), 1)
    parts = jnp.where(lane == 0, high, jnp.where(lane == 1, middle, jnp.where(lane == 2, low, 0.0))).astype(BF)
    for r in range(REQ):
        latent = dot(weights[r * 128 : (r + 1) * 128], keys[r][:, :KVL], nn)
        o_out[:, r, :, :KVL] = latent.astype(BF).reshape(NT, 16, KVL)
        o_out[:, r, :, KVL:] = parts[r * 128 : (r + 1) * 128].reshape(NT, 16, 128)
    slot = links.reserve(NT)
    for k in range(1, NT):
        links.send(slot + k, o_out.at[t_to[k]], o_in.at[t], dp, t_to[k])
    o_in[t] = o_out[t]
    for k in range(1, NT):
        links.arrived(slot + k, o_in.at[t_from[k]], dp, t_from[k])
    lse = [jnp.sum(o_in[s, :, :, KVL:].astype(F32), axis=2, keepdims=True) for s in range(NT)]
    top = functools.reduce(jnp.maximum, lse)
    shares = [jnp.exp(v - top) for v in lse]
    total = functools.reduce(jnp.add, shares)
    latent = jnp.zeros((REQ, 16, KVL), F32)
    for s in range(NT):
        latent = latent + o_in[s, :, :, :KVL].astype(F32) * (shares[s] / total)
    latent = latent.astype(BF).reshape(REQ * 16, KVL)

    for i in (7,):
        loads[i].wait()
    of_token = (div(iota((16, 80), 1), 8) == iota((16, 80), 0)).astype(BF)
    head = rem(iota((80, HD), 0), 8)
    for h in range(8):
        values = jnp.where(head == h, dot(latent, w_uv[h], ((1,), (0,))), 0.0).astype(BF)
        values = dot(of_token, values, ((1,), (0,))).astype(BF)
        ho[h // 4, :, (h % 4) * HD : (h % 4 + 1) * HD] = values

    slot = links.reserve(NG)
    for k in range(1, NG):
        links.send(slot + k, ho.at[lax.rem(g_to[k], 2)], b_in.at[g], group(g_to[k]), t)
    b_in[g] = ho[core]
    for k in range(1, NG):
        links.arrived(slot + k, b_in.at[g_from[k]], group(g_from[k]), t)
    partner = dp + 1 - 2 * core

    def at_y(step):
        return lax.rem(y + NY + step, NY)

    def gather(buf, flip):
        near, far, over = links.reserve(4), links.reserve(3), links.reserve(8)
        held_y = []

        def pass_on(index):
            links.send(over + len(held_y), buf.at[core, index], buf.at[core, index], partner, t)
            held_y.append(index)

        def forward(slot, index, step):
            links.send(slot, buf.at[core, index], buf.at[core, index], dp_of(at_y(step)), t)

        def arrived(slot, index):
            links.arrived(slot, buf.at[core, index], partner, t)

        for i, step in enumerate((2, -2, 1, -1)):
            forward(near + i, y, step)
        pass_on(y)
        yield
        arrived(near, at_y(-2))
        forward(far, at_y(-2), 1)
        if flip:
            forward(far + 2, at_y(-2), 2)
        arrived(near + 1, at_y(2))
        forward(far + 1, at_y(2), -1)
        if not flip:
            forward(far + 2, at_y(2), -2)
        pass_on(at_y(-2))
        pass_on(at_y(2))
        for i, step in ((2, -1), (3, 1)):
            arrived(near + i, at_y(step))
            pass_on(at_y(step))
        yield
        for i, step in ((0, -3), (1, 3), (2, 4)):
            arrived(far + i, at_y(step))
            pass_on(at_y(step))
        for order, index in enumerate(held_y):
            links.arrived(over + order, buf.at[1 - core, index], partner, t)

    def scatter(acc, r_out, r_in, flip):
        slot = links.reserve(7)

        def send(i, value, step):
            r_out[i] = value.astype(BF)
            links.send(slot + i, r_out.at[i], r_in.at[i], dp_of(at_y(step)), t)

        def received(i):
            links.arrived(slot + i, r_in.at[i], partner, t)
            return r_in[i].astype(F32)

        send(2, acc[at_y(4)], 2 if flip else -2)
        send(0, acc[at_y(-3)], -1)
        send(1, acc[at_y(3)], 1)
        send(3, acc[at_y(-1)], -1)
        send(4, acc[at_y(1)], 1)
        yield
        below, above = acc[at_y(-2)] + received(0), acc[at_y(2)] + received(1)
        if flip:
            above = above + received(2)
        else:
            below = below + received(2)
        send(5, below, -2)
        send(6, above, 2)
        yield
        value = acc[y]
        for i in range(3, 7):
            value = value + received(i)
        return value

    def chain(h):
        rows = ROWS[h]
        lanes = NY * rows
        (
            res_h, heads, pj, c_in, stream, gu, e_in, h_all, part, f_out, f_in, acc, r_out, r_in
        ) = halves[h * PER_HALF : (h + 1) * PER_HALF]
        yield from gather(heads, h)

        projected = dot(w_o[:, :KVL], heads[0].reshape(lanes, KVL), nt)
        projected = projected + dot(w_o[:, KVL:], heads[1].reshape(lanes, KVL), nt)
        pj[...] = projected.astype(BF).reshape(NT, 16, lanes)
        slot = links.reserve(NT)
        for k in range(1, NT):
            links.send(slot + k, pj.at[t_to[k]], c_in.at[t], dp, t_to[k])
        c_in[t] = pj[t]
        yield
        for k in range(1, NT):
            links.arrived(slot + k, c_in.at[t_from[k]], dp, t_from[k])
        summed = res_h[...]
        for s in range(NT):
            summed = summed + c_in[s].astype(F32)
        summed = summed.astype(BF).astype(F32)
        squares = jnp.sum(summed * summed, axis=0, keepdims=True)
        high = squares.astype(BF).astype(F32)
        row = iota((16, lanes), 0)
        piece = jnp.where(row == 14, high, jnp.where(row == 15, squares - high, summed)).astype(BF)
        stream[core, y, z] = piece

        slot = links.reserve(4)
        for k in range(1, 4):
            block = stream.at[core, y, z]
            links.send(slot + k, block, block, group(z_to[k] * 2 + core), t)
        yield
        for k in range(1, 4):
            links.arrived(slot + k, stream.at[core, y, z_from[k]], group(z_from[k] * 2 + core), t)
        yield from gather(stream, h)

        slot = links.reserve(NT)
        columns = stream[...].reshape(1024, lanes)
        for k in range(1, NT + 1):
            to = lax.rem(t + k, NT)
            first = pl.multiple_of(to * 80, 80)
            gu[to] = dot(w_gu[pl.ds(first, 80), :], columns, nn).astype(BF)
            if k < NT:
                links.send(slot + k, gu.at[to], e_in.at[t], dp, to)
            else:
                e_in[t] = gu[t]
        yield
        for k in range(1, NT):
            links.arrived(slot + k, e_in.at[t_from[k]], dp, t_from[k])
        total = jnp.zeros((80, lanes), F32)
        for s in range(NT):
            total = total + e_in[s].astype(F32)
        scale = lax.rsqrt(total[36:37] / D + EPS)
        gate, up = total[:40] * scale, total[40:] * scale
        hidden = gate / (1.0 + jnp.exp(-gate)) * up
        hidden = jnp.where(iota((40, lanes), 0) < 36, hidden, 0.0)
        hidden = jnp.concatenate([hidden, jnp.zeros((8, lanes), F32)], axis=0).astype(BF)
        h_all[t] = hidden
        slot = links.reserve(NT)
        for k in range(1, NT):
            links.send(slot + k, h_all.at[t], h_all.at[t], dp, t_to[k])
        yield
        for k in range(1, NT):
            links.arrived(slot + k, h_all.at[t_from[k]], dp, t_from[k])

        for block in range(lanes // 128):
            span = slice(block * 128, (block + 1) * 128)
            value = dot(h_all[:, :, span].reshape(384, 128), w_d[...], tn)
            part[span] = value + dot(stream[core, y, z, :, span], place, tn)

        f_out[...] = part[:, other].astype(BF)
        slot = links.reserve(1)
        links.send(slot, f_out, f_in, partner, t)
        yield
        links.arrived(slot, f_in, partner, t)
        acc[...] = (part[:, mine] + f_in[...].astype(F32)).reshape(NY, rows, KVL)
        value = yield from scatter(acc, r_out, r_in, h)
        last[h * ROWS[0] : h * ROWS[0] + rows] = value.astype(BF)

    place = jnp.logical_and(iota((16, 896), 1) == dp * 14 + iota((16, 896), 0), iota((16, 896), 0) < 14).astype(BF)
    mine = pl.ds(pl.multiple_of(core * 384, 128), KVL)
    other = pl.ds(pl.multiple_of((1 - core) * 384, 128), KVL)
    gathered = b_in[...].reshape(128, KVL)
    for h, rows in enumerate(ROWS):
        row, col = iota((rows, 1), 0) + h * ROWS[0], iota((rows, 128), 1)
        pack = (col == div(row, 10) * 16 + rem(row, 10)).astype(BF)
        halves[h * PER_HALF + 1][core, y] = dot(pack, gathered, nn).astype(BF)
    running = [chain(h) for h in range(len(ROWS))]
    while running:
        running = [steps for steps in running if next(steps, DONE) is not DONE]

    row, col = iota((128, 1), 0), iota((128, 80), 1)
    spread = jnp.logical_and(rem(row, 16) < 10, col == (div(row, 16)) * 10 + rem(row, 16)).astype(BF)
    g_out[...] = dot(spread, last[...], nn).astype(BF).reshape(NG, 16, KVL)
    slot = links.reserve(NG)
    for k in range(1, NG):
        links.send(slot + k, g_out.at[g_to[k]], g_in.at[g], group(g_to[k]), t)
    g_in[g] = g_out[g]
    for k in range(1, NG):
        links.arrived(slot + k, g_in.at[g_from[k]], group(g_from[k]), t)
    first = jnp.zeros((16, KVL), F32)
    second = jnp.zeros((16, KVL), F32)
    for s in range(4):
        first = first + g_in[2 * s].astype(F32)
        second = second + g_in[2 * s + 1].astype(F32)
    out[:, :KVL] = first.astype(BF)[:10]
    out[:, KVL:] = second.astype(BF)[:10, 128:]
    links.finish()


SLOTS = 8 * 8 + 2 * (2 * 15 + 3 * 8 + 4 + 1 + 7)


def layer(*operands):
    scratch = [
        ((144, LAT), BF),
        ((NY, 48, 384), BF),
        ((NY, 48, 384), BF),
        ((NG, 48, 384), BF),
        ((NG, 48, 384), BF),
        ((NG, 48, 192), BF),
        ((NG, 48, 192), BF),
        ((NY, 48, 192), BF),
        ((NY, 48, 192), BF),
        ((NT * 80, 1024), BF),
        ((128, 1024), BF),
        ((384, 896), BF),
        ((NT, REQ, 16, LAT), BF),
        ((REQ, KEYS, LAT), BF),
        ((NT, REQ, 16, 640), BF),
        ((NT, REQ, 16, 640), BF),
        ((2, 16, KVL), BF),
        ((NG, 16, KVL), BF),
        ((80, KVL), BF),
        ((NG, 16, KVL), BF),
        ((NG, 16, KVL), BF),
    ]
    for rows in ROWS:
        lanes = NY * rows
        scratch += [
            ((16, lanes), F32),
            ((2, NY, rows, KVL), BF),
            ((NT, 16, lanes), BF),
            ((NT, 16, lanes), BF),
            ((2, NY, 4, 16, lanes), BF),
            ((NT, 80, lanes), BF),
            ((NT, 80, lanes), BF),
            ((NT, 48, lanes), BF),
            ((lanes, 896), F32),
            ((lanes, KVL), BF),
            ((lanes, KVL), BF),
            ((NY, rows, KVL), F32),
            ((7, rows, KVL), BF),
            ((7, rows, KVL), BF),
        ]
    vmem = pl.BlockSpec(memory_space=pltpu.VMEM)
    held = [
        (pltpu.SMEM if i < 2 else pltpu.VMEM)(operand.shape, operand.dtype) for i, operand in enumerate(operands)
    ]
    return pl.pallas_call(
        kernel,
        out_shape=jax.ShapeDtypeStruct((10, 896), BF),
        in_specs=[pl.BlockSpec(memory_space=pl.ANY)] * 14,
        out_specs=vmem,
        scratch_shapes=held
        + [pltpu.VMEM(shape, kind) for shape, kind in scratch]
        + [pltpu.SemaphoreType.DMA((SLOTS,)), pltpu.SemaphoreType.DMA((SLOTS,)), pltpu.SemaphoreType.DMA((14,))],
        compiler_params=pltpu.CompilerParams(
            collective_id=0, has_side_effects=True, vmem_limit_bytes=60 * 1024 * 1024
        ),
        cost_estimate=pl.CostEstimate(flops=3 * 10**9, bytes_accessed=10**7, transcendentals=10**6),
        name="layer",
    )(*operands)


def local(
    pool,
    page_table,
    lengths,
    mig_page,
    mig_dest,
    queries,
    new_latent,
    w_uv,
    w_out,
    residual,
    norm_gain,
    w_gate,
    w_up,
    w_down,
):
    return layer(
        page_table,
        lengths,
        mig_page,
        mig_dest,
        queries.reshape(REQ, 16, LAT),
        pool.reshape(POOL * PAGE, LAT),
        new_latent,
        w_uv,
        w_out.transpose(2, 1, 0).reshape(112, 1024),
        residual.reshape(TOK, 14).T,
        norm_gain.reshape(1, 896),
        w_gate.T,
        w_up.T,
        w_down,
    )


def solution(mesh):
    in_specs = (
        P("dp", None, None),
        P("dp", None),
        P("dp"),
        P("dp", None),
        P("dp", None),
        P("dp", "tp", None),
        P("dp", None),
        P("tp", None, None),
        P("tp", None, "dp"),
        P(None, "tp", "dp"),
        P("tp"),
        P("tp", "dp"),
        P("tp", "dp"),
        P("dp", "tp"),
    )
    out_specs = P("dp", "tp")
    return jax.shard_map(local, mesh=mesh, in_specs=in_specs, out_specs=out_specs, check_vma=False)
```

```python
import functools

import jax
import jax.numpy as jnp
from jax import lax
from jax.experimental import pallas as pl
from jax.experimental.pallas import tpu as pltpu
from jax.sharding import PartitionSpec as P

D = 7168
HD = 128
KVL = 512
LAT = 576
PAGE = 16
MAXP = 13
REQ = 5
POOL = 65
CAP = 3
NY = 8
NG = 8
NT = 8
KEYS = 32
TOK = 640
EPS = 1e-06
SCALE = 192 ** (-0.5)
BF = jnp.bfloat16
F32 = jnp.float32
MESH = pl.DeviceIdType.MESH
DEAD = -1e30
PARTS = (2, 3)
FIRST = tuple(sum(PARTS[:h]) for h in range(len(PARTS)))
PER_PART = 18
HALF_ROWS = tuple(-(-8 * requests // 16) * 16 for requests in PARTS)
DONE = object()


def dot(a, b, dims):
    return lax.dot_general(a, b, (dims, ((), ())), preferred_element_type=F32)


def div(value, by):
    return lax.shift_right_logical(value * (-(-(1 << 20) // by)), 20)


def rem(value, by):
    return value - by * div(value, by)


def iota(shape, axis):
    return lax.broadcasted_iota(jnp.int32, shape, axis)


class Links:
    def __init__(self, send_sems, recv_sems):
        self.send_sems, self.recv_sems, self.used, self.sent = send_sems, recv_sems, 0, []

    def reserve(self, count):
        first = self.used
        self.used += count
        return first

    def copy(self, slot, src, dst, dp, tp):
        return pltpu.make_async_remote_copy(
            src_ref=src,
            dst_ref=dst,
            send_sem=self.send_sems.at[slot],
            recv_sem=self.recv_sems.at[slot],
            device_id={"dp": dp, "tp": tp},
            device_id_type=MESH,
        )

    def send(self, slot, src, dst, dp, tp):
        copy = self.copy(slot, src, dst, dp, tp)
        copy.start()
        self.sent.append(copy)

    def arrived(self, slot, dst, dp, tp):
        self.copy(slot, dst, dst, dp, tp).wait_recv()

    def finish(self):
        for copy in self.sent:
            copy.wait_send()


def kernel(
    *refs
):
    operands, (out, *held), rest = refs[:14], refs[14:29], refs[29:]
    (
        table, lengths, mig_page, mig_dest, q, pool, fresh, w_uv, w_out, res, gain, w_gate, w_up, w_down
    ) = held
    (
    own, a_y1, a_y2, a_y3, a_y4, a_z1, a_z2, a_z3, a_z4, w_gu, w_o, w_d,
    q_all, keys, last, g_out, g_in, *buffers, send_sems, recv_sems, load_sems,
    ) = rest
    loads = [pltpu.make_async_copy(*pair, load_sems.at[i]) for i, pair in enumerate(zip(operands, held))]
    for i in (5, 2, 3, 4, 8, 9, 13, 10, 11, 12, 6, 0, 1, 7):
        loads[i].start()

    dp, t = lax.axis_index("dp"), lax.axis_index("tp")
    y, g = dp // NG, lax.rem(dp, NG)
    z, core = g // 2, lax.rem(g, 2)
    links = Links(send_sems, recv_sems)
    t_to = [lax.rem(t + k, NT) for k in range(NT)]
    t_from = [lax.rem(t + NT - k, NT) for k in range(NT)]
    g_to = [lax.rem(g + k, NG) for k in range(NG)]
    g_from = [lax.rem(g + NG - k, NG) for k in range(NG)]
    y_to = [lax.rem(y + k, NY) for k in range(NY)]
    y_from = [lax.rem(y + NY - k, NY) for k in range(NY)]
    z_to = [lax.rem(z + k, 4) for k in range(4)]
    z_from = [lax.rem(z + 4 - k, 4) for k in range(4)]
    nn, nt, tn = ((1,), (0,)), ((1,), (1,)), ((0,), (0,))

    def dp_of(yy):
        return yy * NG + g

    def group(gg):
        return y * NG + gg

    barrier = pltpu.get_barrier_semaphore()
    for k in range(1, NT):
        pl.semaphore_signal(barrier, inc=1, device_id={"dp": dp, "tp": t_to[k]}, device_id_type=MESH)
    for k in range(1, NG):
        pl.semaphore_signal(barrier, inc=1, device_id={"dp": group(g_to[k]), "tp": t}, device_id_type=MESH)
    for k in range(1, NY):
        pl.semaphore_signal(barrier, inc=1, device_id={"dp": dp_of(y_to[k]), "tp": t}, device_id_type=MESH)

    for i in (5, 2, 3, 4):
        loads[i].wait()
    row = iota((144, 1), 0)
    column = (div(row, 2)) * PAGE + 2 * t + rem(row, 2)
    own[...] = dot((column == iota((144, POOL * PAGE), 1)).astype(BF), pool[...], nn).astype(BF)
    row = iota((384, 1), 0)
    inner = rem(row, 6)
    entry = rem(iota((1, CAP * 28), 1), CAP)

    def outgoing(rank):
        match = jnp.logical_and(mig_dest[...] == rank, entry == div(inner, 2))
        source = jnp.sum(jnp.where(match, (mig_page[...] + 1).astype(F32), 0.0), axis=1, keepdims=True)
        source = source.astype(jnp.int32) * 2 - 2 + rem(inner, 2)
        return (source == iota((384, 144), 1)).astype(BF)

    first, second = div(row, 48), div(rem(row, 48), 6)
    a_y1[...] = dot(outgoing(first * NG + second), own[:, :384], nn).astype(BF).reshape(NY, 48, 384)
    a_z1[...] = dot(outgoing(second * NG + first), own[:, 384:], nn).astype(BF).reshape(NG, 48, 192)
    q_all[t] = q[...]

    pl.semaphore_wait(barrier, 21)
    along_y, along_g = links.reserve(NY), links.reserve(NG)
    for k in range(1, NY):
        links.send(along_y + k, a_y1.at[y_to[k]], a_y2.at[y], dp_of(y_to[k]), t)
        links.send(along_g + k, a_z1.at[g_to[k]], a_z2.at[g], group(g_to[k]), t)
    to_heads = links.reserve(NT)
    for k in range(1, NT):
        links.send(to_heads + k, q_all.at[t], q_all.at[t], dp, t_to[k])
    a_y2[y] = a_y1[y]
    a_z2[g] = a_z1[g]

    for i in (8, 9, 13, 10, 11, 12):
        loads[i].wait()
    row, col = iota((128, 1), 0), iota((128, 112), 1)
    spread = jnp.logical_and(rem(row, 16) < 14, col == rem(row, 16) * 8 + div(row, 16)).astype(BF)
    w_o[...] = dot(spread, w_out[...], nn).astype(BF)
    row, col = iota((384, 1), 0), iota((384, 288), 1)
    spread = jnp.logical_and(rem(row, 48) < 36, col == (div(row, 48)) * 36 + rem(row, 48)).astype(BF)
    w_d[...] = dot(spread, w_down[...], nn).astype(BF)
    for h, requests in enumerate(PARTS):
        tokens = 2 * requests
        row, col = iota((TOK, 1), 0), iota((1, 64 * tokens), 1)
        at = div(col, tokens) * 10 + rem(col, tokens) + 2 * FIRST[h]
        values = dot(res[...], (row == at).astype(BF), nn)
        buffers[h * PER_PART][...] = jnp.concatenate([values, jnp.zeros((2, 64 * tokens), F32)], axis=0)

    for k in range(1, NY):
        links.arrived(along_y + k, a_y2.at[y_from[k]], dp_of(y_from[k]), t)
        links.arrived(along_g + k, a_z2.at[g_from[k]], group(g_from[k]), t)
    row, col = iota((384, 1), 0), iota((384, 384), 1)
    swap = (col == (div(rem(row, 48), 6)) * 48 + (div(row, 48)) * 6 + rem(row, 6)).astype(BF)
    a_y3[...] = dot(swap, a_y2[...].reshape(384, 384), nn).astype(BF).reshape(NG, 48, 384)
    a_z3[...] = dot(swap, a_z2[...].reshape(384, 192), nn).astype(BF).reshape(NY, 48, 192)
    along_g, along_y = links.reserve(NG), links.reserve(NY)
    for k in range(1, NY):
        links.send(along_g + k, a_y3.at[g_to[k]], a_y4.at[g], group(g_to[k]), t)
        links.send(along_y + k, a_z3.at[y_to[k]], a_z4.at[y], dp_of(y_to[k]), t)
    a_y4[g] = a_y3[g]
    a_z4[y] = a_z3[y]

    row, col = iota((NT * 80, 1), 0), iota((NT * 80, 288), 1)
    slot = rem(row, 80)
    of_gate = jnp.logical_and(slot < 36, col == (div(row, 80)) * 36 + slot).astype(BF)
    of_up = jnp.logical_and(jnp.logical_and(slot >= 40, slot < 76), col == (div(row, 80)) * 36 + slot - 40).astype(BF)
    scale = gain[...].astype(F32).reshape(1, 896)
    rows = dot(of_gate, (w_gate[...].astype(F32) * scale).astype(BF), nn)
    rows = (rows + dot(of_up, (w_up[...].astype(F32) * scale).astype(BF), nn)).astype(BF)
    row, col = iota((896, 1), 0), iota((896, 1024), 1)
    rank = div(row, 14)
    at = rem(rank, 2) * 512 + (div(rank, 2)) * 16 + rem(row, 14)
    spread = (col == at).astype(BF)
    squares_at = jnp.logical_and(rem(iota((NT * 80, 1), 0), 80) == 36, rem(iota((1, 1024), 1), 16) >= 14)
    w_gu[...] = jnp.where(squares_at, 1.0, dot(rows, spread, nn)).astype(BF)

    for k in range(1, NY):
        links.arrived(along_g + k, a_y4.at[g_from[k]], group(g_from[k]), t)
        links.arrived(along_y + k, a_z4.at[y_from[k]], dp_of(y_from[k]), t)

    for i in (6, 0, 1):
        loads[i].wait()
    row = iota((REQ * KEYS, 1), 0)
    place, request = rem(row, KEYS), div(row, KEYS)
    named = jnp.full((REQ * KEYS, 1), -1, jnp.int32)
    for r in range(REQ):
        for k in range(MAXP):
            named = jnp.where(jnp.logical_and(request == r, div(place, 2) == k), table[r, k], named)
    token = rem(place, 2)
    from_own = (jnp.where(jnp.logical_and(named >= 0, named < POOL), 2 * named + token, -1) == iota((REQ * KEYS, 144), 1)).astype(BF)
    migrated = jnp.maximum(named - POOL, 0)
    rank = div(migrated, 3)
    inner = (migrated - CAP * rank) * 2 + token
    rank_y, rank_g = div(rank, NG), rem(rank, NG)
    in_inbox = named >= POOL
    at = jnp.where(in_inbox, rank_g * 48 + rank_y * 6 + inner, -1)
    from_y = (at == iota((REQ * KEYS, 384), 1)).astype(BF)
    at = jnp.where(in_inbox, rank_y * 48 + rank_g * 6 + inner, -1)
    from_z = (at == iota((REQ * KEYS, 384), 1)).astype(BF)
    at = jnp.where(jnp.logical_and(place >= 26, place < 28), 2 * request + place - 26, -1)
    from_fresh = (at == iota((REQ * KEYS, 2 * REQ), 1)).astype(BF)
    low = dot(from_own, own[:, :384], nn) + dot(from_fresh, fresh[:, :384], nn)
    high = dot(from_own, own[:, 384:], nn) + dot(from_fresh, fresh[:, 384:], nn)
    low = low + dot(from_y, a_y4[...].reshape(384, 384), nn)
    high = high + dot(from_z, a_z4[...].reshape(384, 192), nn)
    keys[:, :, :384] = low.astype(BF).reshape(REQ, KEYS, 384)
    keys[:, :, 384:] = high.astype(BF).reshape(REQ, KEYS, 192)
    for k in range(1, NT):
        links.arrived(to_heads + k, q_all.at[t_from[k]], dp, t_from[k])

    scores = [dot(q_all[:, r].reshape(NT * 16, LAT), keys[r], nt) for r in range(REQ)]
    scores = jnp.concatenate(scores, axis=0) * SCALE
    row, col = iota((REQ * 128, 1), 0), iota((REQ * 128, KEYS), 1)
    length = jnp.full((REQ * 128, 1), lengths[0], jnp.int32)
    for r in range(1, REQ):
        length = jnp.where(row >= r * 128, lengths[r], length)
    cached = jnp.logical_and(col < 26, (div(col, 2)) * PAGE + 2 * t + rem(col, 2) < length)
    newer = jnp.logical_and(jnp.logical_and(col >= 26, col <= 26 + rem(div(row, 8), 2)), t == 0)
    live = jnp.logical_or(cached, newer)
    scores = jnp.where(live, scores, DEAD)
    top = jnp.max(scores, axis=1, keepdims=True)
    weights = jnp.where(live, jnp.exp(scores - top), 0.0)
    total = jnp.sum(weights, axis=1, keepdims=True)
    some = total > 0.0
    total = jnp.where(some, total, 1.0)
    weights = (weights / total).astype(BF)
    lse = jnp.where(some, top + jnp.log(total), DEAD)
    high = lse.astype(BF).astype(F32)
    middle = (lse - high).astype(BF).astype(F32)
    low = lse - high - middle
    lane = iota((REQ * 128, 128), 1)
    parts = jnp.where(lane == 0, high, jnp.where(lane == 1, middle, jnp.where(lane == 2, low, 0.0))).astype(BF)
    loads[7].wait()
    partner = dp + 1 - 2 * core

    def at_y(step):
        return lax.rem(y + NY + step, NY)

    def gather(buf, flip):
        near, far, over = links.reserve(4), links.reserve(3), links.reserve(8)
        held_y = []

        def pass_on(index):
            links.send(over + len(held_y), buf.at[core, index], buf.at[core, index], partner, t)
            held_y.append(index)

        def forward(slot, index, step):
            links.send(slot, buf.at[core, index], buf.at[core, index], dp_of(at_y(step)), t)

        def arrived(slot, index):
            links.arrived(slot, buf.at[core, index], partner, t)

        for i, step in enumerate((2, -2, 1, -1)):
            forward(near + i, y, step)
        pass_on(y)
        yield
        arrived(near, at_y(-2))
        forward(far, at_y(-2), 1)
        if flip:
            forward(far + 2, at_y(-2), 2)
        arrived(near + 1, at_y(2))
        forward(far + 1, at_y(2), -1)
        if not flip:
            forward(far + 2, at_y(2), -2)
        pass_on(at_y(-2))
        pass_on(at_y(2))
        for i, step in ((2, -1), (3, 1)):
            arrived(near + i, at_y(step))
            pass_on(at_y(step))
        yield
        for i, step in ((0, -3), (1, 3), (2, 4)):
            arrived(far + i, at_y(step))
            pass_on(at_y(step))
        for order, index in enumerate(held_y):
            links.arrived(over + order, buf.at[1 - core, index], partner, t)

    def scatter(acc, r_out, r_in, flip):
        slot = links.reserve(7)

        def send(i, value, step):
            r_out[i] = value.astype(BF)
            links.send(slot + i, r_out.at[i], r_in.at[i], dp_of(at_y(step)), t)

        def received(i):
            links.arrived(slot + i, r_in.at[i], partner, t)
            return r_in[i].astype(F32)

        send(2, acc[at_y(4)], 2 if flip else -2)
        send(0, acc[at_y(-3)], -1)
        send(1, acc[at_y(3)], 1)
        send(3, acc[at_y(-1)], -1)
        send(4, acc[at_y(1)], 1)
        yield
        below, above = acc[at_y(-2)] + received(0), acc[at_y(2)] + received(1)
        if flip:
            above = above + received(2)
        else:
            below = below + received(2)
        send(5, below, -2)
        send(6, above, 2)
        yield
        value = acc[y]
        for i in range(3, 7):
            value = value + received(i)
        return value

    def chain(h):
        requests = PARTS[h]
        tokens = 2 * requests
        rows, lanes = NG * tokens, 64 * tokens
        padded = HALF_ROWS[h]
        (
            res_h, o_out, o_in, ho, b_in, heads, pj, c_in, stream, gu, e_in, h_all, part, f_out, f_in, acc, r_out, r_in
        ) = buffers[h * PER_PART : (h + 1) * PER_PART]
        for i in range(requests):
            r = FIRST[h] + i
            latent = dot(weights[r * 128 : (r + 1) * 128], keys[r][:, :KVL], nn)
            o_out[:, i, :, :KVL] = latent.astype(BF).reshape(NT, 16, KVL)
            o_out[:, i, :, KVL:] = parts[r * 128 : (r + 1) * 128].reshape(NT, 16, 128)
        slot = links.reserve(NT)
        for k in range(1, NT):
            links.send(slot + k, o_out.at[t_to[k]], o_in.at[t], dp, t_to[k])
        o_in[t] = o_out[t]
        yield
        for k in range(1, NT):
            links.arrived(slot + k, o_in.at[t_from[k]], dp, t_from[k])
        lse = [jnp.sum(o_in[s, :, :, KVL:].astype(F32), axis=2, keepdims=True) for s in range(NT)]
        top = functools.reduce(jnp.maximum, lse)
        shares = [jnp.exp(v - top) for v in lse]
        total = functools.reduce(jnp.add, shares)
        latent = jnp.zeros((requests, 16, KVL), F32)
        for s in range(NT):
            latent = latent + o_in[s, :, :, :KVL].astype(F32) * (shares[s] / total)
        latent = latent.astype(BF).reshape(requests * 16, KVL)

        head = rem(iota((requests * 16, 1), 0), 8)
        values = jnp.zeros((requests * 16, HD), F32)
        for i in range(8):
            values = jnp.where(head == i, dot(latent, w_uv[i], nn), values)
        row, col = iota((2 * padded, 1), 0), iota((2 * padded, requests * 16), 1)
        inner = rem(row, padded)
        at = div(inner, 4) * 8 + div(row, padded) * 4 + rem(inner, 4)
        split = jnp.logical_and(inner < 4 * tokens, col == at).astype(BF)
        ho[...] = dot(split, values.astype(BF), nn).astype(BF).reshape(2, padded, HD)

        slot = links.reserve(NG)
        for k in range(1, NG):
            links.send(slot + k, ho.at[lax.rem(g_to[k], 2)], b_in.at[g], group(g_to[k]), t)
        b_in[g] = ho[core]
        yield
        for k in range(1, NG):
            links.arrived(slot + k, b_in.at[g_from[k]], group(g_from[k]), t)
        row, col = iota((rows, 1), 0), iota((rows, NG * padded), 1)
        at = div(row, tokens) * padded + rem(row, tokens) * 4
        gathered = b_in[...].reshape(NG * padded, HD)
        for i in range(4):
            heads[core, y, :, i * HD : (i + 1) * HD] = dot((col == at + i).astype(BF), gathered, nn).astype(BF)
        yield from gather(heads, h)

        projected = dot(w_o[:, :KVL], heads[0].reshape(lanes, KVL), nt)
        projected = projected + dot(w_o[:, KVL:], heads[1].reshape(lanes, KVL), nt)
        pj[...] = projected.astype(BF).reshape(NT, 16, lanes)
        slot = links.reserve(NT)
        for k in range(1, NT):
            links.send(slot + k, pj.at[t_to[k]], c_in.at[t], dp, t_to[k])
        c_in[t] = pj[t]
        yield
        for k in range(1, NT):
            links.arrived(slot + k, c_in.at[t_from[k]], dp, t_from[k])
        summed = res_h[...]
        for s in range(NT):
            summed = summed + c_in[s].astype(F32)
        summed = summed.astype(BF).astype(F32)
        squares = jnp.sum(summed * summed, axis=0, keepdims=True)
        high = squares.astype(BF).astype(F32)
        row = iota((16, lanes), 0)
        piece = jnp.where(row == 14, high, jnp.where(row == 15, squares - high, summed)).astype(BF)
        stream[core, y, z] = piece

        slot = links.reserve(4)
        for k in range(1, 4):
            block = stream.at[core, y, z]
            links.send(slot + k, block, block, group(z_to[k] * 2 + core), t)
        yield
        for k in range(1, 4):
            links.arrived(slot + k, stream.at[core, y, z_from[k]], group(z_from[k] * 2 + core), t)
        yield from gather(stream, h)

        slot = links.reserve(NT)
        columns = stream[...].reshape(1024, lanes)
        for k in range(1, NT + 1):
            to = lax.rem(t + k, NT)
            first = pl.multiple_of(to * 80, 80)
            gu[to] = dot(w_gu[pl.ds(first, 80), :], columns, nn).astype(BF)
            if k < NT:
                links.send(slot + k, gu.at[to], e_in.at[t], dp, to)
            else:
                e_in[t] = gu[t]
        yield
        for k in range(1, NT):
            links.arrived(slot + k, e_in.at[t_from[k]], dp, t_from[k])
        total = jnp.zeros((80, lanes), F32)
        for s in range(NT):
            total = total + e_in[s].astype(F32)
        scale = lax.rsqrt(total[36:37] / D + EPS)
        gate, up = total[:40] * scale, total[40:] * scale
        hidden = gate / (1.0 + jnp.exp(-gate)) * up
        hidden = jnp.where(iota((40, lanes), 0) < 36, hidden, 0.0)
        hidden = jnp.concatenate([hidden, jnp.zeros((8, lanes), F32)], axis=0).astype(BF)
        h_all[t] = hidden
        slot = links.reserve(NT)
        for k in range(1, NT):
            links.send(slot + k, h_all.at[t], h_all.at[t], dp, t_to[k])
        yield
        for k in range(1, NT):
            links.arrived(slot + k, h_all.at[t_from[k]], dp, t_from[k])

        for block in range(lanes // 128):
            span = slice(block * 128, (block + 1) * 128)
            value = dot(h_all[:, :, span].reshape(384, 128), w_d[...], tn)
            part[span] = value + dot(stream[core, y, z, :, span], place, tn)

        f_out[...] = part[:, other].astype(BF)
        slot = links.reserve(1)
        links.send(slot, f_out, f_in, partner, t)
        yield
        links.arrived(slot, f_in, partner, t)
        acc[...] = (part[:, mine] + f_in[...].astype(F32)).reshape(NY, rows, KVL)
        value = yield from scatter(acc, r_out, r_in, h)
        last[FIRST[h] * 16 : FIRST[h] * 16 + rows] = value.astype(BF)

    place = jnp.logical_and(iota((16, 896), 1) == dp * 14 + iota((16, 896), 0), iota((16, 896), 0) < 14).astype(BF)
    mine = pl.ds(pl.multiple_of(core * 384, 128), KVL)
    other = pl.ds(pl.multiple_of((1 - core) * 384, 128), KVL)
    running = [chain(h) for h in range(len(PARTS))]
    while running:
        running = [steps for steps in running if next(steps, DONE) is not DONE]

    row, col = iota((128, 1), 0), iota((128, 80), 1)
    token = rem(row, 16)
    at = jnp.full((128, 1), -1, jnp.int32)
    for h, requests in enumerate(PARTS):
        inner = token - 2 * FIRST[h]
        here = jnp.logical_and(inner >= 0, inner < 2 * requests)
        at = jnp.where(here, FIRST[h] * 16 + div(row, 16) * (2 * requests) + inner, at)
    spread = (col == at).astype(BF)
    g_out[...] = dot(spread, last[...], nn).astype(BF).reshape(NG, 16, KVL)
    slot = links.reserve(NG)
    for k in range(1, NG):
        links.send(slot + k, g_out.at[g_to[k]], g_in.at[g], group(g_to[k]), t)
    g_in[g] = g_out[g]
    for k in range(1, NG):
        links.arrived(slot + k, g_in.at[g_from[k]], group(g_from[k]), t)
    first = jnp.zeros((16, KVL), F32)
    second = jnp.zeros((16, KVL), F32)
    for s in range(4):
        first = first + g_in[2 * s].astype(F32)
        second = second + g_in[2 * s + 1].astype(F32)
    out[:, :KVL] = first.astype(BF)[:10]
    out[:, KVL:] = second.astype(BF)[:10, 128:]
    links.finish()


SLOTS = 8 * 6 + len(PARTS) * (2 * 15 + 5 * 8 + 4 + 1 + 7)


def layer(*operands):
    scratch = [
        ((144, LAT), BF),
        ((NY, 48, 384), BF),
        ((NY, 48, 384), BF),
        ((NG, 48, 384), BF),
        ((NG, 48, 384), BF),
        ((NG, 48, 192), BF),
        ((NG, 48, 192), BF),
        ((NY, 48, 192), BF),
        ((NY, 48, 192), BF),
        ((NT * 80, 1024), BF),
        ((128, 1024), BF),
        ((384, 896), BF),
        ((NT, REQ, 16, LAT), BF),
        ((REQ, KEYS, LAT), BF),
        ((80, KVL), BF),
        ((NG, 16, KVL), BF),
        ((NG, 16, KVL), BF),
    ]
    for requests, padded in zip(PARTS, HALF_ROWS):
        rows, lanes = 16 * requests, 128 * requests
        scratch += [
            ((16, lanes), F32),
            ((NT, requests, 16, 640), BF),
            ((NT, requests, 16, 640), BF),
            ((2, padded, HD), BF),
            ((NG, padded, HD), BF),
            ((2, NY, rows, KVL), BF),
            ((NT, 16, lanes), BF),
            ((NT, 16, lanes), BF),
            ((2, NY, 4, 16, lanes), BF),
            ((NT, 80, lanes), BF),
            ((NT, 80, lanes), BF),
            ((NT, 48, lanes), BF),
            ((lanes, 896), F32),
            ((lanes, KVL), BF),
            ((lanes, KVL), BF),
            ((NY, rows, KVL), F32),
            ((7, rows, KVL), BF),
            ((7, rows, KVL), BF),
        ]
    vmem = pl.BlockSpec(memory_space=pltpu.VMEM)
    held = [
        (pltpu.SMEM if i < 2 else pltpu.VMEM)(operand.shape, operand.dtype) for i, operand in enumerate(operands)
    ]
    return pl.pallas_call(
        kernel,
        out_shape=jax.ShapeDtypeStruct((10, 896), BF),
        in_specs=[pl.BlockSpec(memory_space=pl.ANY)] * 14,
        out_specs=vmem,
        scratch_shapes=held
        + [pltpu.VMEM(shape, kind) for shape, kind in scratch]
        + [pltpu.SemaphoreType.DMA((SLOTS,)), pltpu.SemaphoreType.DMA((SLOTS,)), pltpu.SemaphoreType.DMA((14,))],
        compiler_params=pltpu.CompilerParams(
            collective_id=0, has_side_effects=True, vmem_limit_bytes=60 * 1024 * 1024
        ),
        cost_estimate=pl.CostEstimate(flops=3 * 10**9, bytes_accessed=10**7, transcendentals=10**6),
        name="layer",
    )(*operands)


def local(
    pool,
    page_table,
    lengths,
    mig_page,
    mig_dest,
    queries,
    new_latent,
    w_uv,
    w_out,
    residual,
    norm_gain,
    w_gate,
    w_up,
    w_down,
):
    return layer(
        page_table,
        lengths,
        mig_page,
        mig_dest,
        queries.reshape(REQ, 16, LAT),
        pool.reshape(POOL * PAGE, LAT),
        new_latent,
        w_uv,
        w_out.transpose(2, 1, 0).reshape(112, 1024),
        residual.reshape(TOK, 14).T,
        norm_gain,
        w_gate.T,
        w_up.T,
        w_down,
    )


def solution(mesh):
    in_specs = (
        P("dp", None, None),
        P("dp", None),
        P("dp"),
        P("dp", None),
        P("dp", None),
        P("dp", "tp", None),
        P("dp", None),
        P("tp", None, None),
        P("tp", None, "dp"),
        P(None, "tp", "dp"),
        P("tp"),
        P("tp", "dp"),
        P("tp", "dp"),
        P("dp", "tp"),
    )
    out_specs = P("dp", "tp")
    return jax.shard_map(local, mesh=mesh, in_specs=in_specs, out_specs=out_specs, check_vma=False)
```

```python
import functools

import jax
import jax.numpy as jnp
from jax import lax
from jax.experimental import pallas as pl
from jax.experimental.pallas import tpu as pltpu
from jax.sharding import PartitionSpec as P

D = 7168
HD = 128
KVL = 512
LAT = 576
PAGE = 16
MAXP = 13
REQ = 5
POOL = 65
CAP = 3
NY = 8
NG = 8
NT = 8
NX = 4
KEYS = 32
TOK = 640
EPS = 1e-06
SCALE = 192 ** (-0.5)
BF = jnp.bfloat16
F32 = jnp.float32
MESH = pl.DeviceIdType.MESH
DEAD = -1e30
PARTS = (2, 3)
FIRST = tuple(sum(PARTS[:h]) for h in range(len(PARTS)))
PER_PART = 18
HALF_ROWS = tuple(-(-8 * requests // 16) * 16 for requests in PARTS)
SPANS = ((slice(0, 384), slice(384, 576)),)
DONE = object()


def dot(a, b, dims):
    return lax.dot_general(a, b, (dims, ((), ())), preferred_element_type=F32)


def div(value, by):
    return lax.shift_right_logical(value * (-(-(1 << 20) // by)), 20)


def rem(value, by):
    return value - by * div(value, by)


def iota(shape, axis):
    return lax.broadcasted_iota(jnp.int32, shape, axis)


class Links:
    def __init__(self, send_sems, recv_sems):
        self.send_sems, self.recv_sems, self.used, self.sent = send_sems, recv_sems, 0, []

    def reserve(self, count):
        first = self.used
        self.used += count
        return first

    def copy(self, slot, src, dst, dp, tp):
        return pltpu.make_async_remote_copy(
            src_ref=src,
            dst_ref=dst,
            send_sem=self.send_sems.at[slot],
            recv_sem=self.recv_sems.at[slot],
            device_id={"dp": dp, "tp": tp},
            device_id_type=MESH,
        )

    def send(self, slot, src, dst, dp, tp):
        copy = self.copy(slot, src, dst, dp, tp)
        copy.start()
        self.sent.append(copy)

    def arrived(self, slot, dst, dp, tp):
        self.copy(slot, dst, dst, dp, tp).wait_recv()

    def finish(self):
        for copy in self.sent:
            copy.wait_send()


def kernel(
    *refs
):
    operands, (out, *held), rest = refs[:14], refs[14:29], refs[29:]
    (
        table, lengths, mig_page, mig_dest, q, pool, fresh, w_uv, w_out, res, gain, w_gate, w_up, w_down
    ) = held
    (
    own, w_gu, w_o, w_d, q_all, keys, last, g_out, g_in, *buffers, send_sems, recv_sems, load_sems,
    ) = rest
    inbox, buffers = buffers[: 8 * len(SPANS)], buffers[8 * len(SPANS) :]
    loads = [pltpu.make_async_copy(*pair, load_sems.at[i]) for i, pair in enumerate(zip(operands, held))]
    for i in (5, 2, 3, 4, 8, 9, 13, 10, 11, 12, 6, 0, 1, 7):
        loads[i].start()

    dp, t = lax.axis_index("dp"), lax.axis_index("tp")
    y, g = dp // NG, lax.rem(dp, NG)
    z, core = g // 2, lax.rem(g, 2)
    links = Links(send_sems, recv_sems)
    t_to = [lax.rem(t + k, NT) for k in range(NT)]
    t_from = [lax.rem(t + NT - k, NT) for k in range(NT)]
    z_lo, x = t // NX, lax.rem(t, NX)
    x_to = [lax.rem(x + k, NX) for k in range(NX)]
    x_from = [lax.rem(x + NX - k, NX) for k in range(NX)]
    g_to = [lax.rem(g + k, NG) for k in range(NG)]
    g_from = [lax.rem(g + NG - k, NG) for k in range(NG)]
    y_to = [lax.rem(y + k, NY) for k in range(NY)]
    y_from = [lax.rem(y + NY - k, NY) for k in range(NY)]
    z_to = [lax.rem(z + k, 4) for k in range(4)]
    z_from = [lax.rem(z + 4 - k, 4) for k in range(4)]
    nn, nt, tn = ((1,), (0,)), ((1,), (1,)), ((0,), (0,))

    def dp_of(yy):
        return yy * NG + g

    def group(gg):
        return y * NG + gg

    barrier = pltpu.get_barrier_semaphore()
    for k in range(1, NT):
        pl.semaphore_signal(barrier, inc=1, device_id={"dp": dp, "tp": t_to[k]}, device_id_type=MESH)
    for k in range(1, NG):
        pl.semaphore_signal(barrier, inc=1, device_id={"dp": group(g_to[k]), "tp": t}, device_id_type=MESH)
    for k in range(1, NY):
        pl.semaphore_signal(barrier, inc=1, device_id={"dp": dp_of(y_to[k]), "tp": t}, device_id_type=MESH)

    for i in (2, 3):
        loads[i].wait()
    row = iota((384, 1), 0)
    inner = rem(row, 6)
    entry = rem(iota((1, CAP * 28), 1), CAP)

    def outgoing(rank):
        match = jnp.logical_and(mig_dest[...] == rank, entry == div(inner, 2))
        source = jnp.sum(jnp.where(match, (mig_page[...] + 1).astype(F32), 0.0), axis=1, keepdims=True)
        source = source.astype(jnp.int32) * 2 - 2 + rem(inner, 2)
        return (source == iota((384, 144), 1)).astype(BF)

    first, second = div(row, 48), div(rem(row, 48), 6)
    for_y, for_g = outgoing(first * NG + second), outgoing(second * NG + first)
    row = iota((144, 1), 0)
    column = (div(row, 2)) * PAGE + 2 * t + rem(row, 2)
    two = (column == iota((144, POOL * PAGE), 1)).astype(BF)
    row, col = iota((384, 1), 0), iota((384, 384), 1)
    swap = (col == (div(rem(row, 48), 6)) * 48 + (div(row, 48)) * 6 + rem(row, 6)).astype(BF)
    for i in (5, 4):
        loads[i].wait()
    own[...] = dot(two, pool[...], nn).astype(BF)

    def exchange(span_y, span_z, y1, y2, y3, y4, z1, z2, z3, z4):
        width_y, width_z = span_y.stop - span_y.start, span_z.stop - span_z.start
        y1[...] = dot(for_y, own[:, span_y], nn).astype(BF).reshape(NY, 48, width_y)
        z1[...] = dot(for_g, own[:, span_z], nn).astype(BF).reshape(NG, 48, width_z)
        along_y, along_g = links.reserve(NY), links.reserve(NG)
        for k in range(1, NY):
            links.send(along_y + k, y1.at[y_to[k]], y2.at[y], dp_of(y_to[k]), t)
            links.send(along_g + k, z1.at[g_to[k]], z2.at[g], group(g_to[k]), t)
        y2[y] = y1[y]
        z2[g] = z1[g]
        yield
        for k in range(1, NY):
            links.arrived(along_y + k, y2.at[y_from[k]], dp_of(y_from[k]), t)
            links.arrived(along_g + k, z2.at[g_from[k]], group(g_from[k]), t)
        y3[...] = dot(swap, y2[...].reshape(384, width_y), nn).astype(BF).reshape(NG, 48, width_y)
        z3[...] = dot(swap, z2[...].reshape(384, width_z), nn).astype(BF).reshape(NY, 48, width_z)
        along_g, along_y = links.reserve(NG), links.reserve(NY)
        for k in range(1, NY):
            links.send(along_g + k, y3.at[g_to[k]], y4.at[g], group(g_to[k]), t)
            links.send(along_y + k, z3.at[y_to[k]], z4.at[y], dp_of(y_to[k]), t)
        y4[g] = y3[g]
        z4[y] = z3[y]
        yield
        for k in range(1, NY):
            links.arrived(along_g + k, y4.at[g_from[k]], group(g_from[k]), t)
            links.arrived(along_y + k, z4.at[y_from[k]], dp_of(y_from[k]), t)

    pages = [exchange(*spans, *inbox[8 * i : 8 * i + 8]) for i, spans in enumerate(SPANS)]
    q_all[x] = q[...]
    pl.semaphore_wait(barrier, 21)
    for steps in pages:
        next(steps)
    to_heads = links.reserve(NX)
    for k in range(1, NX):
        links.send(to_heads + k, q_all.at[x], q_all.at[x], dp, z_lo * NX + x_to[k])

    for i in (8, 9, 13, 10, 11, 12):
        loads[i].wait()
    row, col = iota((128, 1), 0), iota((128, 112), 1)
    spread = jnp.logical_and(rem(row, 16) < 14, col == rem(row, 16) * 8 + div(row, 16)).astype(BF)
    w_o[...] = dot(spread, w_out[...], nn).astype(BF)
    row, col = iota((384, 1), 0), iota((384, 288), 1)
    spread = jnp.logical_and(rem(row, 48) < 36, col == (div(row, 48)) * 36 + rem(row, 48)).astype(BF)
    w_d[...] = dot(spread, w_down[...], nn).astype(BF)
    for h, requests in enumerate(PARTS):
        tokens = 2 * requests
        row, col = iota((TOK, 1), 0), iota((1, 64 * tokens), 1)
        at = div(col, tokens) * 10 + rem(col, tokens) + 2 * FIRST[h]
        values = dot(res[...], (row == at).astype(BF), nn)
        buffers[h * PER_PART][...] = jnp.concatenate([values, jnp.zeros((2, 64 * tokens), F32)], axis=0)

    for steps in pages:
        next(steps)

    row, col = iota((NT * 80, 1), 0), iota((NT * 80, 288), 1)
    slot = rem(row, 80)
    of_gate = jnp.logical_and(slot < 36, col == (div(row, 80)) * 36 + slot).astype(BF)
    of_up = jnp.logical_and(jnp.logical_and(slot >= 40, slot < 76), col == (div(row, 80)) * 36 + slot - 40).astype(BF)
    scale = gain[...].astype(F32).reshape(1, 896)
    rows = dot(of_gate, (w_gate[...].astype(F32) * scale).astype(BF), nn)
    rows = (rows + dot(of_up, (w_up[...].astype(F32) * scale).astype(BF), nn)).astype(BF)
    row, col = iota((896, 1), 0), iota((896, 1024), 1)
    rank = div(row, 14)
    at = rem(rank, 2) * 512 + (div(rank, 2)) * 16 + rem(row, 14)
    spread = (col == at).astype(BF)
    squares_at = jnp.logical_and(rem(iota((NT * 80, 1), 0), 80) == 36, rem(iota((1, 1024), 1), 16) >= 14)
    w_gu[...] = jnp.where(squares_at, 1.0, dot(rows, spread, nn)).astype(BF)

    for steps in pages:
        next(steps, DONE)

    for i in (6, 0, 1):
        loads[i].wait()
    row = iota((REQ * KEYS, 1), 0)
    place, request = rem(row, KEYS), div(row, KEYS)
    named = jnp.full((REQ * KEYS, 1), -1, jnp.int32)
    for r in range(REQ):
        for k in range(MAXP):
            named = jnp.where(jnp.logical_and(request == r, div(place, 2) == k), table[r, k], named)
    token = rem(place, 2)
    from_own = (jnp.where(jnp.logical_and(named >= 0, named < POOL), 2 * named + token, -1) == iota((REQ * KEYS, 144), 1)).astype(BF)
    migrated = jnp.maximum(named - POOL, 0)
    rank = div(migrated, 3)
    inner = (migrated - CAP * rank) * 2 + token
    rank_y, rank_g = div(rank, NG), rem(rank, NG)
    in_inbox = named >= POOL
    at = jnp.where(in_inbox, rank_g * 48 + rank_y * 6 + inner, -1)
    from_y = (at == iota((REQ * KEYS, 384), 1)).astype(BF)
    at = jnp.where(in_inbox, rank_y * 48 + rank_g * 6 + inner, -1)
    from_z = (at == iota((REQ * KEYS, 384), 1)).astype(BF)
    at = jnp.where(jnp.logical_and(place >= 26, place < 28), 2 * request + place - 26, -1)
    from_fresh = (at == iota((REQ * KEYS, 2 * REQ), 1)).astype(BF)
    for i, spans in enumerate(SPANS):
        arrived = inbox[8 * i + 3], inbox[8 * i + 7]
        for span, source, found in zip(spans, (from_y, from_z), arrived):
            width = span.stop - span.start
            rows = dot(from_own, own[:, span], nn) + dot(from_fresh, fresh[:, span], nn)
            rows = rows + dot(source, found[...].reshape(384, width), nn)
            keys[z_lo, :, :, span] = rows.astype(BF).reshape(REQ, KEYS, width)
    opposite = lax.rem(t + NX, NT)
    to_opposite = links.reserve(len(PARTS))
    for h, requests in enumerate(PARTS):
        mine = keys.at[z_lo, FIRST[h] : FIRST[h] + requests]
        links.send(to_opposite + h, mine, mine, dp, opposite)
    for k in range(1, NX):
        links.arrived(to_heads + k, q_all.at[x_from[k]], dp, opposite)

    def attend(h):
        requests = PARTS[h]
        span = range(FIRST[h], FIRST[h] + requests)
        links.arrived(to_opposite + h, keys.at[1 - z_lo, FIRST[h] : FIRST[h] + requests], dp, opposite)
        held = [keys[:, r].reshape(2 * KEYS, LAT) for r in span]
        scores = [dot(q_all[:, r].reshape(NX * 16, LAT), k, nt) for r, k in zip(span, held)]
        scores = jnp.concatenate(scores, axis=0) * SCALE
        row, col = iota((requests * 64, 1), 0), iota((1, 2 * KEYS), 1)
        length = jnp.full((requests * 64, 1), lengths[FIRST[h]], jnp.int32)
        for i in range(1, requests):
            length = jnp.where(row >= i * 64, lengths[FIRST[h] + i], length)
        place, source = rem(col, KEYS), div(col, KEYS) * NX + x
        token = div(place, 2) * PAGE + 2 * source + rem(place, 2)
        cached = jnp.logical_and(jnp.where(place < 26, token, MAXP * PAGE) < length, place < 26)
        newest = jnp.where(source == 0, 26 + rem(div(row, 8), 2), 0)
        newer = jnp.logical_and(place >= 26, place <= newest)
        live = jnp.logical_or(cached, newer)
        scores = jnp.where(live, scores, DEAD)
        top = jnp.max(scores, axis=1, keepdims=True)
        weights = jnp.where(live, jnp.exp(scores - top), 0.0)
        total = jnp.sum(weights, axis=1, keepdims=True)
        some = total > 0.0
        total = jnp.where(some, total, 1.0)
        weights = (weights / total).astype(BF)
        lse = jnp.where(some, top + jnp.log(total), DEAD)
        high = lse.astype(BF).astype(F32)
        middle = (lse - high).astype(BF).astype(F32)
        low = lse - high - middle
        lane = iota((requests * 64, 128), 1)
        parts = jnp.where(lane == 0, high, jnp.where(lane == 1, middle, jnp.where(lane == 2, low, 0.0))).astype(BF)
        latent = [dot(weights[i * 64 : (i + 1) * 64], k[:, :KVL], nn) for i, k in enumerate(held)]
        return latent, [parts[i * 64 : (i + 1) * 64] for i in range(requests)]

    loads[7].wait()
    partner = dp + 1 - 2 * core

    def at_y(step):
        return lax.rem(y + NY + step, NY)

    def gather(buf, flip):
        near, far, over = links.reserve(4), links.reserve(3), links.reserve(8)
        held_y = []

        def pass_on(index):
            links.send(over + len(held_y), buf.at[core, index], buf.at[core, index], partner, t)
            held_y.append(index)

        def forward(slot, index, step):
            links.send(slot, buf.at[core, index], buf.at[core, index], dp_of(at_y(step)), t)

        def arrived(slot, index):
            links.arrived(slot, buf.at[core, index], partner, t)

        for i, step in enumerate((2, -2, 1, -1)):
            forward(near + i, y, step)
        pass_on(y)
        yield
        arrived(near, at_y(-2))
        forward(far, at_y(-2), 1)
        if flip:
            forward(far + 2, at_y(-2), 2)
        arrived(near + 1, at_y(2))
        forward(far + 1, at_y(2), -1)
        if not flip:
            forward(far + 2, at_y(2), -2)
        pass_on(at_y(-2))
        pass_on(at_y(2))
        for i, step in ((2, -1), (3, 1)):
            arrived(near + i, at_y(step))
            pass_on(at_y(step))
        yield
        for i, step in ((0, -3), (1, 3), (2, 4)):
            arrived(far + i, at_y(step))
            pass_on(at_y(step))
        for order, index in enumerate(held_y):
            links.arrived(over + order, buf.at[1 - core, index], partner, t)

    def scatter(acc, r_out, r_in, flip):
        slot = links.reserve(7)

        def send(i, value, step):
            r_out[i] = value.astype(BF)
            links.send(slot + i, r_out.at[i], r_in.at[i], dp_of(at_y(step)), t)

        def received(i):
            links.arrived(slot + i, r_in.at[i], partner, t)
            return r_in[i].astype(F32)

        send(2, acc[at_y(4)], 2 if flip else -2)
        send(0, acc[at_y(-3)], -1)
        send(1, acc[at_y(3)], 1)
        send(3, acc[at_y(-1)], -1)
        send(4, acc[at_y(1)], 1)
        yield
        below, above = acc[at_y(-2)] + received(0), acc[at_y(2)] + received(1)
        if flip:
            above = above + received(2)
        else:
            below = below + received(2)
        send(5, below, -2)
        send(6, above, 2)
        yield
        value = acc[y]
        for i in range(3, 7):
            value = value + received(i)
        return value

    def chain(h):
        requests = PARTS[h]
        tokens = 2 * requests
        rows, lanes = NG * tokens, 64 * tokens
        padded = HALF_ROWS[h]
        (
            res_h, o_out, o_in, ho, b_in, heads, pj, c_in, stream, gu, e_in, h_all, part, f_out, f_in, acc, r_out, r_in
        ) = buffers[h * PER_PART : (h + 1) * PER_PART]
        for i, (latent, lse) in enumerate(zip(*attend(h))):
            o_out[:, i, :, :KVL] = latent.astype(BF).reshape(NX, 16, KVL)
            o_out[:, i, :, KVL:] = lse.reshape(NX, 16, 128)
        slot = links.reserve(NX)
        for k in range(1, NX):
            links.send(slot + k, o_out.at[x_to[k]], o_in.at[x], dp, z_lo * NX + x_to[k])
        o_in[x] = o_out[x]
        yield
        for k in range(1, NX):
            links.arrived(slot + k, o_in.at[x_from[k]], dp, opposite)
        lse = [jnp.sum(o_in[s, :, :, KVL:].astype(F32), axis=2, keepdims=True) for s in range(NX)]
        top = functools.reduce(jnp.maximum, lse)
        shares = [jnp.exp(v - top) for v in lse]
        total = functools.reduce(jnp.add, shares)
        latent = jnp.zeros((requests, 16, KVL), F32)
        for s in range(NX):
            latent = latent + o_in[s, :, :, :KVL].astype(F32) * (shares[s] / total)
        latent = latent.astype(BF).reshape(requests * 16, KVL)

        head = rem(iota((requests * 16, 1), 0), 8)
        values = jnp.zeros((requests * 16, HD), F32)
        for i in range(8):
            values = jnp.where(head == i, dot(latent, w_uv[i], nn), values)
        row, col = iota((2 * padded, 1), 0), iota((2 * padded, requests * 16), 1)
        inner = rem(row, padded)
        at = div(inner, 4) * 8 + div(row, padded) * 4 + rem(inner, 4)
        split = jnp.logical_and(inner < 4 * tokens, col == at).astype(BF)
        ho[...] = dot(split, values.astype(BF), nn).astype(BF).reshape(2, padded, HD)

        slot = links.reserve(NG)
        for k in range(1, NG):
            links.send(slot + k, ho.at[lax.rem(g_to[k], 2)], b_in.at[g], group(g_to[k]), t)
        b_in[g] = ho[core]
        yield
        for k in range(1, NG):
            links.arrived(slot + k, b_in.at[g_from[k]], group(g_from[k]), t)
        row, col = iota((rows, 1), 0), iota((rows, NG * padded), 1)
        at = div(row, tokens) * padded + rem(row, tokens) * 4
        gathered = b_in[...].reshape(NG * padded, HD)
        for i in range(4):
            heads[core, y, :, i * HD : (i + 1) * HD] = dot((col == at + i).astype(BF), gathered, nn).astype(BF)
        yield from gather(heads, h)

        projected = dot(w_o[:, :KVL], heads[0].reshape(lanes, KVL), nt)
        projected = projected + dot(w_o[:, KVL:], heads[1].reshape(lanes, KVL), nt)
        pj[...] = projected.astype(BF).reshape(NT, 16, lanes)
        slot = links.reserve(NT)
        for k in range(1, NT):
            links.send(slot + k, pj.at[t_to[k]], c_in.at[t], dp, t_to[k])
        c_in[t] = pj[t]
        yield
        for k in range(1, NT):
            links.arrived(slot + k, c_in.at[t_from[k]], dp, t_from[k])
        summed = res_h[...]
        for s in range(NT):
            summed = summed + c_in[s].astype(F32)
        summed = summed.astype(BF).astype(F32)
        squares = jnp.sum(summed * summed, axis=0, keepdims=True)
        high = squares.astype(BF).astype(F32)
        row = iota((16, lanes), 0)
        piece = jnp.where(row == 14, high, jnp.where(row == 15, squares - high, summed)).astype(BF)
        stream[core, y, z] = piece

        slot = links.reserve(4)
        for k in range(1, 4):
            block = stream.at[core, y, z]
            links.send(slot + k, block, block, group(z_to[k] * 2 + core), t)
        yield
        for k in range(1, 4):
            links.arrived(slot + k, stream.at[core, y, z_from[k]], group(z_from[k] * 2 + core), t)
        yield from gather(stream, h)

        slot = links.reserve(NT)
        columns = stream[...].reshape(1024, lanes)
        for k in range(1, NT + 1):
            to = lax.rem(t + k, NT)
            first = pl.multiple_of(to * 80, 80)
            gu[to] = dot(w_gu[pl.ds(first, 80), :], columns, nn).astype(BF)
            if k < NT:
                links.send(slot + k, gu.at[to], e_in.at[t], dp, to)
            else:
                e_in[t] = gu[t]
        yield
        for k in range(1, NT):
            links.arrived(slot + k, e_in.at[t_from[k]], dp, t_from[k])
        total = jnp.zeros((80, lanes), F32)
        for s in range(NT):
            total = total + e_in[s].astype(F32)
        scale = lax.rsqrt(total[36:37] / D + EPS)
        gate, up = total[:40] * scale, total[40:] * scale
        hidden = gate / (1.0 + jnp.exp(-gate)) * up
        hidden = jnp.where(iota((40, lanes), 0) < 36, hidden, 0.0)
        hidden = jnp.concatenate([hidden, jnp.zeros((8, lanes), F32)], axis=0).astype(BF)
        h_all[t] = hidden
        slot = links.reserve(NT)
        for k in range(1, NT):
            links.send(slot + k, h_all.at[t], h_all.at[t], dp, t_to[k])
        yield
        for k in range(1, NT):
            links.arrived(slot + k, h_all.at[t_from[k]], dp, t_from[k])

        for block in range(lanes // 128):
            span = slice(block * 128, (block + 1) * 128)
            value = dot(h_all[:, :, span].reshape(384, 128), w_d[...], tn)
            part[span] = value + dot(stream[core, y, z, :, span], place, tn)

        f_out[...] = part[:, other].astype(BF)
        slot = links.reserve(1)
        links.send(slot, f_out, f_in, partner, t)
        yield
        links.arrived(slot, f_in, partner, t)
        acc[...] = (part[:, mine] + f_in[...].astype(F32)).reshape(NY, rows, KVL)
        value = yield from scatter(acc, r_out, r_in, h)
        last[FIRST[h] * 16 : FIRST[h] * 16 + rows] = value.astype(BF)

    place = jnp.logical_and(iota((16, 896), 1) == dp * 14 + iota((16, 896), 0), iota((16, 896), 0) < 14).astype(BF)
    mine = pl.ds(pl.multiple_of(core * 384, 128), KVL)
    other = pl.ds(pl.multiple_of((1 - core) * 384, 128), KVL)
    running = [chain(h) for h in range(len(PARTS))]
    while running:
        running = [steps for steps in running if next(steps, DONE) is not DONE]

    row, col = iota((128, 1), 0), iota((128, 80), 1)
    token = rem(row, 16)
    at = jnp.full((128, 1), -1, jnp.int32)
    for h, requests in enumerate(PARTS):
        inner = token - 2 * FIRST[h]
        here = jnp.logical_and(inner >= 0, inner < 2 * requests)
        at = jnp.where(here, FIRST[h] * 16 + div(row, 16) * (2 * requests) + inner, at)
    spread = (col == at).astype(BF)
    g_out[...] = dot(spread, last[...], nn).astype(BF).reshape(NG, 16, KVL)
    slot = links.reserve(NG)
    for k in range(1, NG):
        links.send(slot + k, g_out.at[g_to[k]], g_in.at[g], group(g_to[k]), t)
    g_in[g] = g_out[g]
    for k in range(1, NG):
        links.arrived(slot + k, g_in.at[g_from[k]], group(g_from[k]), t)
    first = jnp.zeros((16, KVL), F32)
    second = jnp.zeros((16, KVL), F32)
    for s in range(4):
        first = first + g_in[2 * s].astype(F32)
        second = second + g_in[2 * s + 1].astype(F32)
    out[:, :KVL] = first.astype(BF)[:10]
    out[:, KVL:] = second.astype(BF)[:10, 128:]
    links.finish()


SLOTS = 8 * 2 + len(SPANS) * 8 * 4 + len(PARTS) * (2 * 15 + 5 * 8 + 4 + 1 + 7)


def layer(*operands):
    scratch = [
        ((144, LAT), BF),
        ((NT * 80, 1024), BF),
        ((128, 1024), BF),
        ((384, 896), BF),
        ((NX, REQ, 16, LAT), BF),
        ((2, REQ, KEYS, LAT), BF),
        ((80, KVL), BF),
        ((NG, 16, KVL), BF),
        ((NG, 16, KVL), BF),
    ]
    for spans in SPANS:
        for span in spans:
            scratch += [((8, 48, span.stop - span.start), BF)] * 4
    for requests, padded in zip(PARTS, HALF_ROWS):
        rows, lanes = 16 * requests, 128 * requests
        scratch += [
            ((16, lanes), F32),
            ((NX, requests, 16, 640), BF),
            ((NX, requests, 16, 640), BF),
            ((2, padded, HD), BF),
            ((NG, padded, HD), BF),
            ((2, NY, rows, KVL), BF),
            ((NT, 16, lanes), BF),
            ((NT, 16, lanes), BF),
            ((2, NY, 4, 16, lanes), BF),
            ((NT, 80, lanes), BF),
            ((NT, 80, lanes), BF),
            ((NT, 48, lanes), BF),
            ((lanes, 896), F32),
            ((lanes, KVL), BF),
            ((lanes, KVL), BF),
            ((NY, rows, KVL), F32),
            ((7, rows, KVL), BF),
            ((7, rows, KVL), BF),
        ]
    vmem = pl.BlockSpec(memory_space=pltpu.VMEM)
    held = [
        (pltpu.SMEM if i < 2 else pltpu.VMEM)(operand.shape, operand.dtype) for i, operand in enumerate(operands)
    ]
    return pl.pallas_call(
        kernel,
        out_shape=jax.ShapeDtypeStruct((10, 896), BF),
        in_specs=[pl.BlockSpec(memory_space=pl.ANY)] * 14,
        out_specs=vmem,
        scratch_shapes=held
        + [pltpu.VMEM(shape, kind) for shape, kind in scratch]
        + [pltpu.SemaphoreType.DMA((SLOTS,)), pltpu.SemaphoreType.DMA((SLOTS,)), pltpu.SemaphoreType.DMA((14,))],
        compiler_params=pltpu.CompilerParams(
            collective_id=0, has_side_effects=True, vmem_limit_bytes=60 * 1024 * 1024
        ),
        cost_estimate=pl.CostEstimate(flops=3 * 10**9, bytes_accessed=10**7, transcendentals=10**6),
        name="layer",
    )(*operands)


def local(
    pool,
    page_table,
    lengths,
    mig_page,
    mig_dest,
    queries,
    new_latent,
    w_uv,
    w_out,
    residual,
    norm_gain,
    w_gate,
    w_up,
    w_down,
):
    return layer(
        page_table,
        lengths,
        mig_page,
        mig_dest,
        queries.reshape(REQ, 16, LAT),
        pool.reshape(POOL * PAGE, LAT),
        new_latent,
        w_uv,
        w_out.transpose(2, 1, 0).reshape(112, 1024),
        residual.reshape(TOK, 14).T,
        norm_gain,
        w_gate.T,
        w_up.T,
        w_down,
    )


def solution(mesh):
    in_specs = (
        P("dp", None, None),
        P("dp", None),
        P("dp"),
        P("dp", None),
        P("dp", None),
        P("dp", "tp", None),
        P("dp", None),
        P("tp", None, None),
        P("tp", None, "dp"),
        P(None, "tp", "dp"),
        P("tp"),
        P("tp", "dp"),
        P("tp", "dp"),
        P("dp", "tp"),
    )
    out_specs = P("dp", "tp")
    return jax.shard_map(local, mesh=mesh, in_specs=in_specs, out_specs=out_specs, check_vma=False)
```

```python
import functools

import jax
import jax.numpy as jnp
from jax import lax
from jax.experimental import pallas as pl
from jax.experimental.pallas import tpu as pltpu
from jax.sharding import PartitionSpec as P

D = 7168
HD = 128
KVL = 512
LAT = 576
PAGE = 16
MAXP = 13
REQ = 5
POOL = 65
CAP = 3
NY = 8
NG = 8
NT = 8
NX = 4
KEYS = 32
TOK = 640
EPS = 1e-06
SCALE = 192 ** (-0.5)
BF = jnp.bfloat16
F32 = jnp.float32
MESH = pl.DeviceIdType.MESH
DEAD = -1e30
PARTS = (2, 3)
FIRST = tuple(sum(PARTS[:h]) for h in range(len(PARTS)))
PER_PART = 20
HALF_ROWS = tuple(-(-8 * requests // 16) * 16 for requests in PARTS)
SPANS = ((slice(0, 256), slice(384, 512)), (slice(256, 384), slice(512, 576)))
DONE = object()


def dot(a, b, dims):
    return lax.dot_general(a, b, (dims, ((), ())), preferred_element_type=F32)


def div(value, by):
    return lax.shift_right_logical(value * (-(-(1 << 20) // by)), 20)


def rem(value, by):
    return value - by * div(value, by)


def iota(shape, axis):
    return lax.broadcasted_iota(jnp.int32, shape, axis)


class Links:
    def __init__(self, send_sems, recv_sems):
        self.send_sems, self.recv_sems, self.used, self.sent = send_sems, recv_sems, 0, []

    def reserve(self, count):
        first = self.used
        self.used += count
        return first

    def copy(self, slot, src, dst, dp, tp):
        return pltpu.make_async_remote_copy(
            src_ref=src,
            dst_ref=dst,
            send_sem=self.send_sems.at[slot],
            recv_sem=self.recv_sems.at[slot],
            device_id={"dp": dp, "tp": tp},
            device_id_type=MESH,
        )

    def send(self, slot, src, dst, dp, tp):
        copy = self.copy(slot, src, dst, dp, tp)
        copy.start()
        self.sent.append(copy)

    def arrived(self, slot, dst, dp, tp):
        self.copy(slot, dst, dst, dp, tp).wait_recv()

    def finish(self):
        for copy in self.sent:
            copy.wait_send()


def kernel(
    *refs
):
    operands, (out, *held), rest = refs[:14], refs[14:29], refs[29:]
    (
        table, lengths, mig_page, mig_dest, q, pool, fresh, w_uv, w_out, res, gain, w_gate, w_up, w_down
    ) = held
    (
    own, w_gu, w_o, w_d, q_all, keys, *buffers, send_sems, recv_sems, load_sems,
    ) = rest
    inbox, buffers = buffers[: 8 * len(SPANS)], buffers[8 * len(SPANS) :]
    loads = [pltpu.make_async_copy(*pair, load_sems.at[i]) for i, pair in enumerate(zip(operands, held))]
    for i in (5, 2, 3, 4, 8, 9, 13, 10, 11, 12, 6, 0, 1, 7):
        loads[i].start()

    dp, t = lax.axis_index("dp"), lax.axis_index("tp")
    y, g = dp // NG, lax.rem(dp, NG)
    z, core = g // 2, lax.rem(g, 2)
    links = Links(send_sems, recv_sems)
    t_to = [lax.rem(t + k, NT) for k in range(NT)]
    t_from = [lax.rem(t + NT - k, NT) for k in range(NT)]
    z_lo, x = t // NX, lax.rem(t, NX)
    x_to = [lax.rem(x + k, NX) for k in range(NX)]
    x_from = [lax.rem(x + NX - k, NX) for k in range(NX)]
    g_to = [lax.rem(g + k, NG) for k in range(NG)]
    g_from = [lax.rem(g + NG - k, NG) for k in range(NG)]
    y_to = [lax.rem(y + k, NY) for k in range(NY)]
    y_from = [lax.rem(y + NY - k, NY) for k in range(NY)]
    z_to = [lax.rem(z + k, 4) for k in range(4)]
    z_from = [lax.rem(z + 4 - k, 4) for k in range(4)]
    nn, nt, tn = ((1,), (0,)), ((1,), (1,)), ((0,), (0,))

    def dp_of(yy):
        return yy * NG + g

    def group(gg):
        return y * NG + gg

    barrier = pltpu.get_barrier_semaphore()
    for k in range(1, NT):
        pl.semaphore_signal(barrier, inc=1, device_id={"dp": dp, "tp": t_to[k]}, device_id_type=MESH)
    for k in range(1, NG):
        pl.semaphore_signal(barrier, inc=1, device_id={"dp": group(g_to[k]), "tp": t}, device_id_type=MESH)
    for k in range(1, NY):
        pl.semaphore_signal(barrier, inc=1, device_id={"dp": dp_of(y_to[k]), "tp": t}, device_id_type=MESH)

    for i in (2, 3):
        loads[i].wait()
    row = iota((384, 1), 0)
    inner = rem(row, 6)
    entry = rem(iota((1, CAP * 28), 1), CAP)

    def outgoing(rank):
        match = jnp.logical_and(mig_dest[...] == rank, entry == div(inner, 2))
        source = jnp.sum(jnp.where(match, (mig_page[...] + 1).astype(F32), 0.0), axis=1, keepdims=True)
        source = source.astype(jnp.int32) * 2 - 2 + rem(inner, 2)
        return (source == iota((384, 144), 1)).astype(BF)

    first, second = div(row, 48), div(rem(row, 48), 6)
    for_y, for_g = outgoing(first * NG + second), outgoing(second * NG + first)
    row = iota((144, 1), 0)
    column = (div(row, 2)) * PAGE + 2 * t + rem(row, 2)
    two = (column == iota((144, POOL * PAGE), 1)).astype(BF)
    row, col = iota((384, 1), 0), iota((384, 384), 1)
    swap = (col == (div(rem(row, 48), 6)) * 48 + (div(row, 48)) * 6 + rem(row, 6)).astype(BF)
    for i in (5, 4):
        loads[i].wait()
    own[...] = dot(two, pool[...], nn).astype(BF)

    def exchange(span_y, span_z, y1, y2, y3, y4, z1, z2, z3, z4):
        width_y, width_z = span_y.stop - span_y.start, span_z.stop - span_z.start
        y1[...] = dot(for_y, own[:, span_y], nn).astype(BF).reshape(NY, 48, width_y)
        z1[...] = dot(for_g, own[:, span_z], nn).astype(BF).reshape(NG, 48, width_z)
        along_y, along_g = links.reserve(NY), links.reserve(NG)
        for k in range(1, NY):
            links.send(along_y + k, y1.at[y_to[k]], y2.at[y], dp_of(y_to[k]), t)
            links.send(along_g + k, z1.at[g_to[k]], z2.at[g], group(g_to[k]), t)
        y2[y] = y1[y]
        z2[g] = z1[g]
        yield
        for k in range(1, NY):
            links.arrived(along_y + k, y2.at[y_from[k]], dp_of(y_from[k]), t)
            links.arrived(along_g + k, z2.at[g_from[k]], group(g_from[k]), t)
        y3[...] = dot(swap, y2[...].reshape(384, width_y), nn).astype(BF).reshape(NG, 48, width_y)
        z3[...] = dot(swap, z2[...].reshape(384, width_z), nn).astype(BF).reshape(NY, 48, width_z)
        along_g, along_y = links.reserve(NG), links.reserve(NY)
        for k in range(1, NY):
            links.send(along_g + k, y3.at[g_to[k]], y4.at[g], group(g_to[k]), t)
            links.send(along_y + k, z3.at[y_to[k]], z4.at[y], dp_of(y_to[k]), t)
        y4[g] = y3[g]
        z4[y] = z3[y]
        yield
        for k in range(1, NY):
            links.arrived(along_g + k, y4.at[g_from[k]], group(g_from[k]), t)
            links.arrived(along_y + k, z4.at[y_from[k]], dp_of(y_from[k]), t)

    pages = [exchange(*spans, *inbox[8 * i : 8 * i + 8]) for i, spans in enumerate(SPANS)]
    q_all[x] = q[...]
    pl.semaphore_wait(barrier, 21)
    for steps in pages:
        next(steps)
    to_heads = links.reserve(NX)
    for k in range(1, NX):
        links.send(to_heads + k, q_all.at[x], q_all.at[x], dp, z_lo * NX + x_to[k])

    for i in (8, 9, 13, 10, 11, 12):
        loads[i].wait()
    row, col = iota((128, 1), 0), iota((128, 112), 1)
    spread = jnp.logical_and(rem(row, 16) < 14, col == rem(row, 16) * 8 + div(row, 16)).astype(BF)
    w_o[...] = dot(spread, w_out[...], nn).astype(BF)
    row, col = iota((384, 1), 0), iota((384, 288), 1)
    spread = jnp.logical_and(rem(row, 48) < 36, col == (div(row, 48)) * 36 + rem(row, 48)).astype(BF)
    w_d[...] = dot(spread, w_down[...], nn).astype(BF)
    for h, requests in enumerate(PARTS):
        tokens = 2 * requests
        row, col = iota((TOK, 1), 0), iota((1, 64 * tokens), 1)
        at = div(col, tokens) * 10 + rem(col, tokens) + 2 * FIRST[h]
        values = dot(res[...], (row == at).astype(BF), nn)
        buffers[h * PER_PART][...] = jnp.concatenate([values, jnp.zeros((2, 64 * tokens), F32)], axis=0)

    for steps in pages:
        next(steps)

    row, col = iota((NT * 80, 1), 0), iota((NT * 80, 288), 1)
    slot = rem(row, 80)
    of_gate = jnp.logical_and(slot < 36, col == (div(row, 80)) * 36 + slot).astype(BF)
    of_up = jnp.logical_and(jnp.logical_and(slot >= 40, slot < 76), col == (div(row, 80)) * 36 + slot - 40).astype(BF)
    scale = gain[...].astype(F32).reshape(1, 896)
    rows = dot(of_gate, (w_gate[...].astype(F32) * scale).astype(BF), nn)
    rows = (rows + dot(of_up, (w_up[...].astype(F32) * scale).astype(BF), nn)).astype(BF)
    row, col = iota((896, 1), 0), iota((896, 1024), 1)
    rank = div(row, 14)
    at = rem(rank, 2) * 512 + (div(rank, 2)) * 16 + rem(row, 14)
    spread = (col == at).astype(BF)
    squares_at = jnp.logical_and(rem(iota((NT * 80, 1), 0), 80) == 36, rem(iota((1, 1024), 1), 16) >= 14)
    w_gu[...] = jnp.where(squares_at, 1.0, dot(rows, spread, nn)).astype(BF)

    for steps in pages:
        next(steps, DONE)

    for i in (6, 0, 1):
        loads[i].wait()
    row = iota((REQ * KEYS, 1), 0)
    place, request = rem(row, KEYS), div(row, KEYS)
    named = jnp.full((REQ * KEYS, 1), -1, jnp.int32)
    for r in range(REQ):
        for k in range(MAXP):
            named = jnp.where(jnp.logical_and(request == r, div(place, 2) == k), table[r, k], named)
    token = rem(place, 2)
    from_own = (jnp.where(jnp.logical_and(named >= 0, named < POOL), 2 * named + token, -1) == iota((REQ * KEYS, 144), 1)).astype(BF)
    migrated = jnp.maximum(named - POOL, 0)
    rank = div(migrated, 3)
    inner = (migrated - CAP * rank) * 2 + token
    rank_y, rank_g = div(rank, NG), rem(rank, NG)
    in_inbox = named >= POOL
    at = jnp.where(in_inbox, rank_g * 48 + rank_y * 6 + inner, -1)
    from_y = (at == iota((REQ * KEYS, 384), 1)).astype(BF)
    at = jnp.where(in_inbox, rank_y * 48 + rank_g * 6 + inner, -1)
    from_z = (at == iota((REQ * KEYS, 384), 1)).astype(BF)
    at = jnp.where(jnp.logical_and(place >= 26, place < 28), 2 * request + place - 26, -1)
    from_fresh = (at == iota((REQ * KEYS, 2 * REQ), 1)).astype(BF)
    for i, spans in enumerate(SPANS):
        arrived = inbox[8 * i + 3], inbox[8 * i + 7]
        for span, source, found in zip(spans, (from_y, from_z), arrived):
            width = span.stop - span.start
            rows = dot(from_own, own[:, span], nn) + dot(from_fresh, fresh[:, span], nn)
            rows = rows + dot(source, found[...].reshape(384, width), nn)
            keys[z_lo, :, :, span] = rows.astype(BF).reshape(REQ, KEYS, width)
    opposite = lax.rem(t + NX, NT)
    to_opposite = links.reserve(len(PARTS))
    for h, requests in enumerate(PARTS):
        mine = keys.at[z_lo, FIRST[h] : FIRST[h] + requests]
        links.send(to_opposite + h, mine, mine, dp, opposite)
    for k in range(1, NX):
        links.arrived(to_heads + k, q_all.at[x_from[k]], dp, opposite)

    def attend(h):
        requests = PARTS[h]
        span = range(FIRST[h], FIRST[h] + requests)
        links.arrived(to_opposite + h, keys.at[1 - z_lo, FIRST[h] : FIRST[h] + requests], dp, opposite)
        held = [keys[:, r].reshape(2 * KEYS, LAT) for r in span]
        scores = [dot(q_all[:, r].reshape(NX * 16, LAT), k, nt) for r, k in zip(span, held)]
        scores = jnp.concatenate(scores, axis=0) * SCALE
        row, col = iota((requests * 64, 1), 0), iota((1, 2 * KEYS), 1)
        length = jnp.full((requests * 64, 1), lengths[FIRST[h]], jnp.int32)
        for i in range(1, requests):
            length = jnp.where(row >= i * 64, lengths[FIRST[h] + i], length)
        place, source = rem(col, KEYS), div(col, KEYS) * NX + x
        token = div(place, 2) * PAGE + 2 * source + rem(place, 2)
        cached = jnp.logical_and(jnp.where(place < 26, token, MAXP * PAGE) < length, place < 26)
        newest = jnp.where(source == 0, 26 + rem(div(row, 8), 2), 0)
        newer = jnp.logical_and(place >= 26, place <= newest)
        live = jnp.logical_or(cached, newer)
        scores = jnp.where(live, scores, DEAD)
        top = jnp.max(scores, axis=1, keepdims=True)
        weights = jnp.where(live, jnp.exp(scores - top), 0.0)
        total = jnp.sum(weights, axis=1, keepdims=True)
        some = total > 0.0
        total = jnp.where(some, total, 1.0)
        weights = (weights / total).astype(BF)
        lse = jnp.where(some, top + jnp.log(total), DEAD)
        high = lse.astype(BF).astype(F32)
        middle = (lse - high).astype(BF).astype(F32)
        low = lse - high - middle
        lane = iota((requests * 64, 128), 1)
        parts = jnp.where(lane == 0, high, jnp.where(lane == 1, middle, jnp.where(lane == 2, low, 0.0))).astype(BF)
        latent = [dot(weights[i * 64 : (i + 1) * 64], k[:, :KVL], nn) for i, k in enumerate(held)]
        return latent, [parts[i * 64 : (i + 1) * 64] for i in range(requests)]

    loads[7].wait()
    partner = dp + 1 - 2 * core

    def at_y(step):
        return lax.rem(y + NY + step, NY)

    def gather(buf, flip):
        near, far, over = links.reserve(4), links.reserve(3), links.reserve(8)
        held_y = []

        def pass_on(index):
            links.send(over + len(held_y), buf.at[core, index], buf.at[core, index], partner, t)
            held_y.append(index)

        def forward(slot, index, step):
            links.send(slot, buf.at[core, index], buf.at[core, index], dp_of(at_y(step)), t)

        def arrived(slot, index):
            links.arrived(slot, buf.at[core, index], partner, t)

        for i, step in enumerate((2, -2, 1, -1)):
            forward(near + i, y, step)
        pass_on(y)
        yield
        arrived(near, at_y(-2))
        forward(far, at_y(-2), 1)
        if flip:
            forward(far + 2, at_y(-2), 2)
        arrived(near + 1, at_y(2))
        forward(far + 1, at_y(2), -1)
        if not flip:
            forward(far + 2, at_y(2), -2)
        pass_on(at_y(-2))
        pass_on(at_y(2))
        for i, step in ((2, -1), (3, 1)):
            arrived(near + i, at_y(step))
            pass_on(at_y(step))
        yield
        for i, step in ((0, -3), (1, 3), (2, 4)):
            arrived(far + i, at_y(step))
            pass_on(at_y(step))
        for order, index in enumerate(held_y):
            links.arrived(over + order, buf.at[1 - core, index], partner, t)

    def scatter(acc, r_out, r_in, flip):
        slot = links.reserve(7)

        def send(i, value, step):
            r_out[i] = value.astype(BF)
            links.send(slot + i, r_out.at[i], r_in.at[i], dp_of(at_y(step)), t)

        def received(i):
            links.arrived(slot + i, r_in.at[i], partner, t)
            return r_in[i].astype(F32)

        send(2, acc[at_y(4)], 2 if flip else -2)
        send(0, acc[at_y(-3)], -1)
        send(1, acc[at_y(3)], 1)
        send(3, acc[at_y(-1)], -1)
        send(4, acc[at_y(1)], 1)
        yield
        below, above = acc[at_y(-2)] + received(0), acc[at_y(2)] + received(1)
        if flip:
            above = above + received(2)
        else:
            below = below + received(2)
        send(5, below, -2)
        send(6, above, 2)
        yield
        value = acc[y]
        for i in range(3, 7):
            value = value + received(i)
        return value

    def chain(h):
        requests = PARTS[h]
        tokens = 2 * requests
        rows, lanes = NG * tokens, 64 * tokens
        padded = HALF_ROWS[h]
        (
            res_h, o_out, o_in, ho, b_in, heads, pj, c_in, stream, gu, e_in, h_all, part, f_out, f_in, acc, r_out, r_in, g_out, g_in
        ) = buffers[h * PER_PART : (h + 1) * PER_PART]
        for i, (latent, lse) in enumerate(zip(*attend(h))):
            o_out[:, i, :, :KVL] = latent.astype(BF).reshape(NX, 16, KVL)
            o_out[:, i, :, KVL:] = lse.reshape(NX, 16, 128)
        slot = links.reserve(NX)
        for k in range(1, NX):
            links.send(slot + k, o_out.at[x_to[k]], o_in.at[x], dp, z_lo * NX + x_to[k])
        o_in[x] = o_out[x]
        yield
        for k in range(1, NX):
            links.arrived(slot + k, o_in.at[x_from[k]], dp, opposite)
        lse = [jnp.sum(o_in[s, :, :, KVL:].astype(F32), axis=2, keepdims=True) for s in range(NX)]
        top = functools.reduce(jnp.maximum, lse)
        shares = [jnp.exp(v - top) for v in lse]
        total = functools.reduce(jnp.add, shares)
        latent = jnp.zeros((requests, 16, KVL), F32)
        for s in range(NX):
            latent = latent + o_in[s, :, :, :KVL].astype(F32) * (shares[s] / total)
        latent = latent.astype(BF).reshape(requests * 16, KVL)

        head = rem(iota((requests * 16, 1), 0), 8)
        values = jnp.zeros((requests * 16, HD), F32)
        for i in range(8):
            values = jnp.where(head == i, dot(latent, w_uv[i], nn), values)
        row, col = iota((2 * padded, 1), 0), iota((2 * padded, requests * 16), 1)
        inner = rem(row, padded)
        at = div(inner, 4) * 8 + div(row, padded) * 4 + rem(inner, 4)
        split = jnp.logical_and(inner < 4 * tokens, col == at).astype(BF)
        ho[...] = dot(split, values.astype(BF), nn).astype(BF).reshape(2, padded, HD)

        slot = links.reserve(NG)
        for k in range(1, NG):
            links.send(slot + k, ho.at[lax.rem(g_to[k], 2)], b_in.at[g], group(g_to[k]), t)
        b_in[g] = ho[core]
        yield
        for k in range(1, NG):
            links.arrived(slot + k, b_in.at[g_from[k]], group(g_from[k]), t)
        row, col = iota((rows, 1), 0), iota((rows, NG * padded), 1)
        at = div(row, tokens) * padded + rem(row, tokens) * 4
        gathered = b_in[...].reshape(NG * padded, HD)
        for i in range(4):
            heads[core, y, :, i * HD : (i + 1) * HD] = dot((col == at + i).astype(BF), gathered, nn).astype(BF)
        yield from gather(heads, h)

        projected = dot(w_o[:, :KVL], heads[0].reshape(lanes, KVL), nt)
        projected = projected + dot(w_o[:, KVL:], heads[1].reshape(lanes, KVL), nt)
        pj[...] = projected.astype(BF).reshape(NT, 16, lanes)
        slot = links.reserve(NT)
        for k in range(1, NT):
            links.send(slot + k, pj.at[t_to[k]], c_in.at[t], dp, t_to[k])
        c_in[t] = pj[t]
        yield
        for k in range(1, NT):
            links.arrived(slot + k, c_in.at[t_from[k]], dp, t_from[k])
        summed = res_h[...]
        for s in range(NT):
            summed = summed + c_in[s].astype(F32)
        summed = summed.astype(BF).astype(F32)
        squares = jnp.sum(summed * summed, axis=0, keepdims=True)
        high = squares.astype(BF).astype(F32)
        row = iota((16, lanes), 0)
        piece = jnp.where(row == 14, high, jnp.where(row == 15, squares - high, summed)).astype(BF)
        stream[core, y, z] = piece

        slot = links.reserve(4)
        for k in range(1, 4):
            block = stream.at[core, y, z]
            links.send(slot + k, block, block, group(z_to[k] * 2 + core), t)
        yield
        for k in range(1, 4):
            links.arrived(slot + k, stream.at[core, y, z_from[k]], group(z_from[k] * 2 + core), t)
        yield from gather(stream, h)

        slot = links.reserve(NT)
        columns = stream[...].reshape(1024, lanes)
        for k in range(1, NT + 1):
            to = lax.rem(t + k, NT)
            first = pl.multiple_of(to * 80, 80)
            gu[to] = dot(w_gu[pl.ds(first, 80), :], columns, nn).astype(BF)
            if k < NT:
                links.send(slot + k, gu.at[to], e_in.at[t], dp, to)
            else:
                e_in[t] = gu[t]
        yield
        for k in range(1, NT):
            links.arrived(slot + k, e_in.at[t_from[k]], dp, t_from[k])
        total = jnp.zeros((80, lanes), F32)
        for s in range(NT):
            total = total + e_in[s].astype(F32)
        scale = lax.rsqrt(total[36:37] / D + EPS)
        gate, up = total[:40] * scale, total[40:] * scale
        hidden = gate / (1.0 + jnp.exp(-gate)) * up
        hidden = jnp.where(iota((40, lanes), 0) < 36, hidden, 0.0)
        hidden = jnp.concatenate([hidden, jnp.zeros((8, lanes), F32)], axis=0).astype(BF)
        h_all[t] = hidden
        slot = links.reserve(NT)
        for k in range(1, NT):
            links.send(slot + k, h_all.at[t], h_all.at[t], dp, t_to[k])
        yield
        for k in range(1, NT):
            links.arrived(slot + k, h_all.at[t_from[k]], dp, t_from[k])

        for block in range(lanes // 128):
            span = slice(block * 128, (block + 1) * 128)
            value = dot(h_all[:, :, span].reshape(384, 128), w_d[...], tn)
            part[span] = value + dot(stream[core, y, z, :, span], place, tn)

        f_out[...] = part[:, other].astype(BF)
        slot = links.reserve(1)
        links.send(slot, f_out, f_in, partner, t)
        yield
        links.arrived(slot, f_in, partner, t)
        acc[...] = (part[:, mine] + f_in[...].astype(F32)).reshape(NY, rows, KVL)
        value = yield from scatter(acc, r_out, r_in, h)
        value = value.astype(BF)
        row, col = iota((NG * padded, 1), 0), iota((NG * padded, rows), 1)
        inner = rem(row, padded)
        at = jnp.where(inner < 4 * tokens, div(row, padded) * tokens + div(inner, 4), -1)
        spread = jnp.zeros((NG * padded, HD), F32)
        for i in range(4):
            chosen = jnp.logical_and(col == at, rem(inner, 4) == i).astype(BF)
            spread = spread + dot(chosen, value[:, i * HD : (i + 1) * HD], nn)
        g_out[...] = spread.astype(BF).reshape(NG, padded, HD)
        slot = links.reserve(NG)
        for k in range(1, NG):
            links.send(slot + k, g_out.at[g_to[k]], g_in.at[g], group(g_to[k]), t)
        g_in[g] = g_out[g]
        yield
        for k in range(1, NG):
            links.arrived(slot + k, g_in.at[g_from[k]], group(g_from[k]), t)
        row, col = iota((16, 1), 0), iota((16, padded), 1)
        token = row - 2 * FIRST[h]
        at = jnp.where(jnp.logical_and(token >= 0, token < tokens), token * 4, -8)
        chosen = [(col == at + i).astype(BF) for i in range(4)]
        blocks = []
        for side in range(2):
            total = g_in[side].astype(F32)
            for s in range(1, 4):
                total = total + g_in[2 * s + side].astype(F32)
            blocks += [dot(c, total.astype(BF), nn) for c in chosen[side:]]
        results.append(jnp.concatenate(blocks, axis=1))

    place = jnp.logical_and(iota((16, 896), 1) == dp * 14 + iota((16, 896), 0), iota((16, 896), 0) < 14).astype(BF)
    mine = pl.ds(pl.multiple_of(core * 384, 128), KVL)
    other = pl.ds(pl.multiple_of((1 - core) * 384, 128), KVL)
    results = []
    running = [chain(h) for h in range(len(PARTS))]
    while running:
        running = [steps for steps in running if next(steps, DONE) is not DONE]

    out[...] = functools.reduce(jnp.add, results).astype(BF)[:10]
    links.finish()


SLOTS = 8 * 2 + len(SPANS) * 8 * 4 + len(PARTS) * (2 * 15 + 6 * 8 + 4 + 1 + 7)


def layer(*operands):
    scratch = [
        ((144, LAT), BF),
        ((NT * 80, 1024), BF),
        ((128, 1024), BF),
        ((384, 896), BF),
        ((NX, REQ, 16, LAT), BF),
        ((2, REQ, KEYS, LAT), BF),
    ]
    for spans in SPANS:
        for span in spans:
            scratch += [((8, 48, span.stop - span.start), BF)] * 4
    for requests, padded in zip(PARTS, HALF_ROWS):
        rows, lanes = 16 * requests, 128 * requests
        scratch += [
            ((16, lanes), F32),
            ((NX, requests, 16, 640), BF),
            ((NX, requests, 16, 640), BF),
            ((2, padded, HD), BF),
            ((NG, padded, HD), BF),
            ((2, NY, rows, KVL), BF),
            ((NT, 16, lanes), BF),
            ((NT, 16, lanes), BF),
            ((2, NY, 4, 16, lanes), BF),
            ((NT, 80, lanes), BF),
            ((NT, 80, lanes), BF),
            ((NT, 48, lanes), BF),
            ((lanes, 896), F32),
            ((lanes, KVL), BF),
            ((lanes, KVL), BF),
            ((NY, rows, KVL), F32),
            ((7, rows, KVL), BF),
            ((7, rows, KVL), BF),
            ((NG, padded, HD), BF),
            ((NG, padded, HD), BF),
        ]
    vmem = pl.BlockSpec(memory_space=pltpu.VMEM)
    held = [
        (pltpu.SMEM if i < 2 else pltpu.VMEM)(operand.shape, operand.dtype) for i, operand in enumerate(operands)
    ]
    return pl.pallas_call(
        kernel,
        out_shape=jax.ShapeDtypeStruct((10, 896), BF),
        in_specs=[pl.BlockSpec(memory_space=pl.ANY)] * 14,
        out_specs=vmem,
        scratch_shapes=held
        + [pltpu.VMEM(shape, kind) for shape, kind in scratch]
        + [pltpu.SemaphoreType.DMA((SLOTS,)), pltpu.SemaphoreType.DMA((SLOTS,)), pltpu.SemaphoreType.DMA((14,))],
        compiler_params=pltpu.CompilerParams(
            collective_id=0, has_side_effects=True, vmem_limit_bytes=60 * 1024 * 1024
        ),
        cost_estimate=pl.CostEstimate(flops=3 * 10**9, bytes_accessed=10**7, transcendentals=10**6),
        name="layer",
    )(*operands)


def local(
    pool,
    page_table,
    lengths,
    mig_page,
    mig_dest,
    queries,
    new_latent,
    w_uv,
    w_out,
    residual,
    norm_gain,
    w_gate,
    w_up,
    w_down,
):
    return layer(
        page_table,
        lengths,
        mig_page,
        mig_dest,
        queries.reshape(REQ, 16, LAT),
        pool.reshape(POOL * PAGE, LAT),
        new_latent,
        w_uv,
        w_out.transpose(2, 1, 0).reshape(112, 1024),
        residual.reshape(TOK, 14).T,
        norm_gain,
        w_gate.T,
        w_up.T,
        w_down,
    )


def solution(mesh):
    in_specs = (
        P("dp", None, None),
        P("dp", None),
        P("dp"),
        P("dp", None),
        P("dp", None),
        P("dp", "tp", None),
        P("dp", None),
        P("tp", None, None),
        P("tp", None, "dp"),
        P(None, "tp", "dp"),
        P("tp"),
        P("tp", "dp"),
        P("tp", "dp"),
        P("dp", "tp"),
    )
    out_specs = P("dp", "tp")
    return jax.shard_map(local, mesh=mesh, in_specs=in_specs, out_specs=out_specs, check_vma=False)
```

```python
import functools

import jax
import jax.numpy as jnp
from jax import lax
from jax.experimental import pallas as pl
from jax.experimental.pallas import tpu as pltpu
from jax.sharding import PartitionSpec as P

D = 7168
HD = 128
KVL = 512
LAT = 576
PAGE = 16
MAXP = 13
REQ = 5
POOL = 65
CAP = 3
NY = 8
NG = 8
NT = 8
NX = 4
KEYS = 32
TOK = 640
EPS = 1e-06
SCALE = 192 ** (-0.5)
BF = jnp.bfloat16
F32 = jnp.float32
MESH = pl.DeviceIdType.MESH
DEAD = -1e30
PARTS = (2, 3)
FIRST = tuple(sum(PARTS[:h]) for h in range(len(PARTS)))
PER_PART = 20
HALF_ROWS = tuple(-(-8 * requests // 16) * 16 for requests in PARTS)
SPANS = ((slice(0, 256), slice(384, 512)), (slice(256, 384), slice(512, 576)))
DONE = object()


def dot(a, b, dims):
    return lax.dot_general(a, b, (dims, ((), ())), preferred_element_type=F32)


def div(value, by):
    return lax.shift_right_logical(value * (-(-(1 << 20) // by)), 20)


def rem(value, by):
    return value - by * div(value, by)


def iota(shape, axis):
    return lax.broadcasted_iota(jnp.int32, shape, axis)


class Links:
    def __init__(self, send_sems, recv_sems):
        self.send_sems, self.recv_sems, self.used, self.sent = send_sems, recv_sems, 0, []

    def reserve(self, count):
        first = self.used
        self.used += count
        return first

    def copy(self, slot, src, dst, dp, tp):
        return pltpu.make_async_remote_copy(
            src_ref=src,
            dst_ref=dst,
            send_sem=self.send_sems.at[slot],
            recv_sem=self.recv_sems.at[slot],
            device_id={"dp": dp, "tp": tp},
            device_id_type=MESH,
        )

    def send(self, slot, src, dst, dp, tp):
        copy = self.copy(slot, src, dst, dp, tp)
        copy.start()
        self.sent.append(copy)

    def arrived(self, slot, dst, dp, tp):
        self.copy(slot, dst, dst, dp, tp).wait_recv()

    def finish(self):
        for copy in self.sent:
            copy.wait_send()


def kernel(
    *refs
):
    operands, (out, *held), rest = refs[:14], refs[14:29], refs[29:]
    (
        table, lengths, mig_page, mig_dest, q, pool, fresh, w_uv, w_out, res, gain, w_gate, w_up, w_down
    ) = held
    (
    own, w_gu, w_o, w_d, q_all, keys, *buffers, send_sems, recv_sems, load_sems,
    ) = rest
    inbox, buffers = buffers[: 8 * len(SPANS)], buffers[8 * len(SPANS) :]
    loads = [pltpu.make_async_copy(*pair, load_sems.at[i]) for i, pair in enumerate(zip(operands, held))]
    for i in (5, 2, 3, 4, 8, 9, 13, 10, 11, 12, 6, 0, 1, 7):
        loads[i].start()

    dp, t = lax.axis_index("dp"), lax.axis_index("tp")
    y, g = dp // NG, lax.rem(dp, NG)
    z, core = g // 2, lax.rem(g, 2)
    links = Links(send_sems, recv_sems)
    t_to = [lax.rem(t + k, NT) for k in range(NT)]
    t_from = [lax.rem(t + NT - k, NT) for k in range(NT)]
    z_lo, x = t // NX, lax.rem(t, NX)
    x_to = [lax.rem(x + k, NX) for k in range(NX)]
    x_from = [lax.rem(x + NX - k, NX) for k in range(NX)]
    g_to = [lax.rem(g + k, NG) for k in range(NG)]
    g_from = [lax.rem(g + NG - k, NG) for k in range(NG)]
    y_to = [lax.rem(y + k, NY) for k in range(NY)]
    y_from = [lax.rem(y + NY - k, NY) for k in range(NY)]
    z_to = [lax.rem(z + k, 4) for k in range(4)]
    z_from = [lax.rem(z + 4 - k, 4) for k in range(4)]
    nn, nt, tn = ((1,), (0,)), ((1,), (1,)), ((0,), (0,))

    def dp_of(yy):
        return yy * NG + g

    def group(gg):
        return y * NG + gg

    barrier = pltpu.get_barrier_semaphore()
    for k in range(1, NT):
        pl.semaphore_signal(barrier, inc=1, device_id={"dp": dp, "tp": t_to[k]}, device_id_type=MESH)
    for k in range(1, NG):
        pl.semaphore_signal(barrier, inc=1, device_id={"dp": group(g_to[k]), "tp": t}, device_id_type=MESH)
    for k in range(1, NY):
        pl.semaphore_signal(barrier, inc=1, device_id={"dp": dp_of(y_to[k]), "tp": t}, device_id_type=MESH)

    for i in (2, 3):
        loads[i].wait()
    row = iota((384, 1), 0)
    inner = rem(row, 6)
    entry = rem(iota((1, CAP * 28), 1), CAP)

    def outgoing(rank):
        match = jnp.logical_and(mig_dest[...] == rank, entry == div(inner, 2))
        source = jnp.sum(jnp.where(match, (mig_page[...] + 1).astype(F32), 0.0), axis=1, keepdims=True)
        source = source.astype(jnp.int32) * 2 - 2 + rem(inner, 2)
        return (source == iota((384, 144), 1)).astype(BF)

    first, second = div(row, 48), div(rem(row, 48), 6)
    for_y, for_g = outgoing(first * NG + second), outgoing(second * NG + first)
    row = iota((144, 1), 0)
    column = (div(row, 2)) * PAGE + 2 * t + rem(row, 2)
    two = (column == iota((144, POOL * PAGE), 1)).astype(BF)
    row, col = iota((384, 1), 0), iota((384, 384), 1)
    swap = (col == (div(rem(row, 48), 6)) * 48 + (div(row, 48)) * 6 + rem(row, 6)).astype(BF)
    for i in (5, 4):
        loads[i].wait()
    own[...] = dot(two, pool[...], nn).astype(BF)

    def exchange(span_y, span_z, y1, y2, y3, y4, z1, z2, z3, z4):
        width_y, width_z = span_y.stop - span_y.start, span_z.stop - span_z.start
        y1[...] = dot(for_y, own[:, span_y], nn).astype(BF).reshape(NY, 48, width_y)
        z1[...] = dot(for_g, own[:, span_z], nn).astype(BF).reshape(NG, 48, width_z)
        along_y, along_g = links.reserve(NY), links.reserve(NG)
        for k in range(1, NY):
            links.send(along_y + k, y1.at[y_to[k]], y2.at[y], dp_of(y_to[k]), t)
            links.send(along_g + k, z1.at[g_to[k]], z2.at[g], group(g_to[k]), t)
        y2[y] = y1[y]
        z2[g] = z1[g]
        yield
        for k in range(1, NY):
            links.arrived(along_y + k, y2.at[y_from[k]], dp_of(y_from[k]), t)
            links.arrived(along_g + k, z2.at[g_from[k]], group(g_from[k]), t)
        y3[...] = dot(swap, y2[...].reshape(384, width_y), nn).astype(BF).reshape(NG, 48, width_y)
        z3[...] = dot(swap, z2[...].reshape(384, width_z), nn).astype(BF).reshape(NY, 48, width_z)
        along_g, along_y = links.reserve(NG), links.reserve(NY)
        for k in range(1, NY):
            links.send(along_g + k, y3.at[g_to[k]], y4.at[g], group(g_to[k]), t)
            links.send(along_y + k, z3.at[y_to[k]], z4.at[y], dp_of(y_to[k]), t)
        y4[g] = y3[g]
        z4[y] = z3[y]
        yield
        for k in range(1, NY):
            links.arrived(along_g + k, y4.at[g_from[k]], group(g_from[k]), t)
            links.arrived(along_y + k, z4.at[y_from[k]], dp_of(y_from[k]), t)

    pages = [exchange(*spans, *inbox[8 * i : 8 * i + 8]) for i, spans in enumerate(SPANS)]
    q_all[x] = q[...]
    pl.semaphore_wait(barrier, 21)
    for steps in pages:
        next(steps)
    to_heads = links.reserve(NX)
    for k in range(1, NX):
        links.send(to_heads + k, q_all.at[x], q_all.at[x], dp, z_lo * NX + x_to[k])

    for i in (8, 9, 13, 10, 11, 12):
        loads[i].wait()
    row, col = iota((128, 1), 0), iota((128, 112), 1)
    spread = jnp.logical_and(rem(row, 16) < 14, col == rem(row, 16) * 8 + div(row, 16)).astype(BF)
    w_o[...] = dot(spread, w_out[...], nn).astype(BF)
    row, col = iota((384, 1), 0), iota((384, 288), 1)
    spread = jnp.logical_and(rem(row, 48) < 36, col == (div(row, 48)) * 36 + rem(row, 48)).astype(BF)
    w_d[...] = dot(spread, w_down[...], nn).astype(BF)
    for h, requests in enumerate(PARTS):
        tokens = 2 * requests
        row, col = iota((TOK, 1), 0), iota((1, 64 * tokens), 1)
        at = div(col, tokens) * 10 + rem(col, tokens) + 2 * FIRST[h]
        values = dot(res[...], (row == at).astype(BF), nn)
        buffers[h * PER_PART][...] = jnp.concatenate([values, jnp.zeros((2, 64 * tokens), F32)], axis=0)

    for steps in pages:
        next(steps)

    row, col = iota((NT * 80, 1), 0), iota((NT * 80, 288), 1)
    slot = rem(row, 80)
    of_gate = jnp.logical_and(slot < 36, col == (div(row, 80)) * 36 + slot).astype(BF)
    of_up = jnp.logical_and(jnp.logical_and(slot >= 40, slot < 76), col == (div(row, 80)) * 36 + slot - 40).astype(BF)
    scale = gain[...].astype(F32).reshape(1, 896)
    rows = dot(of_gate, (w_gate[...].astype(F32) * scale).astype(BF), nn)
    rows = (rows + dot(of_up, (w_up[...].astype(F32) * scale).astype(BF), nn)).astype(BF)
    row, col = iota((896, 1), 0), iota((896, 1024), 1)
    rank = div(row, 14)
    at = rem(rank, 2) * 512 + (div(rank, 2)) * 16 + rem(row, 14)
    spread = (col == at).astype(BF)
    squares_at = jnp.logical_and(rem(iota((NT * 80, 1), 0), 80) == 36, rem(iota((1, 1024), 1), 16) >= 14)
    w_gu[...] = jnp.where(squares_at, 1.0, dot(rows, spread, nn)).astype(BF)

    for steps in pages:
        next(steps, DONE)

    for i in (6, 0, 1):
        loads[i].wait()
    row = iota((REQ * KEYS, 1), 0)
    place, request = rem(row, KEYS), div(row, KEYS)
    named = jnp.full((REQ * KEYS, 1), -1, jnp.int32)
    for r in range(REQ):
        for k in range(MAXP):
            named = jnp.where(jnp.logical_and(request == r, div(place, 2) == k), table[r, k], named)
    token = rem(place, 2)
    from_own = (jnp.where(jnp.logical_and(named >= 0, named < POOL), 2 * named + token, -1) == iota((REQ * KEYS, 144), 1)).astype(BF)
    migrated = jnp.maximum(named - POOL, 0)
    rank = div(migrated, 3)
    inner = (migrated - CAP * rank) * 2 + token
    rank_y, rank_g = div(rank, NG), rem(rank, NG)
    in_inbox = named >= POOL
    at = jnp.where(in_inbox, rank_g * 48 + rank_y * 6 + inner, -1)
    from_y = (at == iota((REQ * KEYS, 384), 1)).astype(BF)
    at = jnp.where(in_inbox, rank_y * 48 + rank_g * 6 + inner, -1)
    from_z = (at == iota((REQ * KEYS, 384), 1)).astype(BF)
    at = jnp.where(jnp.logical_and(place >= 26, place < 28), 2 * request + place - 26, -1)
    from_fresh = (at == iota((REQ * KEYS, 2 * REQ), 1)).astype(BF)
    for i, spans in enumerate(SPANS):
        arrived = inbox[8 * i + 3], inbox[8 * i + 7]
        for span, source, found in zip(spans, (from_y, from_z), arrived):
            width = span.stop - span.start
            rows = dot(from_own, own[:, span], nn) + dot(from_fresh, fresh[:, span], nn)
            rows = rows + dot(source, found[...].reshape(384, width), nn)
            keys[z_lo, :, :, span] = rows.astype(BF).reshape(REQ, KEYS, width)
    opposite = lax.rem(t + NX, NT)
    to_opposite = links.reserve(len(PARTS))
    for h, requests in enumerate(PARTS):
        mine = keys.at[z_lo, FIRST[h] : FIRST[h] + requests]
        links.send(to_opposite + h, mine, mine, dp, opposite)
    for k in range(1, NX):
        links.arrived(to_heads + k, q_all.at[x_from[k]], dp, opposite)

    def attend(h):
        requests = PARTS[h]
        span = range(FIRST[h], FIRST[h] + requests)
        links.arrived(to_opposite + h, keys.at[1 - z_lo, FIRST[h] : FIRST[h] + requests], dp, opposite)
        held = [keys[:, r].reshape(2 * KEYS, LAT) for r in span]
        scores = [dot(q_all[:, r].reshape(NX * 16, LAT), k, nt) for r, k in zip(span, held)]
        scores = jnp.concatenate(scores, axis=0) * SCALE
        row, col = iota((requests * 64, 1), 0), iota((1, 2 * KEYS), 1)
        length = jnp.full((requests * 64, 1), lengths[FIRST[h]], jnp.int32)
        for i in range(1, requests):
            length = jnp.where(row >= i * 64, lengths[FIRST[h] + i], length)
        place, source = rem(col, KEYS), div(col, KEYS) * NX + x
        token = div(place, 2) * PAGE + 2 * source + rem(place, 2)
        cached = jnp.logical_and(jnp.where(place < 26, token, MAXP * PAGE) < length, place < 26)
        newest = jnp.where(source == 0, 26 + rem(div(row, 8), 2), 0)
        newer = jnp.logical_and(place >= 26, place <= newest)
        live = jnp.logical_or(cached, newer)
        scores = jnp.where(live, scores, DEAD)
        top = jnp.max(scores, axis=1, keepdims=True)
        weights = jnp.where(live, jnp.exp(scores - top), 0.0)
        total = jnp.sum(weights, axis=1, keepdims=True)
        some = total > 0.0
        total = jnp.where(some, total, 1.0)
        weights = (weights / total).astype(BF)
        lse = jnp.where(some, top + jnp.log(total), DEAD)
        high = lse.astype(BF).astype(F32)
        middle = (lse - high).astype(BF).astype(F32)
        low = lse - high - middle
        lane = iota((requests * 64, 128), 1)
        parts = jnp.where(lane == 0, high, jnp.where(lane == 1, middle, jnp.where(lane == 2, low, 0.0))).astype(BF)
        latent = [dot(weights[i * 64 : (i + 1) * 64], k[:, :KVL], nn) for i, k in enumerate(held)]
        return latent, [parts[i * 64 : (i + 1) * 64] for i in range(requests)]

    loads[7].wait()
    partner = dp + 1 - 2 * core

    def at_y(step):
        return lax.rem(y + NY + step, NY)

    def gather(buf, flip):
        near, far, over = links.reserve(4), links.reserve(3), links.reserve(8)
        held_y = []

        def pass_on(index):
            links.send(over + len(held_y), buf.at[core, index], buf.at[core, index], partner, t)
            held_y.append(index)

        def forward(slot, index, step):
            links.send(slot, buf.at[core, index], buf.at[core, index], dp_of(at_y(step)), t)

        def arrived(slot, index):
            links.arrived(slot, buf.at[core, index], partner, t)

        for i, step in enumerate((2, -2, 1, -1)):
            forward(near + i, y, step)
        pass_on(y)
        yield
        arrived(near, at_y(-2))
        forward(far, at_y(-2), 1)
        if flip:
            forward(far + 2, at_y(-2), 2)
        arrived(near + 1, at_y(2))
        forward(far + 1, at_y(2), -1)
        if not flip:
            forward(far + 2, at_y(2), -2)
        pass_on(at_y(-2))
        pass_on(at_y(2))
        yield
        for i, step in ((2, -1), (3, 1)):
            arrived(near + i, at_y(step))
            pass_on(at_y(step))
        for i, step in ((0, -3), (1, 3), (2, 4)):
            arrived(far + i, at_y(step))
            pass_on(at_y(step))
        for order, index in enumerate(held_y):
            links.arrived(over + order, buf.at[1 - core, index], partner, t)

    def scatter(acc, r_out, r_in, flip):
        slot = links.reserve(7)

        def send(i, value, step):
            r_out[i] = value.astype(BF)
            links.send(slot + i, r_out.at[i], r_in.at[i], dp_of(at_y(step)), t)

        def received(i):
            links.arrived(slot + i, r_in.at[i], partner, t)
            return r_in[i].astype(F32)

        send(2, acc[at_y(4)], 2 if flip else -2)
        send(0, acc[at_y(-3)], -1)
        send(1, acc[at_y(3)], 1)
        send(3, acc[at_y(-1)], -1)
        send(4, acc[at_y(1)], 1)
        yield
        below, above = acc[at_y(-2)] + received(0), acc[at_y(2)] + received(1)
        if flip:
            above = above + received(2)
        else:
            below = below + received(2)
        send(5, below, -2)
        send(6, above, 2)
        yield
        value = acc[y]
        for i in range(3, 7):
            value = value + received(i)
        return value

    def chain(h):
        requests = PARTS[h]
        tokens = 2 * requests
        rows, lanes = NG * tokens, 64 * tokens
        padded = HALF_ROWS[h]
        (
            res_h, o_out, o_in, ho, b_in, heads, pj, c_in, stream, gu, e_in, h_all, part, f_out, f_in, acc, r_out, r_in, g_out, g_in
        ) = buffers[h * PER_PART : (h + 1) * PER_PART]
        for i, (latent, lse) in enumerate(zip(*attend(h))):
            o_out[:, i, :, :KVL] = latent.astype(BF).reshape(NX, 16, KVL)
            o_out[:, i, :, KVL:] = lse.reshape(NX, 16, 128)
        slot = links.reserve(NX)
        for k in range(1, NX):
            links.send(slot + k, o_out.at[x_to[k]], o_in.at[x], dp, z_lo * NX + x_to[k])
        o_in[x] = o_out[x]
        yield
        for k in range(1, NX):
            links.arrived(slot + k, o_in.at[x_from[k]], dp, opposite)
        lse = [jnp.sum(o_in[s, :, :, KVL:].astype(F32), axis=2, keepdims=True) for s in range(NX)]
        top = functools.reduce(jnp.maximum, lse)
        shares = [jnp.exp(v - top) for v in lse]
        total = functools.reduce(jnp.add, shares)
        latent = jnp.zeros((requests, 16, KVL), F32)
        for s in range(NX):
            latent = latent + o_in[s, :, :, :KVL].astype(F32) * (shares[s] / total)
        latent = latent.astype(BF).reshape(requests * 16, KVL)

        head = rem(iota((requests * 16, 1), 0), 8)
        values = jnp.zeros((requests * 16, HD), F32)
        for i in range(8):
            values = jnp.where(head == i, dot(latent, w_uv[i], nn), values)
        row, col = iota((2 * padded, 1), 0), iota((2 * padded, requests * 16), 1)
        inner = rem(row, padded)
        at = div(inner, 4) * 8 + div(row, padded) * 4 + rem(inner, 4)
        split = jnp.logical_and(inner < 4 * tokens, col == at).astype(BF)
        ho[...] = dot(split, values.astype(BF), nn).astype(BF).reshape(2, padded, HD)

        slot = links.reserve(NG)
        for k in range(1, NG):
            links.send(slot + k, ho.at[lax.rem(g_to[k], 2)], b_in.at[g], group(g_to[k]), t)
        b_in[g] = ho[core]
        yield
        for k in range(1, NG):
            links.arrived(slot + k, b_in.at[g_from[k]], group(g_from[k]), t)
        row, col = iota((rows, 1), 0), iota((rows, NG * padded), 1)
        at = div(row, tokens) * padded + rem(row, tokens) * 4
        gathered = b_in[...].reshape(NG * padded, HD)
        for i in range(4):
            heads[core, y, :, i * HD : (i + 1) * HD] = dot((col == at + i).astype(BF), gathered, nn).astype(BF)
        yield from gather(heads, h)

        projected = dot(w_o[:, :KVL], heads[0].reshape(lanes, KVL), nt)
        projected = projected + dot(w_o[:, KVL:], heads[1].reshape(lanes, KVL), nt)
        pj[...] = projected.astype(BF).reshape(NT, 16, lanes)
        slot = links.reserve(NT)
        for k in range(1, NT):
            links.send(slot + k, pj.at[t_to[k]], c_in.at[t], dp, t_to[k])
        c_in[t] = pj[t]
        yield
        for k in range(1, NT):
            links.arrived(slot + k, c_in.at[t_from[k]], dp, t_from[k])
        summed = res_h[...]
        for s in range(NT):
            summed = summed + c_in[s].astype(F32)
        summed = summed.astype(BF).astype(F32)
        squares = jnp.sum(summed * summed, axis=0, keepdims=True)
        high = squares.astype(BF).astype(F32)
        row = iota((16, lanes), 0)
        piece = jnp.where(row == 14, high, jnp.where(row == 15, squares - high, summed)).astype(BF)
        stream[core, y, z] = piece

        slot = links.reserve(4)
        for k in range(1, 4):
            block = stream.at[core, y, z]
            links.send(slot + k, block, block, group(z_to[k] * 2 + core), t)
        yield
        for k in range(1, 4):
            links.arrived(slot + k, stream.at[core, y, z_from[k]], group(z_from[k] * 2 + core), t)
        yield from gather(stream, h)

        slot = links.reserve(NT)
        columns = stream[...].reshape(1024, lanes)
        for k in range(1, NT + 1):
            to = lax.rem(t + k, NT)
            first = pl.multiple_of(to * 80, 80)
            gu[to] = dot(w_gu[pl.ds(first, 80), :], columns, nn).astype(BF)
            if k < NT:
                links.send(slot + k, gu.at[to], e_in.at[t], dp, to)
            else:
                e_in[t] = gu[t]
        yield
        for k in range(1, NT):
            links.arrived(slot + k, e_in.at[t_from[k]], dp, t_from[k])
        total = jnp.zeros((80, lanes), F32)
        for s in range(NT):
            total = total + e_in[s].astype(F32)
        scale = lax.rsqrt(total[36:37] / D + EPS)
        gate, up = total[:40] * scale, total[40:] * scale
        hidden = gate / (1.0 + jnp.exp(-gate)) * up
        hidden = jnp.where(iota((40, lanes), 0) < 36, hidden, 0.0)
        hidden = jnp.concatenate([hidden, jnp.zeros((8, lanes), F32)], axis=0).astype(BF)
        h_all[t] = hidden
        slot = links.reserve(NT)
        for k in range(1, NT):
            links.send(slot + k, h_all.at[t], h_all.at[t], dp, t_to[k])
        yield
        for k in range(1, NT):
            links.arrived(slot + k, h_all.at[t_from[k]], dp, t_from[k])

        for block in range(lanes // 128):
            span = slice(block * 128, (block + 1) * 128)
            value = dot(h_all[:, :, span].reshape(384, 128), w_d[...], tn)
            part[span] = value + dot(stream[core, y, z, :, span], place, tn)

        f_out[...] = part[:, other].astype(BF)
        slot = links.reserve(1)
        links.send(slot, f_out, f_in, partner, t)
        yield
        links.arrived(slot, f_in, partner, t)
        acc[...] = (part[:, mine] + f_in[...].astype(F32)).reshape(NY, rows, KVL)
        value = yield from scatter(acc, r_out, r_in, h)
        value = value.astype(BF)
        row, col = iota((NG * padded, 1), 0), iota((NG * padded, rows), 1)
        inner = rem(row, padded)
        at = jnp.where(inner < 4 * tokens, div(row, padded) * tokens + div(inner, 4), -1)
        spread = jnp.zeros((NG * padded, HD), F32)
        for i in range(4):
            chosen = jnp.logical_and(col == at, rem(inner, 4) == i).astype(BF)
            spread = spread + dot(chosen, value[:, i * HD : (i + 1) * HD], nn)
        g_out[...] = spread.astype(BF).reshape(NG, padded, HD)
        slot = links.reserve(NG)
        for k in range(1, NG):
            links.send(slot + k, g_out.at[g_to[k]], g_in.at[g], group(g_to[k]), t)
        g_in[g] = g_out[g]
        yield
        for k in range(1, NG):
            links.arrived(slot + k, g_in.at[g_from[k]], group(g_from[k]), t)
        row, col = iota((16, 1), 0), iota((16, padded), 1)
        token = row - 2 * FIRST[h]
        at = jnp.where(jnp.logical_and(token >= 0, token < tokens), token * 4, -8)
        chosen = [(col == at + i).astype(BF) for i in range(4)]
        blocks = []
        for side in range(2):
            total = g_in[side].astype(F32)
            for s in range(1, 4):
                total = total + g_in[2 * s + side].astype(F32)
            blocks += [dot(c, total.astype(BF), nn) for c in chosen[side:]]
        results.append(jnp.concatenate(blocks, axis=1))

    place = jnp.logical_and(iota((16, 896), 1) == dp * 14 + iota((16, 896), 0), iota((16, 896), 0) < 14).astype(BF)
    mine = pl.ds(pl.multiple_of(core * 384, 128), KVL)
    other = pl.ds(pl.multiple_of((1 - core) * 384, 128), KVL)
    results = []
    running = [chain(h) for h in range(len(PARTS))]
    while running:
        running = [steps for steps in running if next(steps, DONE) is not DONE]

    out[...] = functools.reduce(jnp.add, results).astype(BF)[:10]
    links.finish()


SLOTS = 8 * 2 + len(SPANS) * 8 * 4 + len(PARTS) * (2 * 15 + 6 * 8 + 4 + 1 + 7)


def layer(*operands):
    scratch = [
        ((144, LAT), BF),
        ((NT * 80, 1024), BF),
        ((128, 1024), BF),
        ((384, 896), BF),
        ((NX, REQ, 16, LAT), BF),
        ((2, REQ, KEYS, LAT), BF),
    ]
    for spans in SPANS:
        for span in spans:
            scratch += [((8, 48, span.stop - span.start), BF)] * 4
    for requests, padded in zip(PARTS, HALF_ROWS):
        rows, lanes = 16 * requests, 128 * requests
        scratch += [
            ((16, lanes), F32),
            ((NX, requests, 16, 640), BF),
            ((NX, requests, 16, 640), BF),
            ((2, padded, HD), BF),
            ((NG, padded, HD), BF),
            ((2, NY, rows, KVL), BF),
            ((NT, 16, lanes), BF),
            ((NT, 16, lanes), BF),
            ((2, NY, 4, 16, lanes), BF),
            ((NT, 80, lanes), BF),
            ((NT, 80, lanes), BF),
            ((NT, 48, lanes), BF),
            ((lanes, 896), F32),
            ((lanes, KVL), BF),
            ((lanes, KVL), BF),
            ((NY, rows, KVL), F32),
            ((7, rows, KVL), BF),
            ((7, rows, KVL), BF),
            ((NG, padded, HD), BF),
            ((NG, padded, HD), BF),
        ]
    vmem = pl.BlockSpec(memory_space=pltpu.VMEM)
    held = [
        (pltpu.SMEM if i < 2 else pltpu.VMEM)(operand.shape, operand.dtype) for i, operand in enumerate(operands)
    ]
    return pl.pallas_call(
        kernel,
        out_shape=jax.ShapeDtypeStruct((10, 896), BF),
        in_specs=[pl.BlockSpec(memory_space=pl.ANY)] * 14,
        out_specs=vmem,
        scratch_shapes=held
        + [pltpu.VMEM(shape, kind) for shape, kind in scratch]
        + [pltpu.SemaphoreType.DMA((SLOTS,)), pltpu.SemaphoreType.DMA((SLOTS,)), pltpu.SemaphoreType.DMA((14,))],
        compiler_params=pltpu.CompilerParams(
            collective_id=0, has_side_effects=True, vmem_limit_bytes=60 * 1024 * 1024
        ),
        cost_estimate=pl.CostEstimate(flops=3 * 10**9, bytes_accessed=10**7, transcendentals=10**6),
        name="layer",
    )(*operands)


def local(
    pool,
    page_table,
    lengths,
    mig_page,
    mig_dest,
    queries,
    new_latent,
    w_uv,
    w_out,
    residual,
    norm_gain,
    w_gate,
    w_up,
    w_down,
):
    return layer(
        page_table,
        lengths,
        mig_page,
        mig_dest,
        queries.reshape(REQ, 16, LAT),
        pool.reshape(POOL * PAGE, LAT),
        new_latent,
        w_uv,
        w_out.transpose(2, 1, 0).reshape(112, 1024),
        residual.reshape(TOK, 14).T,
        norm_gain,
        w_gate.T,
        w_up.T,
        w_down,
    )


def solution(mesh):
    in_specs = (
        P("dp", None, None),
        P("dp", None),
        P("dp"),
        P("dp", None),
        P("dp", None),
        P("dp", "tp", None),
        P("dp", None),
        P("tp", None, None),
        P("tp", None, "dp"),
        P(None, "tp", "dp"),
        P("tp"),
        P("tp", "dp"),
        P("tp", "dp"),
        P("dp", "tp"),
    )
    out_specs = P("dp", "tp")
    return jax.shard_map(local, mesh=mesh, in_specs=in_specs, out_specs=out_specs, check_vma=False)
```
